32 devices in a mesh: ctx: 8 (over z, y), wt: 4 (over x, core).
Axes of the slice: x: 2, y: 2, z: 4, core: 2. Of those that a mesh axis runs over, the one named last changes fastest.
Arguments:
- tokens: bfloat16 [4, 1024, 1600], P('wt', 'ctx'), may hold values from -6 to 6
- slots: int32 [16], replicated, may hold values from 0 to 15, as said below
- norm_gains: bfloat16 [2, 1600], P(None, 'wt'), may hold values from 0.25 to 1.75
- norm_shifts: bfloat16 [2, 1600], P(None, 'wt'), may hold values from -2 to 2
- qkv_weight: bfloat16 [1600, 4800], P('wt'), may hold values from -0.21875 to 0.21875
- qv_bias: bfloat16 [2, 1600], P(None, 'wt'), may hold values from -3 to 3
- proj_weight: bfloat16 [1600, 1600], P('wt'), may hold values from -0.625 to 0.625
- proj_bias: bfloat16 [1600], P('wt'), may hold values from -2 to 2
- up_weight: bfloat16 [1600, 6400], P('wt'), may hold values from -0.15625 to 0.15625
- up_bias: bfloat16 [6400], P('wt'), may hold values from -2 to 2
- down_weight: bfloat16 [6400, 1600], P('wt'), may hold values from -0.15625 to 0.15625
- down_bias: bfloat16 [1600], P('wt'), may hold values from -2 to 2
- cotangent: bfloat16 [4, 1024, 1600], P('wt', 'ctx'), may hold values from -6 to 6
Outputs:
- output: bfloat16 [4, 1024, 1600], P('wt', 'ctx')
- d_tokens: bfloat16 [4, 1024, 1600], P('wt', 'ctx')
- d_norm_gains: float32 [2, 1600], P(None, 'wt')
- d_norm_shifts: float32 [2, 1600], P(None, 'wt')
- d_qkv_weight: float32 [1600, 4800], P('wt')
- d_qv_bias: float32 [2, 1600], P(None, 'wt')
- d_proj_weight: float32 [1600, 1600], P('wt')
- d_proj_bias: float32 [1600], P('wt')
- d_up_weight: float32 [1600, 6400], P('wt')
- d_up_bias: float32 [6400], P('wt')
- d_down_weight: float32 [6400, 1600], P('wt')
- d_down_bias: float32 [1600], P('wt')
The draws below stay inside these ranges and needn't reach their ends.
Inputs may be any that keep to these rules, and one draw needn't show every extreme that they name: `slots`: a permutation of the blocks; row blocks 2c and 2c+1 hold blocks b and 15 - b for some b.
All inputs are finite; a program needn't handle non-finite values.
Results may differ from the reference program's by a relative error of at most 0.02.
Values may be sent and summed in bfloat16 or wider, within the bound.
No kernel may reach another device: no remote copies, remote signals or barrier semaphores. Data moves between devices by JAX's collectives and lax.ppermute only.
A program may use at most 384 MiB of HBM per device.

```python
import math
import jax
import jax.numpy as jnp
from jax import lax

D = 1600
HEADS = 25
HD = 64
FF = 6400
BLK = 64
SLOTS = 16
SEQ_LEN = 1024
SEQS = 4


def draw_slots(key, part):
    key = jax.random.fold_in(key, 7)
    half = SLOTS // 2
    lower = jax.random.permutation(jax.random.fold_in(key, 1), half).astype(jnp.int32)
    flips = jax.random.randint(jax.random.fold_in(key, 2), (half,), 0, 2).astype(jnp.int32)
    upper = (SLOTS - 1 - lower).astype(jnp.int32)
    first = jnp.where(flips == 1, upper, lower)
    second = jnp.where(flips == 1, lower, upper)
    return jnp.stack([first, second], axis=1).reshape(SLOTS).astype(jnp.int32)


def levels(own_key, shape, pieces, smallest, largest):
    loudness = 1.0
    for dim, blocks in pieces:
        draws = jax.random.uniform(jax.random.fold_in(jax.random.fold_in(own_key, 6), dim), (blocks,), jnp.float32, smallest / len(pieces), largest / len(pieces))
        loudness = loudness * jnp.repeat(jnp.exp(draws), shape[dim] // blocks).reshape((-1,) + (1,) * (len(shape) - 1 - dim))
    return loudness


def bell_draw(own_key, extent, spread, most, split=(), held_as=jnp.bfloat16):
    result = spread * jax.random.normal(own_key, extent, jnp.float32)
    if split:
        result = result * levels(own_key, extent, split, -0.22, 0.18)
    return jnp.clip(result, -most, most).astype(held_as)


def setup_inputs(seed: int = 0) -> dict:
    streams_of = jax.random.split(jax.random.key(seed), 14)
    tokens = bell_draw(streams_of[0], (SEQS, SEQ_LEN, D), 1.0, 6.0, ((0, 4), (1, 8)))
    slots = draw_slots(jax.random.fold_in(streams_of[13], 71), 0)
    norm_gains = jnp.clip(1.0 + 0.15 * jax.random.normal(streams_of[2], (2, D), jnp.float32), 0.25, 1.75).astype(jnp.bfloat16)
    norm_shifts = bell_draw(streams_of[3], (2, D), 0.3, 2.0, ((1, 4),))
    qkv_weight = bell_draw(streams_of[4], (D, 3 * D), (D // 2) ** -0.5, 0.21875, ((0, 4),))
    qv_bias = bell_draw(streams_of[5], (2, D), 0.5, 3.0, ((1, 4),))
    proj_weight = bell_draw(streams_of[6], (D, D), (D // 16) ** -0.5, 0.625, ((0, 4),))
    proj_bias = bell_draw(streams_of[7], (D,), 0.3, 2.0, ((0, 4),))
    up_weight = bell_draw(streams_of[8], (D, FF), D ** -0.5, 0.15625, ((0, 4),))
    up_bias = bell_draw(streams_of[9], (FF,), 0.3, 2.0, ((0, 4),))
    down_weight = bell_draw(streams_of[10], (FF, D), (FF // 4) ** -0.5, 0.15625, ((0, 4),))
    down_bias = bell_draw(streams_of[11], (D,), 0.3, 2.0, ((0, 4),))
    cotangent = bell_draw(streams_of[12], (SEQS, SEQ_LEN, D), 1.0, 6.0, ((0, 4), (1, 8)))
    return {"tokens": tokens, "slots": slots, "norm_gains": norm_gains, "norm_shifts": norm_shifts, "qkv_weight": qkv_weight, "qv_bias": qv_bias, "proj_weight": proj_weight, "proj_bias": proj_bias, "up_weight": up_weight, "up_bias": up_bias, "down_weight": down_weight, "down_bias": down_bias, "cotangent": cotangent}


@jax.custom_vjp
def low(v):
    return lax.optimization_barrier(v.astype(jnp.bfloat16)).astype(jnp.float32)

@jax.custom_vjp
def low_back(v):
    return v

def low_keep(v):
    return (low(v), None)

def low_pass(kept, grad):
    return (grad,)

def back_keep(v):
    return (v, None)

def back_low(kept, grad):
    return (low(grad),)
low.defvjp(low_keep, low_pass)
low_back.defvjp(back_keep, back_low)

def matmul(left, right):
    return jnp.dot(left, right, precision=lax.Precision.HIGHEST, preferred_element_type=jnp.float32)

def layer_norm(values, gain, shift):
    centred = values - lax.optimization_barrier(jnp.mean(values, axis=-1, keepdims=True))
    scale = lax.rsqrt(lax.optimization_barrier(jnp.mean(centred * centred, axis=-1, keepdims=True)) + 1e-05)
    return centred * scale * gain + shift

def gelu(values):
    return 0.5 * values * (1.0 + jnp.tanh(0.7978845608028654 * (values + 0.044715 * values * values * values)))

def positions(slots):
    return (slots[:, None] * BLK + jnp.arange(BLK, dtype=jnp.int32)[None, :]).reshape(-1).astype(jnp.int32)

def sequence_forward(params, seq, pos):
    gains, shifts, wqkv, qvb, wproj, bproj, wup, bup, wdown, bdown = params
    length = seq.shape[0]
    a1 = low(layer_norm(seq, gains[0], shifts[0]))
    bias = jnp.concatenate([qvb[0], jnp.zeros((D,), jnp.float32), qvb[1]])
    qkv = low(low_back(matmul(a1, wqkv) + bias))
    query = qkv[:, :D].reshape(length, HEADS, HD)
    key = qkv[:, D:2 * D].reshape(length, HEADS, HD)
    value = qkv[:, 2 * D:].reshape(length, HEADS, HD)
    rows = math.gcd(length, 512)

    def block(pair):
        qblock, qpos = pair
        scores = jnp.einsum('rhd,khd->hrk', qblock, key, precision=lax.Precision.HIGHEST) * 0.125
        allowed = pos[None, :] <= qpos[:, None]
        scores = low_back(jnp.where(allowed[None], scores, -1e+30))
        probs = low(jax.nn.softmax(scores, axis=-1))
        return jnp.einsum('hrk,khd->rhd', probs, value, precision=lax.Precision.HIGHEST)
    heads = lax.map(jax.checkpoint(block), (query.reshape(length // rows, rows, HEADS, HD), pos.reshape(length // rows, rows)))
    heads = low(low_back(heads.reshape(length, D)))
    mid = seq + low_back(matmul(heads, wproj) + bproj)
    a2 = low(layer_norm(mid, gains[1], shifts[1]))
    hidden = low(gelu(low_back(matmul(a2, wup) + bup)))
    return mid + matmul(hidden, wdown) + bdown

def reference(tokens, slots, norm_gains, norm_shifts, qkv_weight, qv_bias, proj_weight, proj_bias, up_weight, up_bias, down_weight, down_bias, cotangent):
    params = tuple((p.astype(jnp.float32) for p in (norm_gains, norm_shifts, qkv_weight, qv_bias, proj_weight, proj_bias, up_weight, up_bias, down_weight, down_bias)))
    pos = positions(slots)

    def forward(params, seqs):
        return lax.map(lambda one: sequence_forward(params, one, pos), seqs)
    output, pull = jax.vjp(forward, params, tokens.astype(jnp.float32))
    grads, d_tokens = pull(cotangent.astype(jnp.float32))
    return (output.astype(jnp.bfloat16), d_tokens.astype(jnp.bfloat16), grads[0], grads[1], grads[2], grads[3], grads[4], grads[5], grads[6], grads[7], grads[8], grads[9])
```

```python
import functools
import math

import jax
import jax.numpy as jnp
from jax import lax
from jax.experimental import pallas as pl
from jax.experimental.pallas import tpu as pltpu
from jax.sharding import PartitionSpec as P

AXES = ("ctx", "wt")
F32 = jnp.float32
BF16 = jnp.bfloat16


def standardize(values):
    centred = values - jnp.mean(values, axis=-1, keepdims=True)
    scale = lax.rsqrt(jnp.mean(centred * centred, axis=-1, keepdims=True) + 1e-05)
    return (centred * scale, scale)


def finish_norm(scaled, normed, scale):
    inner = (
        scaled
        - jnp.mean(scaled, axis=-1, keepdims=True)
        - normed * jnp.mean(scaled * normed, axis=-1, keepdims=True)
    )
    return scale * inner


def gelu(values):
    return (
        0.5
        * values
        * (1.0 + jnp.tanh(0.7978845608028654 * (values + 0.044715 * values * values * values)))
    )


def dot(left, right):
    return jnp.dot(left, right, preferred_element_type=F32)


def over_rows(left, right):
    return lax.dot_general(left, right, (((0,), (0,)), ((), ())), preferred_element_type=F32)


def by_transpose(left, right):
    return lax.dot_general(left, right, (((1,), (1,)), ((), ())), preferred_element_type=F32)


def add_low(left, right):
    return (left.astype(F32) + right.astype(F32)).astype(BF16)


UNROLLED = 1024


def for_tiles(one, length, tile, key_axis):
    if length <= UNROLLED:
        shape = (tile, tile)
        key = lax.broadcasted_iota(jnp.int32, shape, key_axis)
        query = lax.broadcasted_iota(jnp.int32, shape, 1 - key_axis)
        for turn in range(length // tile):
            one(turn, turn * tile, pl.ds(turn * tile, tile), key <= query)
        return

    def turn_of(turn, carry):
        shape = (tile, length) if key_axis else (length, tile)
        key = lax.broadcasted_iota(jnp.int32, shape, key_axis)
        query = lax.broadcasted_iota(jnp.int32, shape, 1 - key_axis)
        one(turn, 0, pl.ds(0, length), key <= query + turn * tile)
        return carry

    lax.fori_loop(0, length // tile, turn_of, 0)


def attn_forward_kernel(tile, block, place_ref, qkv_ref, *refs):
    outs, (lse_ref, qs, ks, vs, os) = refs[:-5], refs[-5:]
    length, wide = os.shape

    for i in range(length // block):
        here = pl.ds(pl.multiple_of(place_ref[i] * block, block), block)
        there = slice(i * block, (i + 1) * block)
        qs[here, :] = qkv_ref[there, 0:wide] * 0.125
        ks[here, :] = qkv_ref[there, wide : 2 * wide]
        vs[here, :] = qkv_ref[there, 2 * wide : 3 * wide]
    lane = lax.broadcasted_iota(jnp.int32, (tile, 128), 1)

    def one(turn, before, near, allowed):
        mine = pl.ds(turn * tile, tile)
        stats = jnp.zeros((tile, 128), F32)
        for pair in range(wide // 128):
            cols = slice(pair * 128, (pair + 1) * 128)
            q = qs[mine, cols]
            halves = []
            for half in range(2):
                keep = (lane >= 64) if half else (lane < 64)
                qh = jnp.where(keep, q, jnp.zeros_like(q))
                edge = by_transpose(qh, ks[near, cols])
                edge = jnp.where(allowed, edge, -1e30)
                most = jnp.max(edge, axis=1, keepdims=True)
                if before:
                    past = by_transpose(qh, ks[0:before, cols])
                    most = jnp.maximum(most, jnp.max(past, axis=1, keepdims=True))
                edge = jnp.exp(edge - most)
                total = jnp.sum(edge, axis=1, keepdims=True)
                acc = dot(edge.astype(BF16), vs[near, cols])
                if before:
                    past = jnp.exp(past - most)
                    total = total + jnp.sum(past, axis=1, keepdims=True)
                    acc = acc + dot(past.astype(BF16), vs[0:before, cols])
                halves.append(acc / total)
                stats = jnp.where(lane == 2 * pair + half, most + jnp.log(total), stats)
            os[mine, cols] = jnp.where(lane < 64, halves[0], halves[1]).astype(BF16)
        lse_ref[mine, :] = stats

    for_tiles(one, length, tile, 1)

    for i in range(length // block):
        here = pl.ds(pl.multiple_of(place_ref[i] * block, block), block)
        outs[i // 2][(i % 2) * block : (i % 2 + 1) * block, :] = os[here, :]


def attn_backward_kernel(tile, block, place_ref, qkv_ref, lse_ref, *refs):
    grads, (out_ref, qs, ks, vs, gs, dq, dk, dv) = refs[:-8], refs[-8:]
    length, wide = gs.shape
    for i in range(length // block):
        here = pl.ds(pl.multiple_of(place_ref[i] * block, block), block)
        there = slice(i * block, (i + 1) * block)
        qs[here, :] = qkv_ref[there, 0:wide] * 0.125
        ks[here, :] = qkv_ref[there, wide : 2 * wide]
        vs[here, :] = qkv_ref[there, 2 * wide : 3 * wide]
        gs[here, :] = grads[i // 2][(i % 2) * block : (i % 2 + 1) * block, :]
    lane = lax.broadcasted_iota(jnp.int32, (tile, 128), 1)
    alone = length <= UNROLLED
    if not alone:
        dk[...] = jnp.zeros_like(dk)
        dv[...] = jnp.zeros_like(dv)

    def one(turn, before, near, allowed):
        mine = pl.ds(turn * tile, tile)
        lse = lse_ref[mine, :].T
        for pair in range(wide // 128):
            cols = slice(pair * 128, (pair + 1) * 128)
            q, g = qs[mine, cols], gs[mine, cols]
            halves = []
            for half in range(2):
                keep = (lane >= 64) if half else (lane < 64)
                qh = jnp.where(keep, q, jnp.zeros_like(q))
                gh = jnp.where(keep, g, jnp.zeros_like(g))
                row = lse[2 * pair + half : 2 * pair + half + 1, :]
                edge_p = by_transpose(ks[near, cols], qh)
                edge_p = jnp.where(allowed, jnp.exp(edge_p - row), 0.0)
                edge_t = edge_p * by_transpose(vs[near, cols], gh)
                delta = jnp.sum(edge_t, axis=0, keepdims=True)
                if before:
                    past_p = jnp.exp(by_transpose(ks[0:before, cols], qh) - row)
                    past_t = past_p * by_transpose(vs[0:before, cols], gh)
                    delta = delta + jnp.sum(past_t, axis=0, keepdims=True)
                edge_s = (edge_t - edge_p * delta).astype(BF16)
                own_v = dot(edge_p.astype(BF16), gh)
                own_k = dot(edge_s, qh)
                if half or not alone:
                    dv[near, cols] += own_v
                    dk[near, cols] += own_k
                else:
                    dv[near, cols] = own_v
                    dk[near, cols] = own_k
                acc = over_rows(edge_s, ks[near, cols])
                if before:
                    past_s = (past_t - past_p * delta).astype(BF16)
                    dv[0:before, cols] += dot(past_p.astype(BF16), gh)
                    dk[0:before, cols] += dot(past_s, qh)
                    acc = acc + over_rows(past_s, ks[0:before, cols])
                halves.append(acc)
            dq[mine, cols] = (jnp.where(lane < 64, halves[0], halves[1]) * 0.125).astype(BF16)

    for_tiles(one, length, tile, 0)

    for i in range(length // block):
        here = pl.ds(pl.multiple_of(place_ref[i] * block, block), block)
        there = slice(i * block, (i + 1) * block)
        out_ref[there, 0:wide] = dq[here, :]
        out_ref[there, wide : 2 * wide] = dk[here, :].astype(BF16)
        out_ref[there, 2 * wide : 3 * wide] = dv[here, :].astype(BF16)


SMEM = pl.BlockSpec(memory_space=pltpu.SMEM)
VMEM = pl.BlockSpec(memory_space=pltpu.VMEM)
LIMIT = 48 * 1024 * 1024


def attn_forward(qkv, place, block, tile):
    length, wide = qkv.shape[0], qkv.shape[1] // 3
    n = length // (2 * block)
    *outs, lse = pl.pallas_call(
        functools.partial(attn_forward_kernel, tile, block),
        out_shape=(jax.ShapeDtypeStruct((2 * block, wide), BF16),) * n
        + (jax.ShapeDtypeStruct((length, 128), F32),),
        in_specs=[SMEM, VMEM],
        out_specs=(VMEM,) * (n + 1),
        scratch_shapes=[pltpu.VMEM((length, wide), BF16)] * 4,
        compiler_params=pltpu.CompilerParams(vmem_limit_bytes=LIMIT),
        cost_estimate=pl.CostEstimate(
            flops=4 * length * length * wide,
            bytes_accessed=length * wide * 10,
            transcendentals=length * length * wide // 128,
        ),
    )(place, qkv)
    return outs, lse


def attn_backward(qkv, grads, lse, place, block, tile):
    length, wide = qkv.shape[0], qkv.shape[1] // 3
    return pl.pallas_call(
        functools.partial(attn_backward_kernel, tile, block),
        out_shape=jax.ShapeDtypeStruct((length, 3 * wide), BF16),
        in_specs=[SMEM] + [VMEM] * (2 + len(grads)),
        out_specs=VMEM,
        scratch_shapes=[pltpu.VMEM((length, wide), BF16)] * 5
        + [pltpu.VMEM((length, wide), F32)] * 2,
        compiler_params=pltpu.CompilerParams(vmem_limit_bytes=LIMIT),
        cost_estimate=pl.CostEstimate(
            flops=10 * length * length * wide,
            bytes_accessed=length * wide * 16,
            transcendentals=length * length * wide // 128,
        ),
    )(place, qkv, lse, *grads)


def rearrange(kernel, outs, numbers, arrays, scratch=()):
    size = sum(math.prod(o.shape) * o.dtype.itemsize for o in (*outs, *arrays))
    return pl.pallas_call(
        kernel,
        out_shape=tuple(jax.ShapeDtypeStruct(o.shape, o.dtype) for o in outs),
        in_specs=[SMEM] + [VMEM] * len(arrays),
        out_specs=(VMEM,) * len(outs),
        scratch_shapes=list(scratch),
        compiler_params=pltpu.CompilerParams(vmem_limit_bytes=LIMIT),
        cost_estimate=pl.CostEstimate(flops=0, bytes_accessed=size, transcendentals=0),
    )(jnp.stack(numbers).astype(jnp.int32), *arrays)


def shaped(shape, dtype=BF16):
    return jax.ShapeDtypeStruct(shape, dtype)


class Heads:
    def __init__(self, n, width):
        self.n, self.width = n, width
        self.full, self.rest = width // 128, width % 128
        self.slots = -(-(self.full + (self.rest > 0)) // n)
        self.wide = 128 * self.slots

    def pick_kernel(self, numbers, from_ref, out_ref):
        rows = from_ref.shape[0]
        for t in range(3):
            base = t * self.width
            first, off = base // 128, base % 128
            for j in range(self.slots):
                to = slice((t * self.slots + j) * 128, (t * self.slots + j + 1) * 128)
                p = j * self.n + numbers[0]

                @pl.when(p < self.full)
                def _():
                    start = pl.multiple_of((first + p) * 128, 128)
                    if off:
                        out_ref[:, to] = from_ref[:, pl.ds(start, 256)][:, off : off + 128]
                    else:
                        out_ref[:, to] = from_ref[:, pl.ds(start, 128)]

                @pl.when(p >= self.full)
                def _():
                    out_ref[:, to] = jnp.zeros((rows, 128), out_ref.dtype)

                if self.rest:
                    at = base + self.full * 128

                    @pl.when(p == self.full)
                    def _():
                        out_ref[:, to.start : to.start + self.rest] = from_ref[
                            :, at : at + self.rest
                        ]

    def pick(self, weight, c):
        out = shaped((weight.shape[0], 3 * self.wide))
        return rearrange(self.pick_kernel, [out], [c], [weight])[0]

    def join_kernel(self, numbers, *refs):
        out_ref = refs[-1]
        for d in range(self.n):
            for j in range(self.slots):
                p = j * self.n + (numbers[0] ^ d)
                value = refs[d].at[:, j * 128 : (j + 1) * 128]

                @pl.when(p < self.full)
                def _():
                    out_ref[:, pl.ds(pl.multiple_of(p * 128, 128), 128)] = value[...]

                if self.rest:

                    @pl.when(p == self.full)
                    def _():
                        out_ref[:, self.full * 128 :] = value[:, : self.rest]

    def join(self, blocks, c):
        out = shaped((blocks[0].shape[0], self.width))
        return rearrange(self.join_kernel, [out], [c], blocks)[0]

    def split_kernel(self, numbers, from_ref, *outs):
        rows = from_ref.shape[0]
        for d in range(self.n):
            for j in range(self.slots):
                p = j * self.n + (numbers[0] ^ d)
                to = slice(j * 128, (j + 1) * 128)

                @pl.when(p < self.full)
                def _():
                    outs[d][:, to] = from_ref[:, pl.ds(pl.multiple_of(p * 128, 128), 128)]

                @pl.when(p >= self.full)
                def _():
                    outs[d][:, to] = jnp.zeros((rows, 128), BF16)

                if self.rest:

                    @pl.when(p == self.full)
                    def _():
                        outs[d][:, to.start : to.start + self.rest] = from_ref[
                            :, self.full * 128 :
                        ]

    def split(self, value, c):
        out = shaped((value.shape[0], self.wide))
        return rearrange(self.split_kernel, [out] * self.n, [c], [value])

    def here(self, values, c):
        lead = values.shape[:-1]
        values = jnp.pad(values, [(0, 0)] * len(lead) + [(0, self.n * self.wide - self.width)])
        values = values.reshape(lead + (self.slots, self.n, 128))
        return lax.dynamic_index_in_dim(values, c, len(lead) + 1, False).reshape(
            lead + (self.wide,)
        )

    def back(self, values, c):
        lead = values.shape[:-1]
        zeros = jnp.zeros(lead + (self.slots, self.n, 128), values.dtype)
        values = values.reshape(lead + (self.slots, 1, 128))
        values = lax.dynamic_update_slice(zeros, values, (0,) * (len(lead) + 1) + (c, 0))
        return values.reshape(lead + (self.n * self.wide,))[..., : self.width]


def cut_kernel(per, numbers, from_ref, *outs):
    for r, out_ref in enumerate(outs):
        for part in range(from_ref.shape[1] // per):

            @pl.when(numbers[r] == part)
            def _():
                out_ref[...] = from_ref[:, part * per : (part + 1) * per]


def place_kernel(numbers, *refs):
    out_ref = refs[-1]
    for r, ref in enumerate(refs[:-1]):
        size = ref.shape[0]
        out_ref[pl.ds(pl.multiple_of(numbers[r] * size, 16), size), :] = ref[...]


def lay_kernel(plan, numbers, *refs):
    blocks, out_ref, held = refs[:-2], refs[-2], refs[-1]
    for r, ref in enumerate(blocks):
        held[numbers[r]] = ref[...]
    for b, from_rows, from_cols, rows, cols in plan:
        out_ref[rows, cols] = held[b, from_rows, from_cols].astype(F32)


def lay(blocks, numbers, plan, shape):
    steps = [
        (b, slice(r, r + h), slice(q, q + v), slice(tr, tr + h), slice(tq, tq + v))
        for b, (r, q), (h, v), (tr, tq) in plan
    ]
    scratch = [pltpu.VMEM((len(blocks),) + blocks[0].shape, BF16)]
    kernel = functools.partial(lay_kernel, steps)
    return rearrange(kernel, [shaped(shape, F32)], numbers, blocks, scratch)[0]


class Links:
    def __init__(self):
        self.n, self.m = lax.axis_size("ctx"), lax.axis_size("wt")
        self.nz = self.n // 2
        self.c, self.w = lax.axis_index("ctx"), lax.axis_index("wt")
        self.z, self.y = self.c // 2, self.c % 2

    def swap(self, value, dc, dw):
        pairs = [
            (c * self.m + w, (c ^ dc) * self.m + (w ^ dw))
            for c in range(self.n)
            for w in range(self.m)
        ]
        return lax.ppermute(value, AXES, pairs)

    def core(self, value):
        return self.swap(value, 0, 1)

    def x(self, value):
        return self.swap(value, 0, 2)

    def yy(self, value):
        return self.swap(value, 1, 0)


    def gather_wt(self, value):
        across = self.x(value)
        return [value, self.core(value), across, self.core(across)]

    def rows_wt(self, blocks):
        size, cols = blocks[0].shape
        return rearrange(
            place_kernel,
            [shaped((self.m * size, cols))],
            [self.w ^ r for r in range(self.m)],
            blocks,
        )[0]

    def trade_wt(self, pieces):
        far = self.x(pieces[3])
        return [pieces[0], self.core(pieces[1]), self.x(pieces[2]), self.core(far)]

    def reduce_wt(self, pieces):
        other = add_low(pieces[2], self.core(pieces[3]))
        mine = add_low(pieces[0], self.core(pieces[1]))
        return add_low(mine, self.x(other))


    def gather_ctx(self, value):
        far = [value] + [self.swap(value, 2 * d, 0) for d in range(1, self.nz)]
        return [part for one in far for part in (one, self.yy(one))]

    def sum_z(self, pieces):
        come = [self.swap(pieces[d], 2 * d, 0) for d in range(1, self.nz)]
        return sum((part.astype(F32) for part in come), pieces[0].astype(F32))


    def gather_plane(self, value):
        mine = [value, self.x(value), self.yy(value), self.swap(value, 1, 2)]
        return jnp.concatenate(mine + [self.core(part) for part in mine])

    def sum_plane(self, near, far):
        mine = add_low(near, self.core(far))
        size = mine.shape[0] // 4
        parts = [mine[i * size : (i + 1) * size] for i in range(4)]
        come = [self.swap(parts[3], 1, 2), self.yy(parts[2]), self.x(parts[1])]
        return sum((part.astype(F32) for part in come), parts[0].astype(F32))


def on_device(
    tokens,
    slots,
    norm_gains,
    norm_shifts,
    qkv_weight,
    qv_bias,
    proj_weight,
    proj_bias,
    up_weight,
    up_bias,
    down_weight,
    down_bias,
    cotangent,
):
    links = Links()
    n, m, nz, c, w, z, y = links.n, links.m, links.nz, links.c, links.w, links.z, links.y
    _, rows, width = tokens.shape
    heads = Heads(n, width)
    share = width // m
    block = rows // 2
    length = n * rows
    hid = up_weight.shape[1]
    per = hid // (2 * m)
    tile = 256 if length <= UNROLLED else 128
    near = rows * m

    own = tokens[0]
    seen = jnp.concatenate(links.gather_ctx(own))
    wqkv = links.rows_wt(links.gather_wt(heads.pick(qkv_weight, c)))

    small = jnp.concatenate(
        [
            norm_gains.reshape(-1),
            norm_shifts.reshape(-1),
            qv_bias.reshape(-1),
            proj_bias,
            down_bias,
            up_bias,
        ]
    )
    small = jnp.stack(links.gather_wt(small[None])).reshape(m, -1)
    number = jnp.arange(m, dtype=jnp.int32)
    small = dot((number[:, None] == (number[None, :] ^ w)).astype(BF16), small)
    pairs = small[:, : 6 * share].reshape(m, 3, 2, share).transpose(1, 2, 0, 3).reshape(3, 2, width)
    gains, shifts, qvb = pairs[0], pairs[1], pairs[2]
    bproj = small[:, 6 * share : 7 * share].reshape(width)
    bdown = small[:, 7 * share : 8 * share].reshape(width)
    bup = lax.dynamic_index_in_dim(small[:, 8 * share :].reshape(m * 2, per), w * 2 + y, 0, False)

    a1 = (standardize(seen.astype(F32))[0] * gains[0] + shifts[0]).astype(BF16)
    qvb_here = heads.here(qvb, c)
    bias = jnp.concatenate([qvb_here[0], jnp.zeros((heads.wide,), F32), qvb_here[1]])
    qkv = (dot(a1, wqkv) + bias).astype(BF16)

    table = jnp.arange(slots.shape[0], dtype=jnp.int32)
    wanted = (((table // 2) ^ c) * 2 + table % 2)[:, None] == table[None, :]
    place = jnp.sum(jnp.where(wanted, slots[None, :], 0), axis=1)

    heads_out, lse = attn_forward(qkv, place, block, tile)

    wproj = links.rows_wt(links.gather_wt(proj_weight))
    pieces = rearrange(
        functools.partial(cut_kernel, per),
        [shaped((share, per))] * m,
        [(w ^ r) * 2 + y for r in range(m)],
        [up_weight],
    )
    wup = links.rows_wt(links.trade_wt(pieces))
    wdown = lax.dynamic_slice_in_dim(down_weight, y * per, per, 0)
    grad_out = cotangent[0]
    grad_out_plane = links.gather_plane(grad_out)

    attended = heads.join(
        [heads_out[0]] + [links.swap(heads_out[d], d, 0) for d in range(1, n)], c
    )
    mid = own.astype(F32) + dot(attended, wproj) + bproj
    normed2, scale2 = standardize(mid)
    a2 = (normed2 * gains[1] + shifts[1]).astype(BF16)

    a2_plane = links.gather_plane(a2)
    pre = dot(a2_plane, wup) + bup
    activated, gelu_pull = jax.vjp(gelu, pre)
    hidden = activated.astype(BF16)
    grad_pre = gelu_pull(by_transpose(grad_out_plane, wdown))[0].astype(BF16)
    grad_a2 = links.sum_plane(
        by_transpose(grad_pre[:near], wup).astype(BF16),
        by_transpose(grad_pre[near:], wup).astype(BF16),
    )
    step = -(-(-(-per // nz)) // 8) * 8
    d_down = over_rows(hidden, grad_out_plane).astype(BF16)
    d_down = jnp.pad(d_down, [(0, step * nz - per), (0, 0)])
    d_down = links.sum_z(
        [lax.dynamic_slice_in_dim(d_down, (z ^ d) * step, step, 0) for d in range(nz)]
    ).astype(BF16)
    d_up = over_rows(a2_plane, grad_pre).astype(BF16)
    d_up = links.trade_wt(
        [lax.dynamic_slice_in_dim(d_up, (w ^ r) * share, share, 0) for r in range(m)]
    )
    cut = nz // m
    d_up = jnp.stack(d_up).reshape(m, share, cut, per // cut).transpose(0, 2, 1, 3)

    def up_term(d):
        b = z ^ d
        return lax.dynamic_slice(
            d_up, (w ^ (b // cut), b % cut, 0, 0), (1, 1, share, per // cut)
        ).reshape(share, per // cut)

    d_up = links.sum_z([up_term(d) for d in range(nz)]).astype(BF16)

    grad_out32 = grad_out.astype(F32)
    d_gain2 = jnp.sum(grad_a2 * normed2, axis=0)
    d_shift2 = jnp.sum(grad_a2, axis=0)
    grad_mid = grad_out32 + finish_norm(grad_a2 * gains[1], normed2, scale2)
    grad_proj = grad_mid.astype(BF16)

    grad_heads = heads.split(by_transpose(grad_proj, wproj).astype(BF16), c)
    grad_heads = [grad_heads[0]] + [links.swap(grad_heads[d], d, 0) for d in range(1, n)]
    grad_qkv = attn_backward(qkv, grad_heads, lse, place, block, tile)

    terms = []
    for d in [*range(1, nz), 0]:
        part = grad_qkv[2 * d * rows : 2 * (d + 1) * rows]
        other = by_transpose(part[rows:], wqkv).astype(BF16)
        terms.append(add_low(by_transpose(part[:rows], wqkv), links.yy(other)))
    grad_a1 = links.sum_z(terms[-1:] + terms[:-1])
    d_qkv = over_rows(a1, grad_qkv).astype(BF16)
    d_qkv = links.reduce_wt(
        [lax.dynamic_slice_in_dim(d_qkv, (w ^ r) * share, share, 0) for r in range(m)]
    )

    output = (
        mid
        + links.sum_plane(
            dot(hidden[:near], wdown).astype(BF16), dot(hidden[near:], wdown).astype(BF16)
        )
        + bdown
    )

    d_proj = over_rows(attended, grad_proj).astype(BF16)
    d_proj = links.reduce_wt(
        [lax.dynamic_slice_in_dim(d_proj, (w ^ r) * share, share, 0) for r in range(m)]
    )
    part = -(-(-(-share // n)) // 8) * 8
    d_proj = jnp.pad(d_proj, [(0, n * part - share), (0, 0)]).reshape(nz, 2, part, width)
    d_proj = add_low(
        lax.dynamic_index_in_dim(d_proj, y, 1, False),
        links.yy(lax.dynamic_index_in_dim(d_proj, 1 - y, 1, False)),
    )
    d_proj = links.sum_z(
        [lax.dynamic_index_in_dim(d_proj, z ^ d, 0, False) for d in range(nz)]
    ).astype(BF16)

    numbers = [c ^ d for d in range(n)]
    plan = [
        (b, (0, 0), (min(step, per - (b // 2) * step), width), ((b % 2) * per + (b // 2) * step, 0))
        for b in range(n)
        if (b // 2) * step < per
    ]
    d_down_weight = lay(links.gather_ctx(d_down), numbers, plan, (2 * per, width))
    size = per // cut
    plan = [
        (
            b,
            (0, 0),
            (share, size),
            (0, (b // 2 // cut) * 2 * per + (b % 2) * per + (b // 2 % cut) * size),
        )
        for b in range(n)
    ]
    d_up_weight = lay(links.gather_ctx(d_up), numbers, plan, (share, hid))
    plan = [
        (b, (0, 0), (min(part, share - b * part), width), (b * part, 0))
        for b in range(n)
        if b * part < share
    ]
    d_proj_weight = lay(links.gather_ctx(d_proj), numbers, plan, (share, width))
    plan = [
        (
            p % n,
            (0, (t * heads.slots + p // n) * 128),
            (share, min(128, width - p * 128)),
            (0, t * width + p * 128),
        )
        for t in range(3)
        for p in range(-(-width // 128))
    ]
    d_qkv_weight = lay(links.gather_ctx(d_qkv), numbers, plan, (share, 3 * width))

    normed1, scale1 = standardize(own.astype(F32))
    d_gain1 = jnp.sum(grad_a1 * normed1, axis=0)
    d_shift1 = jnp.sum(grad_a1, axis=0)
    d_tokens = grad_mid + finish_norm(grad_a1 * gains[0], normed1, scale1)

    col_sums = heads.back(jnp.sum(grad_qkv.astype(F32), axis=0).reshape(3, heads.wide), c)
    d_up_bias = lax.dynamic_update_slice(
        jnp.zeros((m * 2, per), F32),
        jnp.sum(grad_pre.astype(F32), axis=0)[None],
        (w * 2 + y, 0),
    ).reshape(m, hid // m)
    vectors = jnp.stack(
        [
            d_gain1,
            d_gain2,
            d_shift1,
            d_shift2,
            col_sums[0],
            col_sums[2],
            jnp.sum(grad_proj.astype(F32), axis=0),
            jnp.sum(grad_out32, axis=0),
        ]
    ).reshape(8, m, share)
    vectors = jnp.concatenate([vectors.transpose(1, 0, 2).reshape(m, 8 * share), d_up_bias], axis=1)
    for dc, dw in [(0, 1), (0, 2)] + [(1 << i, 0) for i in range(n.bit_length() - 1)]:
        vectors = vectors + links.swap(vectors, dc, dw)
    vectors = lax.dynamic_index_in_dim(vectors, w, 0, False)
    eight = vectors[: 8 * share].reshape(8, share)

    return (
        output.astype(BF16)[None],
        d_tokens.astype(BF16)[None],
        eight[0:2],
        eight[2:4],
        d_qkv_weight,
        eight[4:6],
        d_proj_weight,
        eight[6],
        d_up_weight,
        vectors[8 * share :],
        d_down_weight,
        eight[7],
    )


def solution(mesh):
    rows, whole = P("wt", "ctx", None), P(None, "wt")
    weight, vector = P("wt", None), P("wt")
    return jax.shard_map(
        on_device,
        mesh=mesh,
        in_specs=(
            rows,
            P(),
            whole,
            whole,
            weight,
            whole,
            weight,
            vector,
            weight,
            vector,
            weight,
            vector,
            rows,
        ),
        out_specs=(
            rows,
            rows,
            whole,
            whole,
            weight,
            whole,
            weight,
            vector,
            weight,
            vector,
            weight,
            vector,
        ),
        check_vma=False,
    )
```

```python
import functools
import math

import jax
import jax.numpy as jnp
from jax import lax
from jax.experimental import pallas as pl
from jax.experimental.layout import Layout, with_layout_constraint
from jax.experimental.pallas import tpu as pltpu
from jax.sharding import PartitionSpec as P

AXES = ("ctx", "wt")
F32 = jnp.float32
BF16 = jnp.bfloat16


def standardize(values):
    centred = values - jnp.mean(values, axis=-1, keepdims=True)
    scale = lax.rsqrt(jnp.mean(centred * centred, axis=-1, keepdims=True) + 1e-05)
    return (centred * scale, scale)


def finish_norm(scaled, normed, scale):
    inner = (
        scaled
        - jnp.mean(scaled, axis=-1, keepdims=True)
        - normed * jnp.mean(scaled * normed, axis=-1, keepdims=True)
    )
    return scale * inner


def gelu(values):
    return (
        0.5
        * values
        * (1.0 + jnp.tanh(0.7978845608028654 * (values + 0.044715 * values * values * values)))
    )


def dot(left, right):
    return jnp.dot(left, right, preferred_element_type=F32)


def over_rows(left, right):
    return lax.dot_general(left, right, (((0,), (0,)), ((), ())), preferred_element_type=F32)


def by_transpose(left, right):
    return lax.dot_general(left, right, (((1,), (1,)), ((), ())), preferred_element_type=F32)


def add_low(left, right):
    return (left.astype(F32) + right.astype(F32)).astype(BF16)


UNROLLED = 1024
BUMP = 2
TURNS = "mdmuodmpuoudmupdgquqpqgudpqppuqgpp"


def for_tiles(one, length, tile, key_axis):
    if length <= UNROLLED:
        shape = (tile, tile)
        key = lax.broadcasted_iota(jnp.int32, shape, key_axis)
        query = lax.broadcasted_iota(jnp.int32, shape, 1 - key_axis)
        for turn in range(length // tile):
            one(turn, turn * tile, pl.ds(turn * tile, tile), key <= query)
        return

    def turn_of(turn, carry):
        shape = (tile, length) if key_axis else (length, tile)
        key = lax.broadcasted_iota(jnp.int32, shape, key_axis)
        query = lax.broadcasted_iota(jnp.int32, shape, 1 - key_axis)
        one(turn, 0, pl.ds(0, length), key <= query + turn * tile)
        return carry

    lax.fori_loop(0, length // tile, turn_of, 0)


def attn_forward_kernel(tile, block, place_ref, slots_ref, qkv_ref, out_ref, lse_ref, qs, ks, vs, os):
    length, wide = os.shape

    for i in range(length // block):
        here = pl.ds(pl.multiple_of(place_ref[i] * block, block), block)
        there = slice(i * block, (i + 1) * block)
        qs[here, :] = qkv_ref[there, 0:wide] * 0.125
        ks[here, :] = qkv_ref[there, wide : 2 * wide]
        vs[here, :] = qkv_ref[there, 2 * wide : 3 * wide]
    lane = lax.broadcasted_iota(jnp.int32, (tile, 128), 1)

    def one(turn, before, near, allowed):
        mine = pl.ds(turn * tile, tile)
        stats = jnp.zeros((tile, 128), F32)
        for pair in range(wide // 128):
            cols = slice(pair * 128, (pair + 1) * 128)
            q = qs[mine, cols]
            halves = []
            for half in range(2):
                keep = (lane >= 64) if half else (lane < 64)
                qh = jnp.where(keep, q, jnp.zeros_like(q))
                edge = by_transpose(qh, ks[near, cols])
                edge = jnp.where(allowed, edge, -1e30)
                most = jnp.max(edge, axis=1, keepdims=True)
                if before:
                    past = by_transpose(qh, ks[0:before, cols])
                    most = jnp.maximum(most, jnp.max(past, axis=1, keepdims=True))
                edge = jnp.exp(edge - most)
                total = jnp.sum(edge, axis=1, keepdims=True)
                acc = dot(edge.astype(BF16), vs[near, cols])
                if before:
                    past = jnp.exp(past - most)
                    total = total + jnp.sum(past, axis=1, keepdims=True)
                    acc = acc + dot(past.astype(BF16), vs[0:before, cols])
                halves.append(acc / total)
                stats = jnp.where(lane == 2 * pair + half, most + jnp.log(total), stats)
            os[mine, cols] = jnp.where(lane < 64, halves[0], halves[1]).astype(BF16)
        lse_ref[mine, :] = stats

    for_tiles(one, length, tile, 1)

    for i in range(length // block):
        here = pl.ds(pl.multiple_of(slots_ref[i] * block, block), block)
        out_ref[i // 2, (i % 2) * block : (i % 2 + 1) * block, :] = os[here, :]


def attn_backward_kernel(
    tile, block, place_ref, slots_ref, qkv_ref, lse_ref, grad_ref, out_ref, qs, ks, vs, gs, dq, dk, dv
):
    length, wide = gs.shape
    for i in range(length // block):
        here = pl.ds(pl.multiple_of(place_ref[i] * block, block), block)
        there = slice(i * block, (i + 1) * block)
        qs[here, :] = qkv_ref[there, 0:wide] * 0.125
        ks[here, :] = qkv_ref[there, wide : 2 * wide]
        vs[here, :] = qkv_ref[there, 2 * wide : 3 * wide]
        far = pl.ds(pl.multiple_of(slots_ref[i] * block, block), block)
        gs[far, :] = grad_ref[i // 2, (i % 2) * block : (i % 2 + 1) * block, :]
    lane = lax.broadcasted_iota(jnp.int32, (tile, 128), 1)
    alone = length <= UNROLLED
    if not alone:
        dk[...] = jnp.zeros_like(dk)
        dv[...] = jnp.zeros_like(dv)

    def one(turn, before, near, allowed):
        mine = pl.ds(turn * tile, tile)
        lse = lse_ref[mine, :].T
        for pair in range(wide // 128):
            cols = slice(pair * 128, (pair + 1) * 128)
            q, g = qs[mine, cols], gs[mine, cols]
            halves = []
            for half in range(2):
                keep = (lane >= 64) if half else (lane < 64)
                qh = jnp.where(keep, q, jnp.zeros_like(q))
                gh = jnp.where(keep, g, jnp.zeros_like(g))
                row = lse[2 * pair + half : 2 * pair + half + 1, :]
                edge_p = by_transpose(ks[near, cols], qh)
                edge_p = jnp.where(allowed, jnp.exp(edge_p - row), 0.0)
                edge_t = edge_p * by_transpose(vs[near, cols], gh)
                delta = jnp.sum(edge_t, axis=0, keepdims=True)
                if before:
                    past_p = jnp.exp(by_transpose(ks[0:before, cols], qh) - row)
                    past_t = past_p * by_transpose(vs[0:before, cols], gh)
                    delta = delta + jnp.sum(past_t, axis=0, keepdims=True)
                edge_s = (edge_t - edge_p * delta).astype(BF16)
                own_v = dot(edge_p.astype(BF16), gh)
                own_k = dot(edge_s, qh)
                if half or not alone:
                    dv[near, cols] += own_v
                    dk[near, cols] += own_k
                else:
                    dv[near, cols] = own_v
                    dk[near, cols] = own_k
                acc = over_rows(edge_s, ks[near, cols])
                if before:
                    past_s = (past_t - past_p * delta).astype(BF16)
                    dv[0:before, cols] += dot(past_p.astype(BF16), gh)
                    dk[0:before, cols] += dot(past_s, qh)
                    acc = acc + over_rows(past_s, ks[0:before, cols])
                halves.append(acc)
            dq[mine, cols] = (jnp.where(lane < 64, halves[0], halves[1]) * 0.125).astype(BF16)

    for_tiles(one, length, tile, 0)

    for i in range(length // block):
        here = pl.ds(pl.multiple_of(place_ref[i] * block, block), block)
        there = slice(i * block, (i + 1) * block)
        out_ref[there, 0:wide] = dq[here, :]
        out_ref[there, wide : 2 * wide] = dk[here, :].astype(BF16)
        out_ref[there, 2 * wide : 3 * wide] = dv[here, :].astype(BF16)


SMEM = pl.BlockSpec(memory_space=pltpu.SMEM)
VMEM = pl.BlockSpec(memory_space=pltpu.VMEM)
LIMIT = 48 * 1024 * 1024


def attn_forward(qkv, place, slots, block, tile):
    length, wide = qkv.shape[0], qkv.shape[1] // 3
    return pl.pallas_call(
        functools.partial(attn_forward_kernel, tile, block),
        out_shape=(
            jax.ShapeDtypeStruct((length // (2 * block), 2 * block, wide), BF16),
            jax.ShapeDtypeStruct((length, 128), F32),
        ),
        in_specs=[SMEM, SMEM, VMEM],
        out_specs=(VMEM, VMEM),
        scratch_shapes=[pltpu.VMEM((length, wide), BF16)] * 4,
        compiler_params=pltpu.CompilerParams(vmem_limit_bytes=LIMIT),
        cost_estimate=pl.CostEstimate(
            flops=4 * length * length * wide,
            bytes_accessed=length * wide * 10,
            transcendentals=length * length * wide // 128,
        ),
    )(place, slots, qkv)


def attn_backward(qkv, grads, lse, place, slots, block, tile):
    length, wide = qkv.shape[0], qkv.shape[1] // 3
    return pl.pallas_call(
        functools.partial(attn_backward_kernel, tile, block),
        out_shape=jax.ShapeDtypeStruct((length, 3 * wide), BF16),
        in_specs=[SMEM, SMEM, VMEM, VMEM, VMEM],
        out_specs=VMEM,
        scratch_shapes=[pltpu.VMEM((length, wide), BF16)] * 5
        + [pltpu.VMEM((length, wide), F32)] * 2,
        compiler_params=pltpu.CompilerParams(vmem_limit_bytes=LIMIT),
        cost_estimate=pl.CostEstimate(
            flops=10 * length * length * wide,
            bytes_accessed=length * wide * 16,
            transcendentals=length * length * wide // 128,
        ),
    )(place, slots, qkv, lse, grads)


def rearrange(kernel, outs, numbers, arrays, scratch=()):
    size = sum(math.prod(o.shape) * o.dtype.itemsize for o in (*outs, *arrays))
    return pl.pallas_call(
        kernel,
        out_shape=tuple(jax.ShapeDtypeStruct(o.shape, o.dtype) for o in outs),
        in_specs=[SMEM] + [VMEM] * len(arrays),
        out_specs=(VMEM,) * len(outs),
        scratch_shapes=list(scratch),
        compiler_params=pltpu.CompilerParams(vmem_limit_bytes=LIMIT),
        cost_estimate=pl.CostEstimate(flops=0, bytes_accessed=size, transcendentals=0),
    )(jnp.stack(numbers).astype(jnp.int32), *arrays)


def shaped(shape, dtype=BF16):
    return jax.ShapeDtypeStruct(shape, dtype)


class Heads:
    def __init__(self, n, width):
        self.n, self.width = n, width
        self.full, self.rest = width // 128, width % 128
        self.slots = -(-(self.full + (self.rest > 0)) // n)
        self.wide = 128 * self.slots

    def pick_kernel(self, numbers, from_ref, more_ref, out_ref):
        rows = from_ref.shape[0]
        out_ref[rows:, :] = more_ref[...]
        out_ref = out_ref.at[:rows]
        for t in range(3):
            base = t * self.width
            first, off = base // 128, base % 128
            for j in range(self.slots):
                to = slice((t * self.slots + j) * 128, (t * self.slots + j + 1) * 128)
                p = j * self.n + numbers[0]

                @pl.when(p < self.full)
                def _():
                    start = pl.multiple_of((first + p) * 128, 128)
                    if off:
                        out_ref[:, to] = from_ref[:, pl.ds(start, 256)][:, off : off + 128]
                    else:
                        out_ref[:, to] = from_ref[:, pl.ds(start, 128)]

                @pl.when(p >= self.full)
                def _():
                    out_ref[:, to] = jnp.zeros((rows, 128), out_ref.dtype)

                if self.rest:
                    at = base + self.full * 128

                    @pl.when(p == self.full)
                    def _():
                        out_ref[:, to.start : to.start + self.rest] = from_ref[
                            :, at : at + self.rest
                        ]

    def pick(self, weight, more, c):
        out = shaped((weight.shape[0] + more.shape[0], 3 * self.wide))
        return rearrange(self.pick_kernel, [out], [c], [weight, more])[0]

    def join_kernel(self, from_ref, out_ref):
        for p in range(self.full + (self.rest > 0)):
            size = min(128, self.width - p * 128)
            j, owner = divmod(p, self.n)
            out_ref[:, p * 128 : p * 128 + size] = from_ref[owner, :, j * 128 : j * 128 + size]

    def split_kernel(self, from_ref, out_ref):
        for p in range(self.n * self.slots):
            size = max(0, min(128, self.width - p * 128))
            j, owner = divmod(p, self.n)
            if size:
                out_ref[owner, :, j * 128 : j * 128 + size] = from_ref[:, p * 128 : p * 128 + size]
            if size < 128:
                out_ref[owner, :, j * 128 + size : (j + 1) * 128] = jnp.zeros(
                    (out_ref.shape[1], 128 - size), out_ref.dtype
                )

    def turned(self, kernel, value, shape):
        return pl.pallas_call(
            kernel,
            out_shape=shaped(shape),
            in_specs=[VMEM],
            out_specs=VMEM,
            cost_estimate=pl.CostEstimate(
                flops=0, bytes_accessed=4 * math.prod(shape), transcendentals=0
            ),
        )(value)

    def join(self, blocks):
        return self.turned(self.join_kernel, blocks, (blocks.shape[1], self.width))

    def split(self, value):
        return self.turned(self.split_kernel, value, (self.n, value.shape[0], self.wide))

    def here(self, values, c):
        lead = values.shape[:-1]
        values = jnp.pad(values, [(0, 0)] * len(lead) + [(0, self.n * self.wide - self.width)])
        values = values.reshape(lead + (self.slots, self.n, 128))
        return lax.dynamic_index_in_dim(values, c, len(lead) + 1, False).reshape(
            lead + (self.wide,)
        )

    def back(self, values, c):
        lead = values.shape[:-1]
        zeros = jnp.zeros(lead + (self.slots, self.n, 128), values.dtype)
        values = values.reshape(lead + (self.slots, 1, 128))
        values = lax.dynamic_update_slice(zeros, values, (0,) * (len(lead) + 1) + (c, 0))
        return values.reshape(lead + (self.n * self.wide,))[..., : self.width]


def cut_kernel(per, numbers, from_ref, *outs):
    r = 0
    for out_ref in outs:
        for k in range(out_ref.shape[0]):
            for part in range(from_ref.shape[1] // per):

                @pl.when(numbers[r] == part)
                def _():
                    out_ref[k] = from_ref[:, part * per : (part + 1) * per]

            r += 1


def place_kernel(size, numbers, *refs):
    out_ref, r = refs[-1], 0
    for ref in refs[:-1]:
        for k in range(ref.shape[0]):
            to = pl.ds(pl.multiple_of(numbers[r] * size, 16), size)
            out_ref[to, :] = ref[k, :size, :]
            r += 1


def lay_kernel(plan, numbers, *refs):
    blocks, out_ref, held = refs[:-2], refs[-2], refs[-1]
    r = 0
    for ref in blocks:
        for k in range(ref.shape[0]):
            held[numbers[r]] = ref[k]
            r += 1
    for b, from_rows, from_cols, rows, cols in plan:
        out_ref[rows, cols] = held[b, from_rows, from_cols].astype(F32)


def lay(blocks, numbers, plan, shape):
    steps = [
        (b, slice(r, r + h), slice(q, q + v), slice(tr, tr + h), slice(tq, tq + v))
        for b, (r, q), (h, v), (tr, tq) in plan
    ]
    scratch = [pltpu.VMEM((len(numbers),) + blocks[0].shape[1:], BF16)]
    kernel = functools.partial(lay_kernel, steps)
    return rearrange(kernel, [shaped(shape, F32)], numbers, blocks, scratch)[0]


def by_rows(value):
    return with_layout_constraint(value, Layout(major_to_minor=tuple(range(value.ndim))))


def after(value, *others):
    return lax.optimization_barrier((value,) + others)[0]


def together(*values):
    return lax.optimization_barrier(values)


class Links:
    def __init__(self):
        self.n, self.m = lax.axis_size("ctx"), lax.axis_size("wt")
        self.c, self.w = lax.axis_index("ctx"), lax.axis_index("wt")
        self.bits = [1 << i for i in range(self.n.bit_length() - 1)]

    def swap(self, value, dc, dw):
        pairs = [
            (c * self.m + w, (c ^ dc) * self.m + (w ^ dw))
            for c in range(self.n)
            for w in range(self.m)
        ]
        return lax.ppermute(value, AXES, pairs)

    def core(self, value):
        return self.swap(value, 0, 1)

    def x(self, value):
        return self.swap(value, 0, 2)


    def gather_wt(self, value, *others):
        near = jnp.stack([value, after(self.x(value), *others)])
        return [near, self.core(near)]

    def trade_wt(self, own, near, far):
        (far,) = yield [(far, 0, 2)]
        (come,) = yield [(jnp.concatenate([near, far[1:]]), 0, 1)]
        return [own, far[:1], come]

    def sum_wt(self, near, far):
        (come,) = yield [(far, 0, 1)]
        (far,) = yield [(add_low(near[1], come[1]), 0, 2)]
        return add_low(add_low(near[0], come[0]), far)

    def rows_wt(self, blocks, size, numbers=(0, 2, 1, 3)):
        return rearrange(
            functools.partial(place_kernel, size),
            [shaped((self.m * size, blocks[0].shape[2]))],
            [self.w ^ r for r in numbers],
            blocks,
        )[0]


    def gather(self, value, bits):
        blocks = value[None]
        for bit in bits:
            (come,) = yield [(blocks, bit, 0)]
            if bit != bits[-1]:
                blocks = jnp.concatenate([blocks, come])
        return [blocks, come]

    def gathered(self, bits):
        found = [0]
        for bit in bits:
            found = found + [d | bit for d in found]
        return found

    def halving(self, bits):
        found = [0]
        for bit in reversed(bits):
            found = [d | bit for d in found] + found
        return found

    def halve(self, terms, bits):
        for bit in bits:
            half = terms.shape[0] // 2
            (come,) = yield [(terms[:half], bit, 0)]
            terms = add_low(terms[half:], come)
        return terms[0]


    def gather_plane(self, value):
        parts = [value, self.x(value), self.swap(value, 2, 0), self.swap(value, 2, 2)]
        return jnp.concatenate(parts + [self.core(part) for part in parts])

    def sum_plane(self, near, far):
        (come,) = yield [(far, 0, 1)]
        mine = add_low(near(), come)
        size = mine.shape[0] // 4
        parts = [mine[i * size : (i + 1) * size] for i in range(4)]
        come = yield [(parts[3], 2, 2), (parts[2], 2, 0), (parts[1], 0, 2)]
        return sum((part.astype(F32) for part in come), parts[0].astype(F32))


class Traffic:
    AHEAD = 4

    def __init__(self, links, chains):
        self.links, self.chains, self.results = links, chains, {}
        self.come, self.last, self.open = {}, None, []

    def step(self, name):
        chain, come = self.chains[name], self.come.get(name)
        if come is not None:
            self.open = [part for part in self.open if not any(part is other for other in come)]
            come = [after(part, self.last) for part in come]
        try:
            sends = chain.send(come)
        except StopIteration as end:
            self.results[name] = end.value
            self.come.pop(name, None)
            self.chains.pop(name)
            return
        self.come[name] = []
        for value, dc, dw in sends:
            ties = [] if self.last is None else [self.last]
            if dc is not None:
                while len(self.open) > self.AHEAD:
                    ties.append(self.open.pop(0))
            self.last = after(value, *ties)
            if dc is None:
                come = lax.all_to_all(self.last, "ctx", 0, 0, tiled=True)
            else:
                come = self.links.swap(self.last, dc, dw)
                self.open.append(come)
            self.come[name].append(come)

    def run(self, turns):
        for name in turns:
            if name in self.chains:
                self.step(name)
        while self.chains:
            for name in list(self.chains):
                self.step(name)


def on_device(
    tokens,
    slots,
    norm_gains,
    norm_shifts,
    qkv_weight,
    qv_bias,
    proj_weight,
    proj_bias,
    up_weight,
    up_bias,
    down_weight,
    down_bias,
    cotangent,
):
    links = Links()
    n, m, c, w = links.n, links.m, links.c, links.w
    _, rows, width = tokens.shape
    heads = Heads(n, width)
    share = width // m
    block = rows // 2
    length = n * rows
    hid = up_weight.shape[1]
    per = hid // (2 * m)
    tile = 256 if length <= UNROLLED else 128
    near = rows * m
    nq = n // 2
    cut = nq // m

    def half_of(c):
        return (c >> 1) & 1

    def place_of(c):
        return ((c >> 2) << 1) | (c & 1)

    half, place_q = half_of(c), place_of(c)
    spread = links.bits[:1] + links.bits[2:]
    order = links.halving(links.bits)

    own = tokens[0]
    small = jnp.concatenate(
        [
            norm_gains.reshape(-1),
            norm_shifts.reshape(-1),
            qv_bias.reshape(-1),
            proj_bias,
            down_bias,
            up_bias,
        ]
    )
    entries = small.shape[0]
    more = -(-(-(-entries // (3 * heads.wide))) // 16) * 16
    small = jnp.pad(small, [(0, more * 3 * heads.wide - entries)]).reshape(more, 3 * heads.wide)
    seen = {0: own}
    for bit in reversed(links.bits[1:]):
        seen.update({d | bit: links.swap(seen[d], bit, 0) for d in list(seen)})
    firsts = [0] + [bit for bit in links.bits[1:]]
    rest = [d for d in seen if d not in firsts]
    seen[1] = links.swap(own, 1, 0)
    for batch in (firsts[1:], rest):
        sent = links.swap(jnp.concatenate([seen[d] for d in batch]), 1, 0)
        seen.update({d | 1: sent[i * rows : (i + 1) * rows] for i, d in enumerate(batch)})
    found = links.gather_wt(heads.pick(qkv_weight, small, c))
    wqkv = links.rows_wt(found, share)
    small = jnp.concatenate([part[:, share:].reshape(2, -1)[:, :entries] for part in found])
    seen = jnp.concatenate([seen[d] for d in order])

    far_bits = links.bits[:1:-1]
    bits = {
        "down": [*far_bits, 2, 1],
        "up": [*far_bits, 1, 2],
        "qkv": [*far_bits, 2, 1],
        "proj": [*far_bits, 1, 2],
        "up sum": [1, *far_bits],
        "down sum": [1, *far_bits],
        "proj sum": [1, 2, *far_bits],
    }
    pieces = rearrange(
        functools.partial(cut_kernel, per),
        [shaped((k, share, per)) for k in (1, 1, 2)],
        [(w ^ r) * 2 + half for r in range(m)],
        [up_weight],
    )
    pieces = [pieces[0], pieces[1], after(pieces[2], found[0])]
    wdown = lax.dynamic_slice_in_dim(down_weight, half * per, per, 0)
    grad_out = cotangent[0]

    number = jnp.arange(m, dtype=jnp.int32)
    sources = jnp.array([0, 2, 1, 3], jnp.int32) ^ w
    small = dot((number[:, None] == sources[None, :]).astype(BF16), small)
    vectors = small[:, : 6 * share].reshape(m, 3, 2, share).transpose(1, 2, 0, 3)
    gains, shifts, qvb = vectors.reshape(3, 2, width)
    bproj = small[:, 6 * share : 7 * share].reshape(width)
    bdown = small[:, 7 * share : 8 * share].reshape(width)
    bup = small[:, 8 * share :].reshape(m * 2, per)
    bup = lax.dynamic_index_in_dim(bup, w * 2 + half, 0, False)

    a1 = (standardize(seen.astype(F32))[0] * gains[0] + shifts[0]).astype(BF16)
    qvb_here = heads.here(qvb, c)
    bias = jnp.concatenate([qvb_here[0], jnp.zeros((heads.wide,), F32), qvb_here[1]])
    qkv = (dot(a1, wqkv) + bias).astype(BF16)

    table = jnp.arange(slots.shape[0], dtype=jnp.int32)
    wanted = jnp.array(order, jnp.int32)
    wanted = ((wanted[:, None] ^ c) * 2 + jnp.arange(2, dtype=jnp.int32)).reshape(-1)
    place = jnp.sum(jnp.where(wanted[:, None] == table[None, :], slots[None, :], 0), axis=1)

    grad_out_plane = links.gather_plane(after(grad_out, seen))
    heads_out, lse = attn_forward(qkv, place, slots, block, tile)

    wproj = links.gather_wt(after(proj_weight, found[0]), heads_out)
    wproj = links.rows_wt(wproj, share)
    attended = lax.all_to_all(heads_out, "ctx", 0, 0, tiled=True)
    attended = heads.join(after(attended, wproj))
    far = after(links.x(pieces[2]), attended)
    wup = [pieces[0], far[:1], links.core(jnp.concatenate([pieces[1], far[1:]]))]
    wup = links.rows_wt(wup, share)
    mid = own.astype(F32) + dot(attended, wproj) + bproj
    normed2, scale2 = standardize(mid)
    a2 = (normed2 * gains[1] + shifts[1]).astype(BF16)

    a2_plane = links.gather_plane(a2)
    grad_out32 = grad_out.astype(F32)
    middle = length // 2
    step = -(-(-(-per // nq)) // 8) * 8
    part = -(-(-(-share // n)) // 8) * 8
    kept = {}

    def main_chain():
        pre = dot(a2_plane, wup) + bup
        activated, gelu_pull = jax.vjp(gelu, pre)
        hidden = activated.astype(BF16)
        grad_pre = gelu_pull(by_transpose(grad_out_plane, wdown))[0].astype(BF16)
        kept.update(hidden=hidden, grad_pre=grad_pre)
        grad_a2 = yield from links.sum_plane(
            lambda: by_transpose(grad_pre[:near], wup),
            by_transpose(grad_pre[near:], wup).astype(BF16),
        )
        grad_mid = grad_out32 + finish_norm(grad_a2 * gains[1], normed2, scale2)
        grad_proj = grad_mid.astype(BF16)
        kept.update(grad_a2=grad_a2, grad_mid=grad_mid, grad_proj=grad_proj)
        grad_heads = heads.split(by_transpose(grad_proj, wproj).astype(BF16))
        word = after(jnp.zeros((8, 128), F32), grad_heads)
        (grad_heads,) = yield [(grad_heads, None, None)]
        for _ in range(BUMP):
            word = links.core(word)
        grad_heads = after(grad_heads, word)
        grad_qkv = attn_backward(qkv, grad_heads, lse, place, slots, block, tile)
        normed1 = standardize(after(seen, word).astype(F32))[0]
        other, mine = by_transpose(grad_qkv[:middle], wqkv), by_transpose(grad_qkv[middle:], wqkv)
        d_gain1 = jnp.sum(other * normed1[:middle] + mine * normed1[middle:], axis=0)
        kept.update(grad_qkv=grad_qkv, other=other.astype(BF16), mine=mine, d_gain1=d_gain1)

    def down_chain():
        found = by_rows(over_rows(kept["hidden"], grad_out_plane).astype(BF16))
        found = jnp.pad(found, [(0, step * nq - per), (0, 0)])
        found = [
            lax.dynamic_slice_in_dim(found, (place_q ^ place_of(d)) * step, step, 0)
            for d in links.halving(bits["down sum"])
        ]
        found = yield from links.halve(jnp.stack(found), bits["down sum"])
        return (yield from links.gather(found, bits["down"]))

    def up_chain():
        found = by_rows(over_rows(a2_plane, kept["grad_pre"]).astype(BF16))
        pieces = [lax.dynamic_slice_in_dim(found, (w ^ r) * share, share, 0) for r in range(m)]
        found = yield from links.trade_wt(pieces[0][None], pieces[1][None], jnp.stack(pieces[2:]))
        found = jnp.concatenate(found).reshape(m, share, cut, per // cut).transpose(0, 2, 1, 3)
        terms = []
        for d in links.halving(bits["up sum"]):
            b = place_q ^ place_of(d)
            r = w ^ (b // cut)
            r = (r & 1) * 2 + (r >> 1)
            term = lax.dynamic_slice(found, (r, b % cut, 0, 0), (1, 1, share, per // cut))
            terms.append(term[0, 0])
        found = yield from links.halve(jnp.stack(terms), bits["up sum"])
        return (yield from links.gather(found, bits["up"]))

    def output_chain():
        hidden = kept["hidden"]
        near_part = dot(hidden[:near], wdown).astype(BF16)
        far_part = dot(hidden[near:], wdown).astype(BF16)
        return (yield from links.sum_plane(lambda: near_part, far_part))

    def proj_chain():
        found = by_rows(over_rows(attended, kept["grad_proj"]).astype(BF16))
        pieces = [
            lax.dynamic_slice_in_dim(found, (w ^ r) * share, share, 0) for r in (0, 2, 1, 3)
        ]
        found = yield from links.sum_wt(jnp.stack(pieces[:2]), jnp.stack(pieces[2:]))
        found = jnp.pad(found, [(0, n * part - share), (0, 0)])
        found = [
            lax.dynamic_slice_in_dim(found, (c ^ d) * part, part, 0)
            for d in links.halving(bits["proj sum"])
        ]
        found = yield from links.halve(jnp.stack(found), bits["proj sum"])
        return (yield from links.gather(found, bits["proj"]))

    def input_chain():
        (come,) = yield [(kept["other"], 1, 0)]
        terms = add_low(kept["mine"], come).reshape(n // 2, rows, width)
        return (yield from links.halve(terms, links.bits[1:]))

    def qkv_chain():
        grad_a2, grad_proj, grad_qkv = (kept[name] for name in ("grad_a2", "grad_proj", "grad_qkv"))
        sums = jnp.sum(grad_qkv.astype(F32), axis=0)
        d_shift1 = dot(sums[None], wqkv.astype(F32).T)[0]
        sums = heads.back(sums.reshape(3, heads.wide), c)
        d_up_bias = lax.dynamic_update_slice(
            jnp.zeros((m * 2, per), F32),
            jnp.sum(kept["grad_pre"].astype(F32), axis=0)[None],
            (w * 2 + half, 0),
        ).reshape(m, hid // m)
        vectors = [
            kept["d_gain1"],
            jnp.sum(grad_a2 * normed2, axis=0),
            d_shift1,
            jnp.sum(grad_a2, axis=0),
            sums[0],
            sums[2],
            jnp.sum(grad_proj.astype(F32), axis=0),
            jnp.sum(grad_out32, axis=0),
        ]
        vectors = jnp.concatenate([v.reshape(m, share) for v in vectors] + [d_up_bias], axis=1)
        vectors = jnp.pad(vectors, [(0, 0), (0, more * 3 * heads.wide - entries)])
        vectors = vectors.astype(BF16).reshape(m * more, 3 * heads.wide)
        found = by_rows(over_rows(a1, grad_qkv).astype(BF16))
        pieces = [
            jnp.concatenate(
                [
                    lax.dynamic_slice_in_dim(found, (w ^ r) * share, share, 0),
                    lax.dynamic_slice_in_dim(vectors, (w ^ r) * more, more, 0),
                ]
            )
            for r in (0, 2, 1, 3)
        ]
        found = yield from links.sum_wt(jnp.stack(pieces[:2]), jnp.stack(pieces[2:]))
        return (yield from links.gather(found, bits["qkv"]))

    chains = {
        "m": main_chain(),
        "d": down_chain(),
        "u": up_chain(),
        "g": input_chain(),
        "q": qkv_chain(),
        "p": proj_chain(),
        "o": output_chain(),
    }
    traffic = Traffic(links, chains)
    traffic.run(TURNS)
    d_down, d_up, d_qkv, d_proj = (traffic.results[name] for name in "duqp")
    output, grad_a1 = traffic.results["o"], traffic.results["g"].astype(F32)
    grad_mid = kept["grad_mid"]

    output = mid + output + bdown
    own1, scale1 = standardize(own.astype(F32))
    d_tokens = grad_mid + finish_norm(grad_a1 * gains[0], own1, scale1)

    def owners(name):
        return [c ^ d for d in links.gathered(bits[name])]

    plan = [
        (
            b,
            (0, 0),
            (min(step, per - place_of(b) * step), width),
            (half_of(b) * per + place_of(b) * step, 0),
        )
        for b in range(n)
        if place_of(b) * step < per
    ]
    d_down_weight = lay(d_down, owners("down"), plan, (2 * per, width))
    size = per // cut
    plan = [
        (
            b,
            (0, 0),
            (share, size),
            (
                0,
                (place_of(b) // cut) * 2 * per + half_of(b) * per + (place_of(b) % cut) * size,
            ),
        )
        for b in range(n)
    ]
    d_up_weight = lay(d_up, owners("up"), plan, (share, hid))
    plan = [
        (b, (0, 0), (min(part, share - b * part), width), (b * part, 0))
        for b in range(n)
        if b * part < share
    ]
    d_proj_weight = lay(d_proj, owners("proj"), plan, (share, width))
    plan = [
        (
            p % n,
            (0, (t * heads.slots + p // n) * 128),
            (share, min(128, width - p * 128)),
            (0, t * width + p * 128),
        )
        for t in range(3)
        for p in range(-(-width // 128))
    ]
    d_qkv_weight = lay(d_qkv, owners("qkv"), plan, (share, 3 * width))
    vectors = sum(jnp.sum(part[:, share:].astype(F32), axis=0) for part in d_qkv)
    vectors = vectors.reshape(-1)[:entries]
    eight = vectors[: 8 * share].reshape(8, share)

    return (
        output.astype(BF16)[None],
        d_tokens.astype(BF16)[None],
        eight[0:2],
        eight[2:4],
        d_qkv_weight,
        eight[4:6],
        d_proj_weight,
        eight[6],
        d_up_weight,
        vectors[8 * share :],
        d_down_weight,
        eight[7],
    )


def solution(mesh):
    rows, whole = P("wt", "ctx", None), P(None, "wt")
    weight, vector = P("wt", None), P("wt")
    return jax.shard_map(
        on_device,
        mesh=mesh,
        in_specs=(
            rows,
            P(),
            whole,
            whole,
            weight,
            whole,
            weight,
            vector,
            weight,
            vector,
            weight,
            vector,
            rows,
        ),
        out_specs=(
            rows,
            rows,
            whole,
            whole,
            weight,
            whole,
            weight,
            vector,
            weight,
            vector,
            weight,
            vector,
        ),
        check_vma=False,
    )
```

```python
import functools
import math

import jax
import jax.numpy as jnp
from jax import lax
from jax.experimental import pallas as pl
from jax.experimental.layout import Layout, with_layout_constraint
from jax.experimental.pallas import tpu as pltpu
from jax.sharding import PartitionSpec as P

AXES = ("ctx", "wt")
F32 = jnp.float32
BF16 = jnp.bfloat16


def standardize(values):
    centred = values - jnp.mean(values, axis=-1, keepdims=True)
    scale = lax.rsqrt(jnp.mean(centred * centred, axis=-1, keepdims=True) + 1e-05)
    return (centred * scale, scale)


def finish_norm(scaled, normed, scale):
    inner = (
        scaled
        - jnp.mean(scaled, axis=-1, keepdims=True)
        - normed * jnp.mean(scaled * normed, axis=-1, keepdims=True)
    )
    return scale * inner


def gelu(values):
    return (
        0.5
        * values
        * (1.0 + jnp.tanh(0.7978845608028654 * (values + 0.044715 * values * values * values)))
    )


def dot(left, right):
    return jnp.dot(left, right, preferred_element_type=F32)


def over_rows(left, right):
    return lax.dot_general(left, right, (((0,), (0,)), ((), ())), preferred_element_type=F32)


def by_transpose(left, right):
    return lax.dot_general(left, right, (((1,), (1,)), ((), ())), preferred_element_type=F32)


def add_low(left, right):
    return (left.astype(F32) + right.astype(F32)).astype(BF16)


UNROLLED = 1024
BUMP = 2
SPLIT = ("down", "up", "qkv")
TURNS = "mdmudmpudupmgduqpugqdqpuopqpopuqpg"


def for_tiles(one, length, tile, key_axis):
    if length <= UNROLLED:
        shape = (tile, tile)
        key = lax.broadcasted_iota(jnp.int32, shape, key_axis)
        query = lax.broadcasted_iota(jnp.int32, shape, 1 - key_axis)
        for turn in range(length // tile):
            one(turn, turn * tile, pl.ds(turn * tile, tile), key <= query)
        return

    def turn_of(turn, carry):
        shape = (tile, length) if key_axis else (length, tile)
        key = lax.broadcasted_iota(jnp.int32, shape, key_axis)
        query = lax.broadcasted_iota(jnp.int32, shape, 1 - key_axis)
        one(turn, 0, pl.ds(0, length), key <= query + turn * tile)
        return carry

    lax.fori_loop(0, length // tile, turn_of, 0)


def attn_forward_kernel(tile, block, place_ref, slots_ref, qkv_ref, out_ref, lse_ref, qs, ks, vs, os):
    length, wide = os.shape

    for i in range(length // block):
        here = pl.ds(pl.multiple_of(place_ref[i] * block, block), block)
        there = slice(i * block, (i + 1) * block)
        qs[here, :] = qkv_ref[there, 0:wide] * 0.125
        ks[here, :] = qkv_ref[there, wide : 2 * wide]
        vs[here, :] = qkv_ref[there, 2 * wide : 3 * wide]
    lane = lax.broadcasted_iota(jnp.int32, (tile, 128), 1)

    def one(turn, before, near, allowed):
        mine = pl.ds(turn * tile, tile)
        stats = jnp.zeros((tile, 128), F32)
        for pair in range(wide // 128):
            cols = slice(pair * 128, (pair + 1) * 128)
            q = qs[mine, cols]
            halves = []
            for half in range(2):
                keep = (lane >= 64) if half else (lane < 64)
                qh = jnp.where(keep, q, jnp.zeros_like(q))
                edge = by_transpose(qh, ks[near, cols])
                edge = jnp.where(allowed, edge, -1e30)
                most = jnp.max(edge, axis=1, keepdims=True)
                if before:
                    past = by_transpose(qh, ks[0:before, cols])
                    most = jnp.maximum(most, jnp.max(past, axis=1, keepdims=True))
                edge = jnp.exp(edge - most)
                total = jnp.sum(edge, axis=1, keepdims=True)
                acc = dot(edge.astype(BF16), vs[near, cols])
                if before:
                    past = jnp.exp(past - most)
                    total = total + jnp.sum(past, axis=1, keepdims=True)
                    acc = acc + dot(past.astype(BF16), vs[0:before, cols])
                halves.append(acc / total)
                stats = jnp.where(lane == 2 * pair + half, most + jnp.log(total), stats)
            os[mine, cols] = jnp.where(lane < 64, halves[0], halves[1]).astype(BF16)
        lse_ref[mine, :] = stats

    for_tiles(one, length, tile, 1)

    for i in range(length // block):
        here = pl.ds(pl.multiple_of(slots_ref[i] * block, block), block)
        out_ref[i // 2, (i % 2) * block : (i % 2 + 1) * block, :] = os[here, :]


def attn_backward_kernel(
    tile, block, place_ref, slots_ref, qkv_ref, lse_ref, grad_ref, out_ref, qs, ks, vs, gs, dq, dk, dv
):
    length, wide = gs.shape
    for i in range(length // block):
        here = pl.ds(pl.multiple_of(place_ref[i] * block, block), block)
        there = slice(i * block, (i + 1) * block)
        qs[here, :] = qkv_ref[there, 0:wide] * 0.125
        ks[here, :] = qkv_ref[there, wide : 2 * wide]
        vs[here, :] = qkv_ref[there, 2 * wide : 3 * wide]
        far = pl.ds(pl.multiple_of(slots_ref[i] * block, block), block)
        gs[far, :] = grad_ref[i // 2, (i % 2) * block : (i % 2 + 1) * block, :]
    lane = lax.broadcasted_iota(jnp.int32, (tile, 128), 1)
    alone = length <= UNROLLED
    if not alone:
        dk[...] = jnp.zeros_like(dk)
        dv[...] = jnp.zeros_like(dv)

    def one(turn, before, near, allowed):
        mine = pl.ds(turn * tile, tile)
        lse = lse_ref[mine, :].T
        for pair in range(wide // 128):
            cols = slice(pair * 128, (pair + 1) * 128)
            q, g = qs[mine, cols], gs[mine, cols]
            halves = []
            for half in range(2):
                keep = (lane >= 64) if half else (lane < 64)
                qh = jnp.where(keep, q, jnp.zeros_like(q))
                gh = jnp.where(keep, g, jnp.zeros_like(g))
                row = lse[2 * pair + half : 2 * pair + half + 1, :]
                edge_p = by_transpose(ks[near, cols], qh)
                edge_p = jnp.where(allowed, jnp.exp(edge_p - row), 0.0)
                edge_t = edge_p * by_transpose(vs[near, cols], gh)
                delta = jnp.sum(edge_t, axis=0, keepdims=True)
                if before:
                    past_p = jnp.exp(by_transpose(ks[0:before, cols], qh) - row)
                    past_t = past_p * by_transpose(vs[0:before, cols], gh)
                    delta = delta + jnp.sum(past_t, axis=0, keepdims=True)
                edge_s = (edge_t - edge_p * delta).astype(BF16)
                own_v = dot(edge_p.astype(BF16), gh)
                own_k = dot(edge_s, qh)
                if half or not alone:
                    dv[near, cols] += own_v
                    dk[near, cols] += own_k
                else:
                    dv[near, cols] = own_v
                    dk[near, cols] = own_k
                acc = over_rows(edge_s, ks[near, cols])
                if before:
                    past_s = (past_t - past_p * delta).astype(BF16)
                    dv[0:before, cols] += dot(past_p.astype(BF16), gh)
                    dk[0:before, cols] += dot(past_s, qh)
                    acc = acc + over_rows(past_s, ks[0:before, cols])
                halves.append(acc)
            dq[mine, cols] = (jnp.where(lane < 64, halves[0], halves[1]) * 0.125).astype(BF16)

    for_tiles(one, length, tile, 0)

    for i in range(length // block):
        here = pl.ds(pl.multiple_of(place_ref[i] * block, block), block)
        there = slice(i * block, (i + 1) * block)
        out_ref[there, 0:wide] = dq[here, :]
        out_ref[there, wide : 2 * wide] = dk[here, :].astype(BF16)
        out_ref[there, 2 * wide : 3 * wide] = dv[here, :].astype(BF16)


SMEM = pl.BlockSpec(memory_space=pltpu.SMEM)
VMEM = pl.BlockSpec(memory_space=pltpu.VMEM)
LIMIT = 48 * 1024 * 1024


def attn_forward(qkv, place, slots, block, tile):
    length, wide = qkv.shape[0], qkv.shape[1] // 3
    return pl.pallas_call(
        functools.partial(attn_forward_kernel, tile, block),
        out_shape=(
            jax.ShapeDtypeStruct((length // (2 * block), 2 * block, wide), BF16),
            jax.ShapeDtypeStruct((length, 128), F32),
        ),
        in_specs=[SMEM, SMEM, VMEM],
        out_specs=(VMEM, VMEM),
        scratch_shapes=[pltpu.VMEM((length, wide), BF16)] * 4,
        compiler_params=pltpu.CompilerParams(vmem_limit_bytes=LIMIT),
        cost_estimate=pl.CostEstimate(
            flops=4 * length * length * wide,
            bytes_accessed=length * wide * 10,
            transcendentals=length * length * wide // 128,
        ),
    )(place, slots, qkv)


def attn_backward(qkv, grads, lse, place, slots, block, tile):
    length, wide = qkv.shape[0], qkv.shape[1] // 3
    return pl.pallas_call(
        functools.partial(attn_backward_kernel, tile, block),
        out_shape=jax.ShapeDtypeStruct((length, 3 * wide), BF16),
        in_specs=[SMEM, SMEM, VMEM, VMEM, VMEM],
        out_specs=VMEM,
        scratch_shapes=[pltpu.VMEM((length, wide), BF16)] * 5
        + [pltpu.VMEM((length, wide), F32)] * 2,
        compiler_params=pltpu.CompilerParams(vmem_limit_bytes=LIMIT),
        cost_estimate=pl.CostEstimate(
            flops=10 * length * length * wide,
            bytes_accessed=length * wide * 16,
            transcendentals=length * length * wide // 128,
        ),
    )(place, slots, qkv, lse, grads)


def rearrange(kernel, outs, numbers, arrays, scratch=()):
    size = sum(math.prod(o.shape) * o.dtype.itemsize for o in (*outs, *arrays))
    return pl.pallas_call(
        kernel,
        out_shape=tuple(jax.ShapeDtypeStruct(o.shape, o.dtype) for o in outs),
        in_specs=[SMEM] + [VMEM] * len(arrays),
        out_specs=(VMEM,) * len(outs),
        scratch_shapes=list(scratch),
        compiler_params=pltpu.CompilerParams(vmem_limit_bytes=LIMIT),
        cost_estimate=pl.CostEstimate(flops=0, bytes_accessed=size, transcendentals=0),
    )(jnp.stack(numbers).astype(jnp.int32), *arrays)


def shaped(shape, dtype=BF16):
    return jax.ShapeDtypeStruct(shape, dtype)


class Heads:
    def __init__(self, n, width):
        self.n, self.width = n, width
        self.full, self.rest = width // 128, width % 128
        self.slots = -(-(self.full + (self.rest > 0)) // n)
        self.wide = 128 * self.slots

    def pick_kernel(self, numbers, from_ref, more_ref, out_ref):
        rows = from_ref.shape[0]
        out_ref[rows:, :] = more_ref[...]
        out_ref = out_ref.at[:rows]
        for t in range(3):
            base = t * self.width
            first, off = base // 128, base % 128
            for j in range(self.slots):
                to = slice((t * self.slots + j) * 128, (t * self.slots + j + 1) * 128)
                p = j * self.n + numbers[0]

                @pl.when(p < self.full)
                def _():
                    start = pl.multiple_of((first + p) * 128, 128)
                    if off:
                        out_ref[:, to] = from_ref[:, pl.ds(start, 256)][:, off : off + 128]
                    else:
                        out_ref[:, to] = from_ref[:, pl.ds(start, 128)]

                @pl.when(p >= self.full)
                def _():
                    out_ref[:, to] = jnp.zeros((rows, 128), out_ref.dtype)

                if self.rest:
                    at = base + self.full * 128

                    @pl.when(p == self.full)
                    def _():
                        out_ref[:, to.start : to.start + self.rest] = from_ref[
                            :, at : at + self.rest
                        ]

    def pick(self, weight, more, c):
        out = shaped((weight.shape[0] + more.shape[0], 3 * self.wide))
        return rearrange(self.pick_kernel, [out], [c], [weight, more])[0]

    def join_kernel(self, from_ref, out_ref):
        for p in range(self.full + (self.rest > 0)):
            size = min(128, self.width - p * 128)
            j, owner = divmod(p, self.n)
            out_ref[:, p * 128 : p * 128 + size] = from_ref[owner, :, j * 128 : j * 128 + size]

    def split_kernel(self, from_ref, out_ref):
        for p in range(self.n * self.slots):
            size = max(0, min(128, self.width - p * 128))
            j, owner = divmod(p, self.n)
            if size:
                out_ref[owner, :, j * 128 : j * 128 + size] = from_ref[:, p * 128 : p * 128 + size]
            if size < 128:
                out_ref[owner, :, j * 128 + size : (j + 1) * 128] = jnp.zeros(
                    (out_ref.shape[1], 128 - size), out_ref.dtype
                )

    def turned(self, kernel, value, shape):
        return pl.pallas_call(
            kernel,
            out_shape=shaped(shape),
            in_specs=[VMEM],
            out_specs=VMEM,
            cost_estimate=pl.CostEstimate(
                flops=0, bytes_accessed=4 * math.prod(shape), transcendentals=0
            ),
        )(value)

    def join(self, blocks):
        return self.turned(self.join_kernel, blocks, (blocks.shape[1], self.width))

    def split(self, value):
        return self.turned(self.split_kernel, value, (self.n, value.shape[0], self.wide))

    def here(self, values, c):
        lead = values.shape[:-1]
        values = jnp.pad(values, [(0, 0)] * len(lead) + [(0, self.n * self.wide - self.width)])
        values = values.reshape(lead + (self.slots, self.n, 128))
        return lax.dynamic_index_in_dim(values, c, len(lead) + 1, False).reshape(
            lead + (self.wide,)
        )

    def back(self, values, c):
        lead = values.shape[:-1]
        zeros = jnp.zeros(lead + (self.slots, self.n, 128), values.dtype)
        values = values.reshape(lead + (self.slots, 1, 128))
        values = lax.dynamic_update_slice(zeros, values, (0,) * (len(lead) + 1) + (c, 0))
        return values.reshape(lead + (self.n * self.wide,))[..., : self.width]


def cut_kernel(per, numbers, from_ref, *outs):
    r = 0
    for out_ref in outs:
        for k in range(out_ref.shape[0]):
            for part in range(from_ref.shape[1] // per):

                @pl.when(numbers[r] == part)
                def _():
                    out_ref[k] = from_ref[:, part * per : (part + 1) * per]

            r += 1


def place_kernel(size, numbers, *refs):
    out_ref, r = refs[-1], 0
    for ref in refs[:-1]:
        for k in range(ref.shape[0]):
            to = pl.ds(pl.multiple_of(numbers[r] * size, 16), size)
            out_ref[to, :] = ref[k, :size, :]
            r += 1


def lay_kernel(plan, numbers, *refs):
    blocks, out_ref, held = refs[:-2], refs[-2], refs[-1]
    r = 0
    for ref in blocks:
        for k in range(ref.shape[0]):
            held[numbers[r]] = ref[k]
            r += 1
    for b, from_rows, from_cols, rows, cols in plan:
        out_ref[rows, cols] = held[b, from_rows, from_cols].astype(F32)


def lay(blocks, numbers, plan, shape):
    steps = [
        (b, slice(r, r + h), slice(q, q + v), slice(tr, tr + h), slice(tq, tq + v))
        for b, (r, q), (h, v), (tr, tq) in plan
    ]
    scratch = [pltpu.VMEM((len(numbers),) + blocks[0].shape[1:], BF16)]
    kernel = functools.partial(lay_kernel, steps)
    return rearrange(kernel, [shaped(shape, F32)], numbers, blocks, scratch)[0]


def by_rows(value):
    return with_layout_constraint(value, Layout(major_to_minor=tuple(range(value.ndim))))


def after(value, *others):
    return lax.optimization_barrier((value,) + others)[0]


def together(*values):
    return lax.optimization_barrier(values)


class Links:
    def __init__(self):
        self.n, self.m = lax.axis_size("ctx"), lax.axis_size("wt")
        self.c, self.w = lax.axis_index("ctx"), lax.axis_index("wt")
        self.bits = [1 << i for i in range(self.n.bit_length() - 1)]

    def swap(self, value, dc, dw):
        pairs = [
            (c * self.m + w, (c ^ dc) * self.m + (w ^ dw))
            for c in range(self.n)
            for w in range(self.m)
        ]
        return lax.ppermute(value, AXES, pairs)

    def core(self, value):
        return self.swap(value, 0, 1)

    def x(self, value):
        return self.swap(value, 0, 2)


    def gather_wt(self, value):
        near = jnp.stack([value, self.x(value)])
        return [near, self.core(near)]

    def trade_wt(self, own, near, far):
        (far,) = yield [(far, 0, 2)]
        (come,) = yield [(jnp.concatenate([near, far[1:]]), 0, 1)]
        return [own, far[:1], come]

    def sum_wt(self, near, far):
        (come,) = yield [(far, 0, 1)]
        (far,) = yield [(add_low(near[1], come[1]), 0, 2)]
        return add_low(add_low(near[0], come[0]), far)

    def rows_wt(self, blocks, size, numbers=(0, 2, 1, 3)):
        return rearrange(
            functools.partial(place_kernel, size),
            [shaped((self.m * size, blocks[0].shape[2]))],
            [self.w ^ r for r in numbers],
            blocks,
        )[0]


    def gather(self, value, bits, split):
        blocks = value[None]
        for bit in bits[:-2]:
            (come,) = yield [(blocks, bit, 0)]
            blocks = jnp.concatenate([blocks, come])
        if split:
            come, first = yield [(blocks, bits[-2], 0), (blocks, bits[-1], 0)]
            (second,) = yield [(come, bits[-1], 0)]
            return [blocks, come, first, second]
        (come,) = yield [(blocks, bits[-2], 0)]
        blocks = jnp.concatenate([blocks, come])
        (come,) = yield [(blocks, bits[-1], 0)]
        return [blocks, come]

    def gathered(self, bits):
        found = [0]
        for bit in bits:
            found = found + [d | bit for d in found]
        return found

    def halving(self, bits):
        found = [0]
        for bit in reversed(bits):
            found = [d | bit for d in found] + found
        return found

    def halve(self, terms, bits):
        for bit in bits:
            half = terms.shape[0] // 2
            (come,) = yield [(terms[:half], bit, 0)]
            terms = add_low(terms[half:], come)
        return terms[0]


    def plane_hops(self, value):
        return [self.x(value), self.swap(value, 2, 0), self.swap(value, 2, 2)]

    def gather_plane(self, value, come):
        parts = [value] + come
        return jnp.concatenate(parts + [self.core(part) for part in parts])

    def sum_plane(self, near, far):
        (come,) = yield [(far, 0, 1)]
        mine = add_low(near(), come)
        size = mine.shape[0] // 4
        parts = [mine[i * size : (i + 1) * size] for i in range(4)]
        come = yield [(parts[3], 2, 2), (parts[2], 2, 0), (parts[1], 0, 2)]
        return sum((part.astype(F32) for part in come), parts[0].astype(F32))


class Traffic:
    AHEAD = 4

    def __init__(self, links, chains):
        self.links, self.chains, self.results = links, chains, {}
        self.come, self.last, self.open = {}, None, []

    def step(self, name):
        chain, come = self.chains[name], self.come.get(name)
        if come is not None:
            self.open = [part for part in self.open if not any(part is other for other in come)]
            come = [after(part, self.last) for part in come]
        try:
            sends = chain.send(come)
        except StopIteration as end:
            self.results[name] = end.value
            self.come.pop(name, None)
            self.chains.pop(name)
            return
        self.come[name] = []
        for value, dc, dw in sends:
            ties = [] if self.last is None else [self.last]
            if dc is not None:
                while len(self.open) > self.AHEAD:
                    ties.append(self.open.pop(0))
            self.last = after(value, *ties)
            if dc is None:
                come = lax.all_to_all(self.last, "ctx", 0, 0, tiled=True)
            else:
                come = self.links.swap(self.last, dc, dw)
                self.open.append(come)
            self.come[name].append(come)

    def now(self, value):
        return after(value, self.last)

    def run(self, turns):
        for name in turns:
            if name in self.chains:
                self.step(name)
        while self.chains:
            for name in list(self.chains):
                self.step(name)


def on_device(
    tokens,
    slots,
    norm_gains,
    norm_shifts,
    qkv_weight,
    qv_bias,
    proj_weight,
    proj_bias,
    up_weight,
    up_bias,
    down_weight,
    down_bias,
    cotangent,
):
    links = Links()
    n, m, c, w = links.n, links.m, links.c, links.w
    _, rows, width = tokens.shape
    heads = Heads(n, width)
    share = width // m
    block = rows // 2
    length = n * rows
    hid = up_weight.shape[1]
    per = hid // (2 * m)
    tile = 256 if length <= UNROLLED else 128
    near = rows * m
    nq = n // 2
    cut = nq // m

    def half_of(c):
        return (c >> 1) & 1

    def place_of(c):
        return ((c >> 2) << 1) | (c & 1)

    half, place_q = half_of(c), place_of(c)
    spread = links.bits[:1] + links.bits[2:]
    order = links.halving(links.bits)

    own = tokens[0]
    small = jnp.concatenate(
        [
            norm_gains.reshape(-1),
            norm_shifts.reshape(-1),
            qv_bias.reshape(-1),
            proj_bias,
            down_bias,
            up_bias,
        ]
    )
    entries = small.shape[0]
    more = -(-(-(-entries // (3 * heads.wide))) // 16) * 16
    small = jnp.pad(small, [(0, more * 3 * heads.wide - entries)]).reshape(more, 3 * heads.wide)
    seen = {0: own}
    for bit in reversed(links.bits[1:]):
        seen.update({d | bit: links.swap(seen[d], bit, 0) for d in list(seen)})
    firsts = [0] + [bit for bit in links.bits[1:]]
    rest = [d for d in seen if d not in firsts]
    seen[1] = links.swap(own, 1, 0)
    for batch in (firsts[1:], rest):
        sent = links.swap(after(jnp.concatenate([seen[d] for d in batch]), seen[1]), 1, 0)
        seen.update({d | 1: sent[i * rows : (i + 1) * rows] for i, d in enumerate(batch)})
    found = links.gather_wt(heads.pick(qkv_weight, small, c))
    wqkv = links.rows_wt(found, share)
    small = jnp.concatenate([part[:, share:].reshape(2, -1)[:, :entries] for part in found])
    word = seen[1][:16, :128]
    for _ in range(5):
        word = links.core(word)
    last = seen[links.n - 1]
    seen = after(jnp.concatenate([seen[d] for d in order]), word)
    wqkv = after(wqkv, word)

    far_bits = links.bits[:1:-1]
    bits = {
        "down": [*far_bits, 2, 1],
        "up": [*far_bits, 2, 1],
        "qkv": [*far_bits, 1, 2],
        "proj": [*far_bits, 2, 1],
        "up sum": [1, *far_bits],
        "down sum": [1, *far_bits],
        "proj sum": [1, 2, *far_bits],
    }
    pieces = rearrange(
        functools.partial(cut_kernel, per),
        [shaped((k, share, per)) for k in (1, 1, 2)],
        [(w ^ r) * 2 + half for r in range(m)],
        [up_weight],
    )
    wproj = links.gather_wt(proj_weight)
    up_far = links.x(after(pieces[2], wproj[0]))
    wdown = lax.dynamic_slice_in_dim(down_weight, half * per, per, 0)
    grad_out = cotangent[0]

    number = jnp.arange(m, dtype=jnp.int32)
    sources = jnp.array([0, 2, 1, 3], jnp.int32) ^ w
    small = dot((number[:, None] == sources[None, :]).astype(BF16), small)
    vectors = small[:, : 6 * share].reshape(m, 3, 2, share).transpose(1, 2, 0, 3)
    gains, shifts, qvb = vectors.reshape(3, 2, width)
    bproj = small[:, 6 * share : 7 * share].reshape(width)
    bdown = small[:, 7 * share : 8 * share].reshape(width)
    bup = small[:, 8 * share :].reshape(m * 2, per)
    bup = lax.dynamic_index_in_dim(bup, w * 2 + half, 0, False)

    a1 = (standardize(seen.astype(F32))[0] * gains[0] + shifts[0]).astype(BF16)
    qvb_here = heads.here(qvb, c)
    bias = jnp.concatenate([qvb_here[0], jnp.zeros((heads.wide,), F32), qvb_here[1]])
    qkv = (dot(a1, wqkv) + bias).astype(BF16)

    table = jnp.arange(slots.shape[0], dtype=jnp.int32)
    wanted = jnp.array(order, jnp.int32)
    wanted = ((wanted[:, None] ^ c) * 2 + jnp.arange(2, dtype=jnp.int32)).reshape(-1)
    place = jnp.sum(jnp.where(wanted[:, None] == table[None, :], slots[None, :], 0), axis=1)

    come = links.plane_hops(after(grad_out, last))
    heads_out, lse = attn_forward(qkv, place, slots, block, tile)

    wproj = links.rows_wt([after(part, heads_out) for part in wproj], share)
    attended = lax.all_to_all(heads_out, "ctx", 0, 0, tiled=True)
    attended = heads.join(after(attended, wproj, up_far))
    grad_out_plane = links.gather_plane(
        after(grad_out, attended), [after(part, attended) for part in come]
    )
    far = after(up_far, attended)
    wup = [pieces[0], far[:1], links.core(jnp.concatenate([pieces[1], far[1:]]))]
    wup = links.rows_wt(wup, share)
    mid = own.astype(F32) + dot(attended, wproj) + bproj
    normed2, scale2 = standardize(mid)
    a2 = (normed2 * gains[1] + shifts[1]).astype(BF16)

    a2_plane = links.gather_plane(a2, links.plane_hops(a2))
    grad_out32 = grad_out.astype(F32)
    middle = length // 2
    step = -(-(-(-per // nq)) // 8) * 8
    part = -(-(-(-share // n)) // 8) * 8
    kept = {}

    def main_chain():
        pre = dot(a2_plane, wup) + bup
        activated, gelu_pull = jax.vjp(gelu, pre)
        hidden = activated.astype(BF16)
        grad_pre = gelu_pull(by_transpose(grad_out_plane, wdown))[0].astype(BF16)
        kept.update(hidden=hidden, grad_pre=grad_pre)
        grad_a2 = yield from links.sum_plane(
            lambda: by_transpose(grad_pre[:near], wup),
            by_transpose(grad_pre[near:], wup).astype(BF16),
        )
        grad_mid = grad_out32 + finish_norm(grad_a2 * gains[1], normed2, scale2)
        grad_proj = grad_mid.astype(BF16)
        kept.update(grad_a2=grad_a2, grad_mid=grad_mid, grad_proj=grad_proj)
        grad_heads = heads.split(by_transpose(grad_proj, wproj).astype(BF16))
        word = after(jnp.zeros((8, 128), F32), grad_heads)
        (grad_heads,) = yield [(grad_heads, None, None)]
        for _ in range(BUMP):
            word = links.core(word)
        grad_heads = after(grad_heads, word)
        grad_qkv = attn_backward(qkv, grad_heads, lse, place, slots, block, tile)
        normed1 = standardize(after(seen, word).astype(F32))[0]
        other, mine = by_transpose(grad_qkv[:middle], wqkv), by_transpose(grad_qkv[middle:], wqkv)
        d_gain1 = jnp.sum(other * normed1[:middle] + mine * normed1[middle:], axis=0)
        kept.update(grad_qkv=grad_qkv, other=other.astype(BF16), mine=mine, d_gain1=d_gain1)

    def down_chain():
        found = by_rows(over_rows(kept["hidden"], grad_out_plane).astype(BF16))
        found = jnp.pad(found, [(0, step * nq - per), (0, 0)])
        found = [
            lax.dynamic_slice_in_dim(found, (place_q ^ place_of(d)) * step, step, 0)
            for d in links.halving(bits["down sum"])
        ]
        found = yield from links.halve(jnp.stack(found), bits["down sum"])
        return (yield from links.gather(found, bits["down"], "down" in SPLIT))

    def up_chain():
        found = by_rows(over_rows(a2_plane, kept["grad_pre"]).astype(BF16))
        pieces = [lax.dynamic_slice_in_dim(found, (w ^ r) * share, share, 0) for r in range(m)]
        found = yield from links.trade_wt(pieces[0][None], pieces[1][None], jnp.stack(pieces[2:]))
        found = jnp.concatenate(found).reshape(m, share, cut, per // cut).transpose(0, 2, 1, 3)
        terms = []
        for d in links.halving(bits["up sum"]):
            b = place_q ^ place_of(d)
            r = w ^ (b // cut)
            r = (r & 1) * 2 + (r >> 1)
            term = lax.dynamic_slice(found, (r, b % cut, 0, 0), (1, 1, share, per // cut))
            terms.append(term[0, 0])
        found = yield from links.halve(jnp.stack(terms), bits["up sum"])
        return (yield from links.gather(found, bits["up"], "up" in SPLIT))

    def output_chain():
        hidden = kept["hidden"]
        near_part = dot(hidden[:near], wdown).astype(BF16)
        far_part = dot(hidden[near:], wdown).astype(BF16)
        return (yield from links.sum_plane(lambda: near_part, far_part))

    def proj_chain():
        found = by_rows(over_rows(attended, kept["grad_proj"]).astype(BF16))
        pieces = [
            lax.dynamic_slice_in_dim(found, (w ^ r) * share, share, 0) for r in (0, 2, 1, 3)
        ]
        found = yield from links.sum_wt(jnp.stack(pieces[:2]), jnp.stack(pieces[2:]))
        found = jnp.pad(found, [(0, n * part - share), (0, 0)])
        found = [
            lax.dynamic_slice_in_dim(found, (c ^ d) * part, part, 0)
            for d in links.halving(bits["proj sum"])
        ]
        found = yield from links.halve(jnp.stack(found), bits["proj sum"])
        return (yield from links.gather(found, bits["proj"], "proj" in SPLIT))

    def input_chain():
        (come,) = yield [(kept["other"], 1, 0)]
        terms = add_low(kept["mine"], come).reshape(n // 2, rows, width)
        return (yield from links.halve(terms, links.bits[1:]))

    def qkv_chain():
        grad_a2, grad_proj, grad_qkv = (kept[name] for name in ("grad_a2", "grad_proj", "grad_qkv"))
        sums = jnp.sum(grad_qkv.astype(F32), axis=0)
        d_shift1 = dot(sums[None], wqkv.astype(F32).T)[0]
        sums = heads.back(sums.reshape(3, heads.wide), c)
        d_up_bias = lax.dynamic_update_slice(
            jnp.zeros((m * 2, per), F32),
            jnp.sum(kept["grad_pre"].astype(F32), axis=0)[None],
            (w * 2 + half, 0),
        ).reshape(m, hid // m)
        vectors = [
            kept["d_gain1"],
            jnp.sum(grad_a2 * normed2, axis=0),
            d_shift1,
            jnp.sum(grad_a2, axis=0),
            sums[0],
            sums[2],
            jnp.sum(grad_proj.astype(F32), axis=0),
            jnp.sum(grad_out32, axis=0),
        ]
        vectors = jnp.concatenate([v.reshape(m, share) for v in vectors] + [d_up_bias], axis=1)
        vectors = jnp.pad(vectors, [(0, 0), (0, more * 3 * heads.wide - entries)])
        vectors = vectors.astype(BF16).reshape(m * more, 3 * heads.wide)
        found = by_rows(over_rows(a1, grad_qkv).astype(BF16))
        pieces = [
            jnp.concatenate(
                [
                    lax.dynamic_slice_in_dim(found, (w ^ r) * share, share, 0),
                    lax.dynamic_slice_in_dim(vectors, (w ^ r) * more, more, 0),
                ]
            )
            for r in (0, 2, 1, 3)
        ]
        found = yield from links.sum_wt(jnp.stack(pieces[:2]), jnp.stack(pieces[2:]))
        return (yield from links.gather(found, bits["qkv"], "qkv" in SPLIT))

    chains = {
        "m": main_chain(),
        "d": down_chain(),
        "u": up_chain(),
        "g": input_chain(),
        "q": qkv_chain(),
        "p": proj_chain(),
        "o": output_chain(),
    }
    traffic = Traffic(links, chains)
    traffic.run(TURNS)
    d_down, d_up, d_qkv, d_proj = (traffic.results[name] for name in "duqp")
    output, grad_a1 = traffic.results["o"], traffic.results["g"].astype(F32)
    grad_mid = kept["grad_mid"]

    output = mid + output + bdown
    own1, scale1 = standardize(own.astype(F32))
    d_tokens = grad_mid + finish_norm(grad_a1 * gains[0], own1, scale1)

    def owners(name):
        return [c ^ d for d in links.gathered(bits[name])]

    plan = [
        (
            b,
            (0, 0),
            (min(step, per - place_of(b) * step), width),
            (half_of(b) * per + place_of(b) * step, 0),
        )
        for b in range(n)
        if place_of(b) * step < per
    ]
    d_down_weight = lay(d_down, owners("down"), plan, (2 * per, width))
    size = per // cut
    plan = [
        (
            b,
            (0, 0),
            (share, size),
            (
                0,
                (place_of(b) // cut) * 2 * per + half_of(b) * per + (place_of(b) % cut) * size,
            ),
        )
        for b in range(n)
    ]
    d_up_weight = lay(d_up, owners("up"), plan, (share, hid))
    plan = [
        (b, (0, 0), (min(part, share - b * part), width), (b * part, 0))
        for b in range(n)
        if b * part < share
    ]
    d_proj_weight = lay(d_proj, owners("proj"), plan, (share, width))
    plan = [
        (
            p % n,
            (0, (t * heads.slots + p // n) * 128),
            (share, min(128, width - p * 128)),
            (0, t * width + p * 128),
        )
        for t in range(3)
        for p in range(-(-width // 128))
    ]
    d_qkv_weight = lay(d_qkv, owners("qkv"), plan, (share, 3 * width))
    vectors = sum(jnp.sum(part[:, share:].astype(F32), axis=0) for part in d_qkv)
    vectors = vectors.reshape(-1)[:entries]
    eight = vectors[: 8 * share].reshape(8, share)

    return (
        output.astype(BF16)[None],
        d_tokens.astype(BF16)[None],
        eight[0:2],
        eight[2:4],
        d_qkv_weight,
        eight[4:6],
        d_proj_weight,
        eight[6],
        d_up_weight,
        vectors[8 * share :],
        d_down_weight,
        eight[7],
    )


def solution(mesh):
    rows, whole = P("wt", "ctx", None), P(None, "wt")
    weight, vector = P("wt", None), P("wt")
    return jax.shard_map(
        on_device,
        mesh=mesh,
        in_specs=(
            rows,
            P(),
            whole,
            whole,
            weight,
            whole,
            weight,
            vector,
            weight,
            vector,
            weight,
            vector,
            rows,
        ),
        out_specs=(
            rows,
            rows,
            whole,
            whole,
            weight,
            whole,
            weight,
            vector,
            weight,
            vector,
            weight,
            vector,
        ),
        check_vma=False,
    )
```

```python
import functools
import math

import jax
import jax.numpy as jnp
from jax import lax
from jax.experimental import pallas as pl
from jax.experimental.layout import Layout, with_layout_constraint
from jax.experimental.pallas import tpu as pltpu
from jax.sharding import PartitionSpec as P

AXES = ("ctx", "wt")
F32 = jnp.float32
BF16 = jnp.bfloat16


def standardize(values):
    centred = values - jnp.mean(values, axis=-1, keepdims=True)
    scale = lax.rsqrt(jnp.mean(centred * centred, axis=-1, keepdims=True) + 1e-05)
    return (centred * scale, scale)


def finish_norm(scaled, normed, scale):
    inner = (
        scaled
        - jnp.mean(scaled, axis=-1, keepdims=True)
        - normed * jnp.mean(scaled * normed, axis=-1, keepdims=True)
    )
    return scale * inner


def gelu(values):
    return (
        0.5
        * values
        * (1.0 + jnp.tanh(0.7978845608028654 * (values + 0.044715 * values * values * values)))
    )


def dot(left, right):
    return jnp.dot(left, right, preferred_element_type=F32)


def over_rows(left, right):
    return lax.dot_general(left, right, (((0,), (0,)), ((), ())), preferred_element_type=F32)


def by_transpose(left, right):
    return lax.dot_general(left, right, (((1,), (1,)), ((), ())), preferred_element_type=F32)


def add_low(left, right):
    return (left.astype(F32) + right.astype(F32)).astype(BF16)


UNROLLED = 1024
BUMP = 1
SPLIT = ("down", "up", "qkv")
TURNS = "mdmudmpudupmgduqpugqdqpuopqpopuqpg"


def for_tiles(one, length, tile, key_axis):
    if length <= UNROLLED:
        shape = (tile, tile)
        key = lax.broadcasted_iota(jnp.int32, shape, key_axis)
        query = lax.broadcasted_iota(jnp.int32, shape, 1 - key_axis)
        for turn in range(length // tile):
            one(turn, turn * tile, pl.ds(turn * tile, tile), key <= query)
        return

    def turn_of(turn, carry):
        shape = (tile, length) if key_axis else (length, tile)
        key = lax.broadcasted_iota(jnp.int32, shape, key_axis)
        query = lax.broadcasted_iota(jnp.int32, shape, 1 - key_axis)
        one(turn, 0, pl.ds(0, length), key <= query + turn * tile)
        return carry

    lax.fori_loop(0, length // tile, turn_of, 0)


def attn_forward_kernel(tile, block, place_ref, slots_ref, qkv_ref, out_ref, lse_ref, qs, ks, vs, os):
    length, wide = os.shape

    for i in range(length // block):
        here = pl.ds(pl.multiple_of(place_ref[i] * block, block), block)
        there = slice(i * block, (i + 1) * block)
        qs[here, :] = qkv_ref[there, 0:wide] * 0.125
        ks[here, :] = qkv_ref[there, wide : 2 * wide]
        vs[here, :] = qkv_ref[there, 2 * wide : 3 * wide]
    lane = lax.broadcasted_iota(jnp.int32, (tile, 128), 1)

    def one(turn, before, near, allowed):
        mine = pl.ds(turn * tile, tile)
        stats = jnp.zeros((tile, 128), F32)
        for pair in range(wide // 128):
            cols = slice(pair * 128, (pair + 1) * 128)
            q = qs[mine, cols]
            halves = []
            for half in range(2):
                keep = (lane >= 64) if half else (lane < 64)
                qh = jnp.where(keep, q, jnp.zeros_like(q))
                edge = by_transpose(qh, ks[near, cols])
                edge = jnp.where(allowed, edge, -1e30)
                most = jnp.max(edge, axis=1, keepdims=True)
                if before:
                    past = by_transpose(qh, ks[0:before, cols])
                    most = jnp.maximum(most, jnp.max(past, axis=1, keepdims=True))
                edge = jnp.exp(edge - most)
                total = jnp.sum(edge, axis=1, keepdims=True)
                acc = dot(edge.astype(BF16), vs[near, cols])
                if before:
                    past = jnp.exp(past - most)
                    total = total + jnp.sum(past, axis=1, keepdims=True)
                    acc = acc + dot(past.astype(BF16), vs[0:before, cols])
                halves.append(acc / total)
                stats = jnp.where(lane == 2 * pair + half, most + jnp.log(total), stats)
            os[mine, cols] = jnp.where(lane < 64, halves[0], halves[1]).astype(BF16)
        lse_ref[mine, :] = stats

    for_tiles(one, length, tile, 1)

    for i in range(length // block):
        here = pl.ds(pl.multiple_of(slots_ref[i] * block, block), block)
        out_ref[i // 2, (i % 2) * block : (i % 2 + 1) * block, :] = os[here, :]


def attn_backward_kernel(
    tile, block, place_ref, slots_ref, qkv_ref, lse_ref, grad_ref, out_ref, qs, ks, vs, gs, dq, dk, dv
):
    length, wide = gs.shape
    for i in range(length // block):
        here = pl.ds(pl.multiple_of(place_ref[i] * block, block), block)
        there = slice(i * block, (i + 1) * block)
        qs[here, :] = qkv_ref[there, 0:wide] * 0.125
        ks[here, :] = qkv_ref[there, wide : 2 * wide]
        vs[here, :] = qkv_ref[there, 2 * wide : 3 * wide]
        far = pl.ds(pl.multiple_of(slots_ref[i] * block, block), block)
        gs[far, :] = grad_ref[i // 2, (i % 2) * block : (i % 2 + 1) * block, :]
    lane = lax.broadcasted_iota(jnp.int32, (tile, 128), 1)
    alone = length <= UNROLLED
    if not alone:
        dk[...] = jnp.zeros_like(dk)
        dv[...] = jnp.zeros_like(dv)

    def one(turn, before, near, allowed):
        mine = pl.ds(turn * tile, tile)
        lse = lse_ref[mine, :].T
        for pair in range(wide // 128):
            cols = slice(pair * 128, (pair + 1) * 128)
            q, g = qs[mine, cols], gs[mine, cols]
            halves = []
            for half in range(2):
                keep = (lane >= 64) if half else (lane < 64)
                qh = jnp.where(keep, q, jnp.zeros_like(q))
                gh = jnp.where(keep, g, jnp.zeros_like(g))
                row = lse[2 * pair + half : 2 * pair + half + 1, :]
                edge_p = by_transpose(ks[near, cols], qh)
                edge_p = jnp.where(allowed, jnp.exp(edge_p - row), 0.0)
                edge_t = edge_p * by_transpose(vs[near, cols], gh)
                delta = jnp.sum(edge_t, axis=0, keepdims=True)
                if before:
                    past_p = jnp.exp(by_transpose(ks[0:before, cols], qh) - row)
                    past_t = past_p * by_transpose(vs[0:before, cols], gh)
                    delta = delta + jnp.sum(past_t, axis=0, keepdims=True)
                edge_s = (edge_t - edge_p * delta).astype(BF16)
                own_v = dot(edge_p.astype(BF16), gh)
                own_k = dot(edge_s, qh)
                if half or not alone:
                    dv[near, cols] += own_v
                    dk[near, cols] += own_k
                else:
                    dv[near, cols] = own_v
                    dk[near, cols] = own_k
                acc = over_rows(edge_s, ks[near, cols])
                if before:
                    past_s = (past_t - past_p * delta).astype(BF16)
                    dv[0:before, cols] += dot(past_p.astype(BF16), gh)
                    dk[0:before, cols] += dot(past_s, qh)
                    acc = acc + over_rows(past_s, ks[0:before, cols])
                halves.append(acc)
            dq[mine, cols] = (jnp.where(lane < 64, halves[0], halves[1]) * 0.125).astype(BF16)

    for_tiles(one, length, tile, 0)

    for i in range(length // block):
        here = pl.ds(pl.multiple_of(place_ref[i] * block, block), block)
        there = slice(i * block, (i + 1) * block)
        out_ref[there, 0:wide] = dq[here, :]
        out_ref[there, wide : 2 * wide] = dk[here, :].astype(BF16)
        out_ref[there, 2 * wide : 3 * wide] = dv[here, :].astype(BF16)


SMEM = pl.BlockSpec(memory_space=pltpu.SMEM)
VMEM = pl.BlockSpec(memory_space=pltpu.VMEM)
LIMIT = 48 * 1024 * 1024


def attn_forward(qkv, place, slots, block, tile):
    length, wide = qkv.shape[0], qkv.shape[1] // 3
    return pl.pallas_call(
        functools.partial(attn_forward_kernel, tile, block),
        out_shape=(
            jax.ShapeDtypeStruct((length // (2 * block), 2 * block, wide), BF16),
            jax.ShapeDtypeStruct((length, 128), F32),
        ),
        in_specs=[SMEM, SMEM, VMEM],
        out_specs=(VMEM, VMEM),
        scratch_shapes=[pltpu.VMEM((length, wide), BF16)] * 4,
        compiler_params=pltpu.CompilerParams(vmem_limit_bytes=LIMIT),
        cost_estimate=pl.CostEstimate(
            flops=4 * length * length * wide,
            bytes_accessed=length * wide * 10,
            transcendentals=length * length * wide // 128,
        ),
    )(place, slots, qkv)


def attn_backward(qkv, grads, lse, place, slots, block, tile):
    length, wide = qkv.shape[0], qkv.shape[1] // 3
    return pl.pallas_call(
        functools.partial(attn_backward_kernel, tile, block),
        out_shape=jax.ShapeDtypeStruct((length, 3 * wide), BF16),
        in_specs=[SMEM, SMEM, VMEM, VMEM, VMEM],
        out_specs=VMEM,
        scratch_shapes=[pltpu.VMEM((length, wide), BF16)] * 5
        + [pltpu.VMEM((length, wide), F32)] * 2,
        compiler_params=pltpu.CompilerParams(vmem_limit_bytes=LIMIT),
        cost_estimate=pl.CostEstimate(
            flops=10 * length * length * wide,
            bytes_accessed=length * wide * 16,
            transcendentals=length * length * wide // 128,
        ),
    )(place, slots, qkv, lse, grads)


def rearrange(kernel, outs, numbers, arrays, scratch=()):
    size = sum(math.prod(o.shape) * o.dtype.itemsize for o in (*outs, *arrays))
    return pl.pallas_call(
        kernel,
        out_shape=tuple(jax.ShapeDtypeStruct(o.shape, o.dtype) for o in outs),
        in_specs=[SMEM] + [VMEM] * len(arrays),
        out_specs=(VMEM,) * len(outs),
        scratch_shapes=list(scratch),
        compiler_params=pltpu.CompilerParams(vmem_limit_bytes=LIMIT),
        cost_estimate=pl.CostEstimate(flops=0, bytes_accessed=size, transcendentals=0),
    )(jnp.stack(numbers).astype(jnp.int32), *arrays)


def shaped(shape, dtype=BF16):
    return jax.ShapeDtypeStruct(shape, dtype)


class Heads:
    def __init__(self, n, width):
        self.n, self.width = n, width
        self.full, self.rest = width // 128, width % 128
        self.slots = -(-(self.full + (self.rest > 0)) // n)
        self.wide = 128 * self.slots

    def pick_kernel(self, numbers, from_ref, more_ref, out_ref):
        rows = from_ref.shape[0]
        out_ref[rows:, :] = more_ref[...]
        out_ref = out_ref.at[:rows]
        for t in range(3):
            base = t * self.width
            first, off = base // 128, base % 128
            for j in range(self.slots):
                to = slice((t * self.slots + j) * 128, (t * self.slots + j + 1) * 128)
                p = j * self.n + numbers[0]

                @pl.when(p < self.full)
                def _():
                    start = pl.multiple_of((first + p) * 128, 128)
                    if off:
                        out_ref[:, to] = from_ref[:, pl.ds(start, 256)][:, off : off + 128]
                    else:
                        out_ref[:, to] = from_ref[:, pl.ds(start, 128)]

                @pl.when(p >= self.full)
                def _():
                    out_ref[:, to] = jnp.zeros((rows, 128), out_ref.dtype)

                if self.rest:
                    at = base + self.full * 128

                    @pl.when(p == self.full)
                    def _():
                        out_ref[:, to.start : to.start + self.rest] = from_ref[
                            :, at : at + self.rest
                        ]

    def pick(self, weight, more, c):
        out = shaped((weight.shape[0] + more.shape[0], 3 * self.wide))
        return rearrange(self.pick_kernel, [out], [c], [weight, more])[0]

    def join_kernel(self, from_ref, out_ref):
        for p in range(self.full + (self.rest > 0)):
            size = min(128, self.width - p * 128)
            j, owner = divmod(p, self.n)
            out_ref[:, p * 128 : p * 128 + size] = from_ref[owner, :, j * 128 : j * 128 + size]

    def split_kernel(self, from_ref, out_ref):
        for p in range(self.n * self.slots):
            size = max(0, min(128, self.width - p * 128))
            j, owner = divmod(p, self.n)
            if size:
                out_ref[owner, :, j * 128 : j * 128 + size] = from_ref[:, p * 128 : p * 128 + size]
            if size < 128:
                out_ref[owner, :, j * 128 + size : (j + 1) * 128] = jnp.zeros(
                    (out_ref.shape[1], 128 - size), out_ref.dtype
                )

    def turned(self, kernel, value, shape):
        return pl.pallas_call(
            kernel,
            out_shape=shaped(shape),
            in_specs=[VMEM],
            out_specs=VMEM,
            cost_estimate=pl.CostEstimate(
                flops=0, bytes_accessed=4 * math.prod(shape), transcendentals=0
            ),
        )(value)

    def join(self, blocks):
        return self.turned(self.join_kernel, blocks, (blocks.shape[1], self.width))

    def split(self, value):
        return self.turned(self.split_kernel, value, (self.n, value.shape[0], self.wide))

    def here(self, values, c):
        lead = values.shape[:-1]
        values = jnp.pad(values, [(0, 0)] * len(lead) + [(0, self.n * self.wide - self.width)])
        values = values.reshape(lead + (self.slots, self.n, 128))
        return lax.dynamic_index_in_dim(values, c, len(lead) + 1, False).reshape(
            lead + (self.wide,)
        )

    def back(self, values, c):
        lead = values.shape[:-1]
        zeros = jnp.zeros(lead + (self.slots, self.n, 128), values.dtype)
        values = values.reshape(lead + (self.slots, 1, 128))
        values = lax.dynamic_update_slice(zeros, values, (0,) * (len(lead) + 1) + (c, 0))
        return values.reshape(lead + (self.n * self.wide,))[..., : self.width]


def cut_kernel(per, numbers, from_ref, *outs):
    r = 0
    for out_ref in outs:
        for k in range(out_ref.shape[0]):
            for part in range(from_ref.shape[1] // per):

                @pl.when(numbers[r] == part)
                def _():
                    out_ref[k] = from_ref[:, part * per : (part + 1) * per]

            r += 1


def place_kernel(size, numbers, *refs):
    out_ref, r = refs[-1], 0
    for ref in refs[:-1]:
        for k in range(ref.shape[0]):
            to = pl.ds(pl.multiple_of(numbers[r] * size, 16), size)
            out_ref[to, :] = ref[k, :size, :]
            r += 1


def lay_kernel(plan, more, numbers, *refs):
    refs, held = refs[:-1], refs[-1]
    if more:
        refs, sum_ref = refs[:-1], refs[-1]
        last = slice(held.shape[1] - more, held.shape[1])
        sum_ref[...] = sum(
            ref[k, last, :].astype(F32) for ref in refs[:-1] for k in range(ref.shape[0])
        )
    blocks, out_ref = refs[:-1], refs[-1]
    r = 0
    for ref in blocks:
        for k in range(ref.shape[0]):
            held[numbers[r]] = ref[k]
            r += 1
    for b, from_rows, from_cols, rows, cols in plan:
        out_ref[rows, cols] = held[b, from_rows, from_cols].astype(F32)


def lay(blocks, numbers, plan, shape, more=0):
    steps = [
        (b, slice(r, r + h), slice(q, q + v), slice(tr, tr + h), slice(tq, tq + v))
        for b, (r, q), (h, v), (tr, tq) in plan
    ]
    scratch = [pltpu.VMEM((len(numbers),) + blocks[0].shape[1:], BF16)]
    kernel = functools.partial(lay_kernel, steps, more)
    outs = [shaped(shape, F32)] + ([shaped((more, blocks[0].shape[2]), F32)] if more else [])
    found = rearrange(kernel, outs, numbers, blocks, scratch)
    return found if more else found[0]


def by_rows(value):
    return with_layout_constraint(value, Layout(major_to_minor=tuple(range(value.ndim))))


def after(value, *others):
    return lax.optimization_barrier((value,) + others)[0]


def together(*values):
    return lax.optimization_barrier(values)


class Links:
    def __init__(self):
        self.n, self.m = lax.axis_size("ctx"), lax.axis_size("wt")
        self.c, self.w = lax.axis_index("ctx"), lax.axis_index("wt")
        self.bits = [1 << i for i in range(self.n.bit_length() - 1)]

    def swap(self, value, dc, dw):
        pairs = [
            (c * self.m + w, (c ^ dc) * self.m + (w ^ dw))
            for c in range(self.n)
            for w in range(self.m)
        ]
        return lax.ppermute(value, AXES, pairs)

    def core(self, value):
        return self.swap(value, 0, 1)

    def x(self, value):
        return self.swap(value, 0, 2)


    def gather_wt(self, value):
        near = jnp.stack([value, self.x(value)])
        return [near, self.core(near)]

    def trade_wt(self, own, near, far):
        (far,) = yield [(far, 0, 2)]
        (come,) = yield [(jnp.concatenate([near, far[1:]]), 0, 1)]
        return [own, far[:1], come]

    def sum_wt(self, near, far):
        (come,) = yield [(far, 0, 1)]
        (far,) = yield [(add_low(near[1], come[1]), 0, 2)]
        return add_low(add_low(near[0], come[0]), far)

    def rows_wt(self, blocks, size, numbers=(0, 2, 1, 3)):
        return rearrange(
            functools.partial(place_kernel, size),
            [shaped((self.m * size, blocks[0].shape[2]))],
            [self.w ^ r for r in numbers],
            blocks,
        )[0]


    def gather(self, value, bits, split):
        blocks = value[None]
        for bit in bits[:-2]:
            (come,) = yield [(blocks, bit, 0)]
            blocks = jnp.concatenate([blocks, come])
        if split:
            come, first = yield [(blocks, bits[-2], 0), (blocks, bits[-1], 0)]
            (second,) = yield [(come, bits[-1], 0)]
            return [blocks, come, first, second]
        (come,) = yield [(blocks, bits[-2], 0)]
        blocks = jnp.concatenate([blocks, come])
        (come,) = yield [(blocks, bits[-1], 0)]
        return [blocks, come]

    def gathered(self, bits):
        found = [0]
        for bit in bits:
            found = found + [d | bit for d in found]
        return found

    def halving(self, bits):
        found = [0]
        for bit in reversed(bits):
            found = [d | bit for d in found] + found
        return found

    def halve(self, terms, bits):
        for bit in bits:
            half = terms.shape[0] // 2
            (come,) = yield [(terms[:half], bit, 0)]
            terms = add_low(terms[half:], come)
        return terms[0]


    def plane_hops(self, value):
        return [self.x(value), self.swap(value, 2, 0), self.swap(value, 2, 2)]

    def gather_plane(self, value, come):
        parts = [value] + come
        return jnp.concatenate(parts + [self.core(part) for part in parts])

    def sum_plane(self, near, far):
        (come,) = yield [(far, 0, 1)]
        mine = add_low(near(), come)
        size = mine.shape[0] // 4
        parts = [mine[i * size : (i + 1) * size] for i in range(4)]
        come = yield [(parts[3], 2, 2), (parts[2], 2, 0), (parts[1], 0, 2)]
        return sum((part.astype(F32) for part in come), parts[0].astype(F32))


class Traffic:
    AHEAD = 4

    def __init__(self, links, chains):
        self.links, self.chains, self.results = links, chains, {}
        self.come, self.last, self.open = {}, None, []

    def step(self, name):
        chain, come = self.chains[name], self.come.get(name)
        if come is not None:
            self.open = [part for part in self.open if not any(part is other for other in come)]
            come = [after(part, self.last) for part in come]
        try:
            sends = chain.send(come)
        except StopIteration as end:
            self.results[name] = end.value
            self.come.pop(name, None)
            self.chains.pop(name)
            return
        self.come[name] = []
        for value, dc, dw in sends:
            ties = [] if self.last is None else [self.last]
            if dc is not None:
                while len(self.open) > self.AHEAD:
                    ties.append(self.open.pop(0))
            self.last = after(value, *ties)
            if dc is None:
                come = lax.all_to_all(self.last, "ctx", 0, 0, tiled=True)
            else:
                come = self.links.swap(self.last, dc, dw)
                self.open.append(come)
            self.come[name].append(come)

    def now(self, value):
        return after(value, self.last)

    def run(self, turns):
        for name in turns:
            if name in self.chains:
                self.step(name)
        while self.chains:
            for name in list(self.chains):
                self.step(name)


def on_device(
    tokens,
    slots,
    norm_gains,
    norm_shifts,
    qkv_weight,
    qv_bias,
    proj_weight,
    proj_bias,
    up_weight,
    up_bias,
    down_weight,
    down_bias,
    cotangent,
):
    links = Links()
    n, m, c, w = links.n, links.m, links.c, links.w
    _, rows, width = tokens.shape
    heads = Heads(n, width)
    share = width // m
    block = rows // 2
    length = n * rows
    hid = up_weight.shape[1]
    per = hid // (2 * m)
    tile = 256 if length <= UNROLLED else 128
    near = rows * m
    nq = n // 2
    cut = nq // m

    def half_of(c):
        return (c >> 1) & 1

    def place_of(c):
        return ((c >> 2) << 1) | (c & 1)

    half, place_q = half_of(c), place_of(c)
    spread = links.bits[:1] + links.bits[2:]
    order = links.halving(links.bits)

    own = tokens[0]
    small = jnp.concatenate(
        [
            norm_gains.reshape(-1),
            norm_shifts.reshape(-1),
            qv_bias.reshape(-1),
            proj_bias,
            down_bias,
            up_bias,
        ]
    )
    entries = small.shape[0]
    take = share if 3 * heads.wide >= share else share // 2
    more = -(-max(-(-entries // (3 * heads.wide)), entries // take) // 16) * 16
    small = jnp.pad(small, [(0, more * 3 * heads.wide - entries)]).reshape(more, 3 * heads.wide)
    seen = {0: own}
    for bit in reversed(links.bits[1:]):
        seen.update({d | bit: links.swap(seen[d], bit, 0) for d in list(seen)})
    firsts = [0] + [bit for bit in links.bits[1:]]
    rest = [d for d in seen if d not in firsts]
    seen[1] = links.swap(own, 1, 0)
    for batch in (firsts[1:], rest):
        sent = links.swap(after(jnp.concatenate([seen[d] for d in batch]), seen[1]), 1, 0)
        seen.update({d | 1: sent[i * rows : (i + 1) * rows] for i, d in enumerate(batch)})
    found = links.gather_wt(heads.pick(qkv_weight, small, c))
    wqkv = links.rows_wt(found, share)
    small = jnp.concatenate([part[:, share:].reshape(2, -1)[:, :entries] for part in found])
    word = seen[1][:16, :128]
    for _ in range(5):
        word = links.core(word)
    last = seen[links.n - 1]
    seen = after(jnp.concatenate([seen[d] for d in order]), word)
    wqkv = after(wqkv, word)

    far_bits = links.bits[:1:-1]
    bits = {
        "down": [*far_bits, 2, 1],
        "up": [*far_bits, 2, 1],
        "qkv": [*far_bits, 1, 2],
        "proj": [*far_bits, 2, 1],
        "up sum": [1, *far_bits],
        "down sum": [1, *far_bits],
        "proj sum": [1, 2, *far_bits],
    }
    pieces = rearrange(
        functools.partial(cut_kernel, per),
        [shaped((k, share, per)) for k in (1, 1, 2)],
        [(w ^ r) * 2 + half for r in range(m)],
        [up_weight],
    )
    wproj = links.gather_wt(proj_weight)
    up_far = links.x(after(pieces[2], wproj[0]))
    wdown = lax.dynamic_slice_in_dim(down_weight, half * per, per, 0)
    grad_out = cotangent[0]

    number = jnp.arange(m, dtype=jnp.int32)
    sources = jnp.array([0, 2, 1, 3], jnp.int32) ^ w
    small = dot((number[:, None] == sources[None, :]).astype(BF16), small)
    vectors = small[:, : 6 * share].reshape(m, 3, 2, share).transpose(1, 2, 0, 3)
    gains, shifts, qvb = vectors.reshape(3, 2, width)
    bproj = small[:, 6 * share : 7 * share].reshape(width)
    bdown = small[:, 7 * share : 8 * share].reshape(width)
    bup = small[:, 8 * share :].reshape(m * 2, per)
    bup = lax.dynamic_index_in_dim(bup, w * 2 + half, 0, False)

    a1 = (standardize(seen.astype(F32))[0] * gains[0] + shifts[0]).astype(BF16)
    qvb_here = heads.here(qvb, c)
    bias = jnp.concatenate([qvb_here[0], jnp.zeros((heads.wide,), F32), qvb_here[1]])
    qkv = (dot(a1, wqkv) + bias).astype(BF16)

    table = jnp.arange(slots.shape[0], dtype=jnp.int32)
    wanted = jnp.array(order, jnp.int32)
    wanted = ((wanted[:, None] ^ c) * 2 + jnp.arange(2, dtype=jnp.int32)).reshape(-1)
    place = jnp.sum(jnp.where(wanted[:, None] == table[None, :], slots[None, :], 0), axis=1)

    come = links.plane_hops(after(grad_out, last))
    heads_out, lse = attn_forward(qkv, place, slots, block, tile)

    wproj = links.rows_wt([after(part, heads_out) for part in wproj], share)
    attended = lax.all_to_all(heads_out, "ctx", 0, 0, tiled=True)
    attended = heads.join(after(attended, wproj, up_far))
    grad_out_plane = links.gather_plane(
        after(grad_out, attended), [after(part, attended) for part in come]
    )
    far = after(up_far, attended)
    wup = [pieces[0], far[:1], links.core(jnp.concatenate([pieces[1], far[1:]]))]
    wup = links.rows_wt(wup, share)
    mid = own.astype(F32) + dot(attended, wproj) + bproj
    normed2, scale2 = standardize(mid)
    a2 = (normed2 * gains[1] + shifts[1]).astype(BF16)

    a2_plane = links.gather_plane(a2, links.plane_hops(a2))
    grad_out32 = grad_out.astype(F32)
    middle = length // 2
    step = -(-(-(-per // nq)) // 8) * 8
    part = -(-(-(-share // n)) // 8) * 8
    kept = {}

    def main_chain():
        pre = dot(a2_plane, wup) + bup
        activated, gelu_pull = jax.vjp(gelu, pre)
        hidden = activated.astype(BF16)
        grad_pre = gelu_pull(by_transpose(grad_out_plane, wdown))[0].astype(BF16)
        kept.update(hidden=hidden, grad_pre=grad_pre)
        grad_a2 = yield from links.sum_plane(
            lambda: by_transpose(grad_pre[:near], wup),
            by_transpose(grad_pre[near:], wup).astype(BF16),
        )
        grad_mid = grad_out32 + finish_norm(grad_a2 * gains[1], normed2, scale2)
        grad_proj = grad_mid.astype(BF16)
        kept.update(grad_a2=grad_a2, grad_mid=grad_mid, grad_proj=grad_proj)
        grad_heads = heads.split(by_transpose(grad_proj, wproj).astype(BF16))
        word = after(jnp.zeros((8, 128), F32), grad_heads)
        (grad_heads,) = yield [(grad_heads, None, None)]
        for _ in range(BUMP):
            word = links.core(word)
        grad_heads = after(grad_heads, word)
        grad_qkv = attn_backward(qkv, grad_heads, lse, place, slots, block, tile)
        normed1 = standardize(after(seen, word).astype(F32))[0]
        other, mine = by_transpose(grad_qkv[:middle], wqkv), by_transpose(grad_qkv[middle:], wqkv)
        d_gain1 = jnp.sum(other * normed1[:middle] + mine * normed1[middle:], axis=0)
        kept.update(grad_qkv=grad_qkv, other=other.astype(BF16), mine=mine, d_gain1=d_gain1)

    def down_chain():
        found = by_rows(over_rows(kept["hidden"], grad_out_plane).astype(BF16))
        found = jnp.pad(found, [(0, step * nq - per), (0, 0)])
        found = [
            lax.dynamic_slice_in_dim(found, (place_q ^ place_of(d)) * step, step, 0)
            for d in links.halving(bits["down sum"])
        ]
        found = yield from links.halve(jnp.stack(found), bits["down sum"])
        return (yield from links.gather(found, bits["down"], "down" in SPLIT))

    def up_chain():
        found = by_rows(over_rows(a2_plane, kept["grad_pre"]).astype(BF16))
        pieces = [lax.dynamic_slice_in_dim(found, (w ^ r) * share, share, 0) for r in range(m)]
        found = yield from links.trade_wt(pieces[0][None], pieces[1][None], jnp.stack(pieces[2:]))
        found = jnp.concatenate(found).reshape(m, share, cut, per // cut).transpose(0, 2, 1, 3)
        terms = []
        for d in links.halving(bits["up sum"]):
            b = place_q ^ place_of(d)
            r = w ^ (b // cut)
            r = (r & 1) * 2 + (r >> 1)
            term = lax.dynamic_slice(found, (r, b % cut, 0, 0), (1, 1, share, per // cut))
            terms.append(term[0, 0])
        found = yield from links.halve(jnp.stack(terms), bits["up sum"])
        return (yield from links.gather(found, bits["up"], "up" in SPLIT))

    def output_chain():
        hidden = traffic.now(kept["hidden"])
        near_part = dot(hidden[:near], wdown).astype(BF16)
        far_part = dot(hidden[near:], wdown).astype(BF16)
        return (yield from links.sum_plane(lambda: near_part, far_part))

    def proj_chain():
        found = by_rows(over_rows(attended, kept["grad_proj"]).astype(BF16))
        pieces = [
            lax.dynamic_slice_in_dim(found, (w ^ r) * share, share, 0) for r in (0, 2, 1, 3)
        ]
        found = yield from links.sum_wt(jnp.stack(pieces[:2]), jnp.stack(pieces[2:]))
        found = jnp.pad(found, [(0, n * part - share), (0, 0)])
        found = [
            lax.dynamic_slice_in_dim(found, (c ^ d) * part, part, 0)
            for d in links.halving(bits["proj sum"])
        ]
        found = yield from links.halve(jnp.stack(found), bits["proj sum"])
        return (yield from links.gather(found, bits["proj"], "proj" in SPLIT))

    def input_chain():
        (come,) = yield [(kept["other"], 1, 0)]
        terms = add_low(kept["mine"], come).reshape(n // 2, rows, width)
        return (yield from links.halve(terms, links.bits[1:]))

    def qkv_chain():
        grad_a2, grad_proj, grad_qkv = (kept[name] for name in ("grad_a2", "grad_proj", "grad_qkv"))
        sums = jnp.sum(grad_qkv.astype(F32), axis=0)
        d_shift1 = dot(sums[None], wqkv.astype(F32).T)[0]
        sums = heads.back(sums.reshape(3, heads.wide), c)
        d_up_bias = lax.dynamic_update_slice(
            jnp.zeros((m * 2, per), F32),
            jnp.sum(kept["grad_pre"].astype(F32), axis=0)[None],
            (w * 2 + half, 0),
        ).reshape(m, hid // m // share, share)
        vectors = [
            kept["d_gain1"],
            jnp.sum(grad_a2 * normed2, axis=0),
            d_shift1,
            jnp.sum(grad_a2, axis=0),
            sums[0],
            sums[2],
            jnp.sum(grad_proj.astype(F32), axis=0),
            jnp.sum(grad_out32, axis=0),
        ]
        vectors = jnp.stack([v.reshape(m, share) for v in vectors], axis=1)
        vectors = jnp.concatenate([vectors, d_up_bias], axis=1).astype(BF16)
        vectors = vectors.reshape(m, entries // take, take)
        beside = (more - entries // take, 3 * heads.wide - take)
        vectors = jnp.pad(vectors, [(0, 0), (0, beside[0]), (0, beside[1])])
        vectors = vectors.reshape(m * more, 3 * heads.wide)
        found = by_rows(over_rows(a1, grad_qkv).astype(BF16))
        pieces = [
            jnp.concatenate(
                [
                    lax.dynamic_slice_in_dim(found, (w ^ r) * share, share, 0),
                    lax.dynamic_slice_in_dim(vectors, (w ^ r) * more, more, 0),
                ]
            )
            for r in (0, 2, 1, 3)
        ]
        found = yield from links.sum_wt(jnp.stack(pieces[:2]), jnp.stack(pieces[2:]))
        return (yield from links.gather(found, bits["qkv"], "qkv" in SPLIT))

    chains = {
        "m": main_chain(),
        "d": down_chain(),
        "u": up_chain(),
        "g": input_chain(),
        "q": qkv_chain(),
        "p": proj_chain(),
        "o": output_chain(),
    }
    traffic = Traffic(links, chains)
    traffic.run(TURNS)
    d_down, d_up, d_qkv, d_proj = (traffic.results[name] for name in "duqp")
    output, grad_a1 = traffic.results["o"], traffic.results["g"].astype(F32)
    grad_mid = kept["grad_mid"]

    output = mid + output + bdown
    own1, scale1 = standardize(own.astype(F32))
    d_tokens = grad_mid + finish_norm(grad_a1 * gains[0], own1, scale1)

    def owners(name):
        return [c ^ d for d in links.gathered(bits[name])]

    plan = [
        (
            b,
            (0, 0),
            (min(step, per - place_of(b) * step), width),
            (half_of(b) * per + place_of(b) * step, 0),
        )
        for b in range(n)
        if place_of(b) * step < per
    ]
    d_down_weight = lay(d_down, owners("down"), plan, (2 * per, width))
    size = per // cut
    plan = [
        (
            b,
            (0, 0),
            (share, size),
            (
                0,
                (place_of(b) // cut) * 2 * per + half_of(b) * per + (place_of(b) % cut) * size,
            ),
        )
        for b in range(n)
    ]
    d_up_weight = lay(d_up, owners("up"), plan, (share, hid))
    plan = [
        (b, (0, 0), (min(part, share - b * part), width), (b * part, 0))
        for b in range(n)
        if b * part < share
    ]
    d_proj_weight = lay(d_proj, owners("proj"), plan, (share, width))
    plan = [
        (
            p % n,
            (0, (t * heads.slots + p // n) * 128),
            (share, min(128, width - p * 128)),
            (0, t * width + p * 128),
        )
        for t in range(3)
        for p in range(-(-width // 128))
    ]
    d_qkv_weight, vectors = lay(d_qkv, owners("qkv"), plan, (share, 3 * width), more)
    vectors = vectors[: entries // take, :take].reshape(entries // share, share)
    return (
        output.astype(BF16)[None],
        d_tokens.astype(BF16)[None],
        vectors[0:2],
        vectors[2:4],
        d_qkv_weight,
        vectors[4:6],
        d_proj_weight,
        vectors[6],
        d_up_weight,
        vectors[8 : 8 + hid // width].reshape(-1),
        d_down_weight,
        vectors[7],
    )


def solution(mesh):
    rows, whole = P("wt", "ctx", None), P(None, "wt")
    weight, vector = P("wt", None), P("wt")
    return jax.shard_map(
        on_device,
        mesh=mesh,
        in_specs=(
            rows,
            P(),
            whole,
            whole,
            weight,
            whole,
            weight,
            vector,
            weight,
            vector,
            weight,
            vector,
            rows,
        ),
        out_specs=(
            rows,
            rows,
            whole,
            whole,
            weight,
            whole,
            weight,
            vector,
            weight,
            vector,
            weight,
            vector,
        ),
        check_vma=False,
    )
```

```python
import functools
import math

import jax
import jax.numpy as jnp
from jax import lax
from jax.experimental import pallas as pl
from jax.experimental.layout import Layout, with_layout_constraint
from jax.experimental.pallas import tpu as pltpu
from jax.sharding import PartitionSpec as P

AXES = ("ctx", "wt")
F32 = jnp.float32
BF16 = jnp.bfloat16


def standardize(values):
    centred = values - jnp.mean(values, axis=-1, keepdims=True)
    scale = lax.rsqrt(jnp.mean(centred * centred, axis=-1, keepdims=True) + 1e-05)
    return (centred * scale, scale)


def finish_norm(scaled, normed, scale):
    inner = (
        scaled
        - jnp.mean(scaled, axis=-1, keepdims=True)
        - normed * jnp.mean(scaled * normed, axis=-1, keepdims=True)
    )
    return scale * inner


def gelu(values):
    return (
        0.5
        * values
        * (1.0 + jnp.tanh(0.7978845608028654 * (values + 0.044715 * values * values * values)))
    )


def dot(left, right):
    return jnp.dot(left, right, preferred_element_type=F32)


def over_rows(left, right):
    return lax.dot_general(left, right, (((0,), (0,)), ((), ())), preferred_element_type=F32)


def by_transpose(left, right):
    return lax.dot_general(left, right, (((1,), (1,)), ((), ())), preferred_element_type=F32)


def add_low(left, right):
    return (left.astype(F32) + right.astype(F32)).astype(BF16)


UNROLLED = 1024
BUMP = 1
SPLIT = ("down", "up", "qkv")
TURNS = "mdmudmpudupmgduqpugqdqpuopqpgupoqp"


def for_tiles(one, length, tile, key_axis):
    if length <= UNROLLED:
        shape = (tile, tile)
        key = lax.broadcasted_iota(jnp.int32, shape, key_axis)
        query = lax.broadcasted_iota(jnp.int32, shape, 1 - key_axis)
        for turn in range(length // tile):
            one(turn, turn * tile, pl.ds(turn * tile, tile), key <= query)
        return

    def turn_of(turn, carry):
        shape = (tile, length) if key_axis else (length, tile)
        key = lax.broadcasted_iota(jnp.int32, shape, key_axis)
        query = lax.broadcasted_iota(jnp.int32, shape, 1 - key_axis)
        one(turn, 0, pl.ds(0, length), key <= query + turn * tile)
        return carry

    lax.fori_loop(0, length // tile, turn_of, 0)


def attn_forward_kernel(tile, block, place_ref, slots_ref, qkv_ref, out_ref, lse_ref, qs, ks, vs, os):
    length, wide = os.shape

    for i in range(length // block):
        here = pl.ds(pl.multiple_of(place_ref[i] * block, block), block)
        there = slice(i * block, (i + 1) * block)
        qs[here, :] = qkv_ref[there, 0:wide] * 0.125
        ks[here, :] = qkv_ref[there, wide : 2 * wide]
        vs[here, :] = qkv_ref[there, 2 * wide : 3 * wide]
    lane = lax.broadcasted_iota(jnp.int32, (tile, 128), 1)

    def one(turn, before, near, allowed):
        mine = pl.ds(turn * tile, tile)
        stats = jnp.zeros((tile, 128), F32)
        for pair in range(wide // 128):
            cols = slice(pair * 128, (pair + 1) * 128)
            q = qs[mine, cols]
            halves = []
            for half in range(2):
                keep = (lane >= 64) if half else (lane < 64)
                qh = jnp.where(keep, q, jnp.zeros_like(q))
                edge = by_transpose(qh, ks[near, cols])
                edge = jnp.where(allowed, edge, -1e30)
                most = jnp.max(edge, axis=1, keepdims=True)
                if before:
                    past = by_transpose(qh, ks[0:before, cols])
                    most = jnp.maximum(most, jnp.max(past, axis=1, keepdims=True))
                edge = jnp.exp(edge - most)
                total = jnp.sum(edge, axis=1, keepdims=True)
                acc = dot(edge.astype(BF16), vs[near, cols])
                if before:
                    past = jnp.exp(past - most)
                    total = total + jnp.sum(past, axis=1, keepdims=True)
                    acc = acc + dot(past.astype(BF16), vs[0:before, cols])
                halves.append(acc / total)
                stats = jnp.where(lane == 2 * pair + half, most + jnp.log(total), stats)
            os[mine, cols] = jnp.where(lane < 64, halves[0], halves[1]).astype(BF16)
        lse_ref[mine, :] = stats

    for_tiles(one, length, tile, 1)

    for i in range(length // block):
        here = pl.ds(pl.multiple_of(slots_ref[i] * block, block), block)
        out_ref[i // 2, (i % 2) * block : (i % 2 + 1) * block, :] = os[here, :]


def attn_backward_kernel(
    tile, block, place_ref, slots_ref, qkv_ref, lse_ref, grad_ref, out_ref, qs, ks, vs, gs, dq, dk, dv
):
    length, wide = gs.shape
    for i in range(length // block):
        here = pl.ds(pl.multiple_of(place_ref[i] * block, block), block)
        there = slice(i * block, (i + 1) * block)
        qs[here, :] = qkv_ref[there, 0:wide] * 0.125
        ks[here, :] = qkv_ref[there, wide : 2 * wide]
        vs[here, :] = qkv_ref[there, 2 * wide : 3 * wide]
        far = pl.ds(pl.multiple_of(slots_ref[i] * block, block), block)
        gs[far, :] = grad_ref[i // 2, (i % 2) * block : (i % 2 + 1) * block, :]
    lane = lax.broadcasted_iota(jnp.int32, (tile, 128), 1)
    alone = length <= UNROLLED
    if not alone:
        dk[...] = jnp.zeros_like(dk)
        dv[...] = jnp.zeros_like(dv)

    def one(turn, before, near, allowed):
        mine = pl.ds(turn * tile, tile)
        lse = lse_ref[mine, :].T
        for pair in range(wide // 128):
            cols = slice(pair * 128, (pair + 1) * 128)
            q, g = qs[mine, cols], gs[mine, cols]
            halves = []
            for half in range(2):
                keep = (lane >= 64) if half else (lane < 64)
                qh = jnp.where(keep, q, jnp.zeros_like(q))
                gh = jnp.where(keep, g, jnp.zeros_like(g))
                row = lse[2 * pair + half : 2 * pair + half + 1, :]
                edge_p = by_transpose(ks[near, cols], qh)
                edge_p = jnp.where(allowed, jnp.exp(edge_p - row), 0.0)
                edge_t = edge_p * by_transpose(vs[near, cols], gh)
                delta = jnp.sum(edge_t, axis=0, keepdims=True)
                if before:
                    past_p = jnp.exp(by_transpose(ks[0:before, cols], qh) - row)
                    past_t = past_p * by_transpose(vs[0:before, cols], gh)
                    delta = delta + jnp.sum(past_t, axis=0, keepdims=True)
                edge_s = (edge_t - edge_p * delta).astype(BF16)
                own_v = dot(edge_p.astype(BF16), gh)
                own_k = dot(edge_s, qh)
                if half or not alone:
                    dv[near, cols] += own_v
                    dk[near, cols] += own_k
                else:
                    dv[near, cols] = own_v
                    dk[near, cols] = own_k
                acc = over_rows(edge_s, ks[near, cols])
                if before:
                    past_s = (past_t - past_p * delta).astype(BF16)
                    dv[0:before, cols] += dot(past_p.astype(BF16), gh)
                    dk[0:before, cols] += dot(past_s, qh)
                    acc = acc + over_rows(past_s, ks[0:before, cols])
                halves.append(acc)
            dq[mine, cols] = (jnp.where(lane < 64, halves[0], halves[1]) * 0.125).astype(BF16)

    for_tiles(one, length, tile, 0)

    for i in range(length // block):
        here = pl.ds(pl.multiple_of(place_ref[i] * block, block), block)
        there = slice(i * block, (i + 1) * block)
        out_ref[there, 0:wide] = dq[here, :]
        out_ref[there, wide : 2 * wide] = dk[here, :].astype(BF16)
        out_ref[there, 2 * wide : 3 * wide] = dv[here, :].astype(BF16)


SMEM = pl.BlockSpec(memory_space=pltpu.SMEM)
VMEM = pl.BlockSpec(memory_space=pltpu.VMEM)
LIMIT = 48 * 1024 * 1024


def attn_forward(qkv, place, slots, block, tile):
    length, wide = qkv.shape[0], qkv.shape[1] // 3
    return pl.pallas_call(
        functools.partial(attn_forward_kernel, tile, block),
        out_shape=(
            jax.ShapeDtypeStruct((length // (2 * block), 2 * block, wide), BF16),
            jax.ShapeDtypeStruct((length, 128), F32),
        ),
        in_specs=[SMEM, SMEM, VMEM],
        out_specs=(VMEM, VMEM),
        scratch_shapes=[pltpu.VMEM((length, wide), BF16)] * 4,
        compiler_params=pltpu.CompilerParams(vmem_limit_bytes=LIMIT),
        cost_estimate=pl.CostEstimate(
            flops=4 * length * length * wide,
            bytes_accessed=length * wide * 10,
            transcendentals=length * length * wide // 128,
        ),
    )(place, slots, qkv)


def attn_backward(qkv, grads, lse, place, slots, block, tile):
    length, wide = qkv.shape[0], qkv.shape[1] // 3
    return pl.pallas_call(
        functools.partial(attn_backward_kernel, tile, block),
        out_shape=jax.ShapeDtypeStruct((length, 3 * wide), BF16),
        in_specs=[SMEM, SMEM, VMEM, VMEM, VMEM],
        out_specs=VMEM,
        scratch_shapes=[pltpu.VMEM((length, wide), BF16)] * 5
        + [pltpu.VMEM((length, wide), F32)] * 2,
        compiler_params=pltpu.CompilerParams(vmem_limit_bytes=LIMIT),
        cost_estimate=pl.CostEstimate(
            flops=10 * length * length * wide,
            bytes_accessed=length * wide * 16,
            transcendentals=length * length * wide // 128,
        ),
    )(place, slots, qkv, lse, grads)


def rearrange(kernel, outs, numbers, arrays, scratch=()):
    size = sum(math.prod(o.shape) * o.dtype.itemsize for o in (*outs, *arrays))
    return pl.pallas_call(
        kernel,
        out_shape=tuple(jax.ShapeDtypeStruct(o.shape, o.dtype) for o in outs),
        in_specs=[SMEM] + [VMEM] * len(arrays),
        out_specs=(VMEM,) * len(outs),
        scratch_shapes=list(scratch),
        compiler_params=pltpu.CompilerParams(vmem_limit_bytes=LIMIT),
        cost_estimate=pl.CostEstimate(flops=0, bytes_accessed=size, transcendentals=0),
    )(jnp.stack(numbers).astype(jnp.int32), *arrays)


def shaped(shape, dtype=BF16):
    return jax.ShapeDtypeStruct(shape, dtype)


class Heads:
    def __init__(self, n, width):
        self.n, self.width = n, width
        self.full, self.rest = width // 128, width % 128
        self.slots = -(-(self.full + (self.rest > 0)) // n)
        self.wide = 128 * self.slots

    def pick_kernel(self, numbers, from_ref, more_ref, out_ref):
        rows = from_ref.shape[0]
        out_ref[rows:, :] = more_ref[...]
        out_ref = out_ref.at[:rows]
        for t in range(3):
            base = t * self.width
            first, off = base // 128, base % 128
            for j in range(self.slots):
                to = slice((t * self.slots + j) * 128, (t * self.slots + j + 1) * 128)
                p = j * self.n + numbers[0]

                @pl.when(p < self.full)
                def _():
                    start = pl.multiple_of((first + p) * 128, 128)
                    if off:
                        out_ref[:, to] = from_ref[:, pl.ds(start, 256)][:, off : off + 128]
                    else:
                        out_ref[:, to] = from_ref[:, pl.ds(start, 128)]

                @pl.when(p >= self.full)
                def _():
                    out_ref[:, to] = jnp.zeros((rows, 128), out_ref.dtype)

                if self.rest:
                    at = base + self.full * 128

                    @pl.when(p == self.full)
                    def _():
                        out_ref[:, to.start : to.start + self.rest] = from_ref[
                            :, at : at + self.rest
                        ]

    def pick(self, weight, more, c):
        out = shaped((weight.shape[0] + more.shape[0], 3 * self.wide))
        return rearrange(self.pick_kernel, [out], [c], [weight, more])[0]

    def join_kernel(self, from_ref, out_ref):
        for p in range(self.full + (self.rest > 0)):
            size = min(128, self.width - p * 128)
            j, owner = divmod(p, self.n)
            out_ref[:, p * 128 : p * 128 + size] = from_ref[owner, :, j * 128 : j * 128 + size]

    def split_kernel(self, from_ref, out_ref):
        for p in range(self.n * self.slots):
            size = max(0, min(128, self.width - p * 128))
            j, owner = divmod(p, self.n)
            if size:
                out_ref[owner, :, j * 128 : j * 128 + size] = from_ref[:, p * 128 : p * 128 + size]
            if size < 128:
                out_ref[owner, :, j * 128 + size : (j + 1) * 128] = jnp.zeros(
                    (out_ref.shape[1], 128 - size), out_ref.dtype
                )

    def turned(self, kernel, value, shape):
        return pl.pallas_call(
            kernel,
            out_shape=shaped(shape),
            in_specs=[VMEM],
            out_specs=VMEM,
            cost_estimate=pl.CostEstimate(
                flops=0, bytes_accessed=4 * math.prod(shape), transcendentals=0
            ),
        )(value)

    def join(self, blocks):
        return self.turned(self.join_kernel, blocks, (blocks.shape[1], self.width))

    def split(self, value):
        return self.turned(self.split_kernel, value, (self.n, value.shape[0], self.wide))

    def here(self, values, c):
        lead = values.shape[:-1]
        values = jnp.pad(values, [(0, 0)] * len(lead) + [(0, self.n * self.wide - self.width)])
        values = values.reshape(lead + (self.slots, self.n, 128))
        return lax.dynamic_index_in_dim(values, c, len(lead) + 1, False).reshape(
            lead + (self.wide,)
        )

    def back(self, values, c):
        lead = values.shape[:-1]
        zeros = jnp.zeros(lead + (self.slots, self.n, 128), values.dtype)
        values = values.reshape(lead + (self.slots, 1, 128))
        values = lax.dynamic_update_slice(zeros, values, (0,) * (len(lead) + 1) + (c, 0))
        return values.reshape(lead + (self.n * self.wide,))[..., : self.width]


def cut_kernel(per, numbers, from_ref, *outs):
    r = 0
    for out_ref in outs:
        for k in range(out_ref.shape[0]):
            for part in range(from_ref.shape[1] // per):

                @pl.when(numbers[r] == part)
                def _():
                    out_ref[k] = from_ref[:, part * per : (part + 1) * per]

            r += 1


def place_kernel(size, numbers, *refs):
    out_ref, r = refs[-1], 0
    for ref in refs[:-1]:
        for k in range(ref.shape[0]):
            to = pl.ds(pl.multiple_of(numbers[r] * size, 16), size)
            out_ref[to, :] = ref[k, :size, :]
            r += 1


def lay_kernel(plan, more, numbers, *refs):
    refs, held = refs[:-1], refs[-1]
    if more:
        refs, sum_ref = refs[:-1], refs[-1]
        last = slice(held.shape[1] - more, held.shape[1])
        sum_ref[...] = sum(
            ref[k, last, :].astype(F32) for ref in refs[:-1] for k in range(ref.shape[0])
        )
    blocks, out_ref = refs[:-1], refs[-1]
    r = 0
    for ref in blocks:
        for k in range(ref.shape[0]):
            held[numbers[r]] = ref[k]
            r += 1
    for b, from_rows, from_cols, rows, cols in plan:
        out_ref[rows, cols] = held[b, from_rows, from_cols].astype(F32)


def lay(blocks, numbers, plan, shape, more=0):
    steps = [
        (b, slice(r, r + h), slice(q, q + v), slice(tr, tr + h), slice(tq, tq + v))
        for b, (r, q), (h, v), (tr, tq) in plan
    ]
    scratch = [pltpu.VMEM((len(numbers),) + blocks[0].shape[1:], BF16)]
    kernel = functools.partial(lay_kernel, steps, more)
    outs = [shaped(shape, F32)] + ([shaped((more, blocks[0].shape[2]), F32)] if more else [])
    found = rearrange(kernel, outs, numbers, blocks, scratch)
    return found if more else found[0]


def by_rows(value):
    return with_layout_constraint(value, Layout(major_to_minor=tuple(range(value.ndim))))


def after(value, *others):
    return lax.optimization_barrier((value,) + others)[0]


def together(*values):
    return lax.optimization_barrier(values)


class Links:
    def __init__(self):
        self.n, self.m = lax.axis_size("ctx"), lax.axis_size("wt")
        self.c, self.w = lax.axis_index("ctx"), lax.axis_index("wt")
        self.bits = [1 << i for i in range(self.n.bit_length() - 1)]

    def swap(self, value, dc, dw):
        pairs = [
            (c * self.m + w, (c ^ dc) * self.m + (w ^ dw))
            for c in range(self.n)
            for w in range(self.m)
        ]
        return lax.ppermute(value, AXES, pairs)

    def core(self, value):
        return self.swap(value, 0, 1)

    def x(self, value):
        return self.swap(value, 0, 2)


    def gather_wt(self, value):
        near = jnp.stack([value, self.x(value)])
        return [near, self.core(near)]

    def trade_wt(self, own, near, far):
        (far,) = yield [(far, 0, 2)]
        (come,) = yield [(jnp.concatenate([near, far[1:]]), 0, 1)]
        return [own, far[:1], come]

    def sum_wt(self, near, far):
        (come,) = yield [(far, 0, 1)]
        (far,) = yield [(add_low(near[1], come[1]), 0, 2)]
        return add_low(add_low(near[0], come[0]), far)

    def rows_wt(self, blocks, size, numbers=(0, 2, 1, 3)):
        return rearrange(
            functools.partial(place_kernel, size),
            [shaped((self.m * size, blocks[0].shape[2]))],
            [self.w ^ r for r in numbers],
            blocks,
        )[0]


    def gather(self, value, bits, split):
        blocks = value[None]
        for bit in bits[:-2]:
            (come,) = yield [(blocks, bit, 0)]
            blocks = jnp.concatenate([blocks, come])
        if split:
            come, first = yield [(blocks, bits[-2], 0), (blocks, bits[-1], 0)]
            (second,) = yield [(come, bits[-1], 0)]
            return [blocks, come, first, second]
        (come,) = yield [(blocks, bits[-2], 0)]
        blocks = jnp.concatenate([blocks, come])
        (come,) = yield [(blocks, bits[-1], 0)]
        return [blocks, come]

    def gathered(self, bits):
        found = [0]
        for bit in bits:
            found = found + [d | bit for d in found]
        return found

    def halving(self, bits):
        found = [0]
        for bit in reversed(bits):
            found = [d | bit for d in found] + found
        return found

    def halve(self, terms, bits):
        for bit in bits:
            half = terms.shape[0] // 2
            (come,) = yield [(terms[:half], bit, 0)]
            terms = add_low(terms[half:], come)
        return terms[0]


    def plane_hops(self, value):
        return [self.x(value), self.swap(value, 2, 0), self.swap(value, 2, 2)]

    def gather_plane(self, value, come):
        parts = [value] + come
        return jnp.concatenate(parts + [self.core(part) for part in parts])

    def sum_plane(self, near, far):
        (come,) = yield [(far, 0, 1)]
        mine = add_low(near(), come)
        size = mine.shape[0] // 4
        parts = [mine[i * size : (i + 1) * size] for i in range(4)]
        come = yield [(parts[3], 2, 2), (parts[2], 2, 0), (parts[1], 0, 2)]
        return sum((part.astype(F32) for part in come), parts[0].astype(F32))


class Traffic:
    AHEAD = 4

    def __init__(self, links, chains):
        self.links, self.chains, self.results = links, chains, {}
        self.come, self.last, self.open = {}, None, []

    def step(self, name):
        chain, come = self.chains[name], self.come.get(name)
        if come is not None:
            self.open = [part for part in self.open if not any(part is other for other in come)]
            come = [after(part, self.last) for part in come]
        try:
            sends = chain.send(come)
        except StopIteration as end:
            self.results[name] = end.value
            self.come.pop(name, None)
            self.chains.pop(name)
            return
        self.come[name] = []
        for value, dc, dw in sends:
            ties = [] if self.last is None else [self.last]
            if dc is not None:
                while len(self.open) > self.AHEAD:
                    ties.append(self.open.pop(0))
            self.last = after(value, *ties)
            if dc is None:
                come = lax.all_to_all(self.last, "ctx", 0, 0, tiled=True)
            else:
                come = self.links.swap(self.last, dc, dw)
                self.open.append(come)
            self.come[name].append(come)

    def now(self, value):
        return after(value, self.last)

    def run(self, turns):
        for name in turns:
            if name in self.chains:
                self.step(name)
        while self.chains:
            for name in list(self.chains):
                self.step(name)


def on_device(
    tokens,
    slots,
    norm_gains,
    norm_shifts,
    qkv_weight,
    qv_bias,
    proj_weight,
    proj_bias,
    up_weight,
    up_bias,
    down_weight,
    down_bias,
    cotangent,
):
    links = Links()
    n, m, c, w = links.n, links.m, links.c, links.w
    _, rows, width = tokens.shape
    heads = Heads(n, width)
    share = width // m
    block = rows // 2
    length = n * rows
    hid = up_weight.shape[1]
    per = hid // (2 * m)
    tile = 256 if length <= UNROLLED else 128
    near = rows * m
    nq = n // 2
    cut = nq // m

    def half_of(c):
        return (c >> 1) & 1

    def place_of(c):
        return ((c >> 2) << 1) | (c & 1)

    half, place_q = half_of(c), place_of(c)
    spread = links.bits[:1] + links.bits[2:]
    order = links.halving(links.bits)

    own = tokens[0]
    small = jnp.concatenate(
        [
            norm_gains.reshape(-1),
            norm_shifts.reshape(-1),
            qv_bias.reshape(-1),
            proj_bias,
            down_bias,
            up_bias,
        ]
    )
    entries = small.shape[0]
    take = share if 3 * heads.wide >= share else share // 2
    more = -(-max(-(-entries // (3 * heads.wide)), entries // take) // 16) * 16
    small = jnp.pad(small, [(0, more * 3 * heads.wide - entries)]).reshape(more, 3 * heads.wide)
    seen = {0: own}
    for bit in reversed(links.bits[1:]):
        seen.update({d | bit: links.swap(seen[d], bit, 0) for d in list(seen)})
    firsts = [0] + [bit for bit in links.bits[1:]]
    rest = [d for d in seen if d not in firsts]
    seen[1] = links.swap(own, 1, 0)
    for batch in (firsts[1:], rest):
        sent = links.swap(after(jnp.concatenate([seen[d] for d in batch]), seen[1]), 1, 0)
        seen.update({d | 1: sent[i * rows : (i + 1) * rows] for i, d in enumerate(batch)})
    found = links.gather_wt(heads.pick(qkv_weight, small, c))
    wqkv = links.rows_wt(found, share)
    small = jnp.concatenate([part[:, share:].reshape(2, -1)[:, :entries] for part in found])
    word = seen[1][:16, :128]
    for _ in range(5):
        word = links.core(word)
    last = seen[links.n - 1]
    seen = after(jnp.concatenate([seen[d] for d in order]), word)
    wqkv = after(wqkv, word)

    far_bits = links.bits[:1:-1]
    bits = {
        "down": [*far_bits, 2, 1],
        "up": [*far_bits, 2, 1],
        "qkv": [*far_bits, 1, 2],
        "proj": [*far_bits, 2, 1],
        "up sum": [1, *far_bits],
        "down sum": [1, *far_bits],
        "proj sum": [1, 2, *far_bits],
    }
    pieces = rearrange(
        functools.partial(cut_kernel, per),
        [shaped((k, share, per)) for k in (1, 1, 2)],
        [(w ^ r) * 2 + half for r in range(m)],
        [up_weight],
    )
    wproj = links.gather_wt(proj_weight)
    up_far = links.x(after(pieces[2], wproj[0]))
    wdown = lax.dynamic_slice_in_dim(down_weight, half * per, per, 0)
    grad_out = cotangent[0]

    number = jnp.arange(m, dtype=jnp.int32)
    sources = jnp.array([0, 2, 1, 3], jnp.int32) ^ w
    small = dot((number[:, None] == sources[None, :]).astype(BF16), small)
    vectors = small[:, : 6 * share].reshape(m, 3, 2, share).transpose(1, 2, 0, 3)
    gains, shifts, qvb = vectors.reshape(3, 2, width)
    bproj = small[:, 6 * share : 7 * share].reshape(width)
    bdown = small[:, 7 * share : 8 * share].reshape(width)
    bup = small[:, 8 * share :].reshape(m * 2, per)
    bup = lax.dynamic_index_in_dim(bup, w * 2 + half, 0, False)

    a1 = (standardize(seen.astype(F32))[0] * gains[0] + shifts[0]).astype(BF16)
    qvb_here = heads.here(qvb, c)
    bias = jnp.concatenate([qvb_here[0], jnp.zeros((heads.wide,), F32), qvb_here[1]])
    qkv = (dot(a1, wqkv) + bias).astype(BF16)

    table = jnp.arange(slots.shape[0], dtype=jnp.int32)
    wanted = jnp.array(order, jnp.int32)
    wanted = ((wanted[:, None] ^ c) * 2 + jnp.arange(2, dtype=jnp.int32)).reshape(-1)
    place = jnp.sum(jnp.where(wanted[:, None] == table[None, :], slots[None, :], 0), axis=1)

    come = links.plane_hops(after(grad_out, last))
    heads_out, lse = attn_forward(qkv, place, slots, block, tile)

    wproj = links.rows_wt([after(part, heads_out) for part in wproj], share)
    attended = lax.all_to_all(heads_out, "ctx", 0, 0, tiled=True)
    attended = heads.join(after(attended, wproj, up_far))
    grad_out_plane = links.gather_plane(
        after(grad_out, attended), [after(part, attended) for part in come]
    )
    far = after(up_far, attended)
    wup = [pieces[0], far[:1], links.core(jnp.concatenate([pieces[1], far[1:]]))]
    wup = links.rows_wt(wup, share)
    mid = own.astype(F32) + dot(attended, wproj) + bproj
    normed2, scale2 = standardize(mid)
    a2 = (normed2 * gains[1] + shifts[1]).astype(BF16)

    a2_plane = links.gather_plane(a2, links.plane_hops(a2))
    grad_out32 = grad_out.astype(F32)
    middle = length // 2
    step = -(-(-(-per // nq)) // 8) * 8
    part = -(-(-(-share // n)) // 8) * 8
    kept = {}

    def main_chain():
        pre = dot(a2_plane, wup) + bup
        activated, gelu_pull = jax.vjp(gelu, pre)
        hidden = activated.astype(BF16)
        grad_pre = gelu_pull(by_transpose(grad_out_plane, wdown))[0].astype(BF16)
        kept.update(hidden=hidden, grad_pre=grad_pre)
        grad_a2 = yield from links.sum_plane(
            lambda: by_transpose(grad_pre[:near], wup),
            by_transpose(grad_pre[near:], wup).astype(BF16),
        )
        grad_mid = grad_out32 + finish_norm(grad_a2 * gains[1], normed2, scale2)
        grad_proj = grad_mid.astype(BF16)
        kept.update(grad_a2=grad_a2, grad_mid=grad_mid, grad_proj=grad_proj)
        grad_heads = heads.split(by_transpose(grad_proj, wproj).astype(BF16))
        word = after(jnp.zeros((8, 128), F32), grad_heads)
        (grad_heads,) = yield [(grad_heads, None, None)]
        for _ in range(BUMP):
            word = links.core(word)
        grad_heads = after(grad_heads, word)
        grad_qkv = attn_backward(qkv, grad_heads, lse, place, slots, block, tile)
        normed1 = standardize(after(seen, word).astype(F32))[0]
        other, mine = by_transpose(grad_qkv[:middle], wqkv), by_transpose(grad_qkv[middle:], wqkv)
        d_gain1 = jnp.sum(other * normed1[:middle] + mine * normed1[middle:], axis=0)
        kept.update(grad_qkv=grad_qkv, other=other.astype(BF16), mine=mine, d_gain1=d_gain1)

    def down_chain():
        found = by_rows(over_rows(kept["hidden"], grad_out_plane).astype(BF16))
        found = jnp.pad(found, [(0, step * nq - per), (0, 0)])
        found = [
            lax.dynamic_slice_in_dim(found, (place_q ^ place_of(d)) * step, step, 0)
            for d in links.halving(bits["down sum"])
        ]
        found = yield from links.halve(jnp.stack(found), bits["down sum"])
        return (yield from links.gather(found, bits["down"], "down" in SPLIT))

    def up_chain():
        found = by_rows(over_rows(a2_plane, kept["grad_pre"]).astype(BF16))
        pieces = [lax.dynamic_slice_in_dim(found, (w ^ r) * share, share, 0) for r in range(m)]
        found = yield from links.trade_wt(pieces[0][None], pieces[1][None], jnp.stack(pieces[2:]))
        found = jnp.concatenate(found).reshape(m, share, cut, per // cut).transpose(0, 2, 1, 3)
        terms = []
        for d in links.halving(bits["up sum"]):
            b = place_q ^ place_of(d)
            r = w ^ (b // cut)
            r = (r & 1) * 2 + (r >> 1)
            term = lax.dynamic_slice(found, (r, b % cut, 0, 0), (1, 1, share, per // cut))
            terms.append(term[0, 0])
        found = yield from links.halve(jnp.stack(terms), bits["up sum"])
        return (yield from links.gather(found, bits["up"], "up" in SPLIT))

    def output_chain():
        hidden = traffic.now(kept["hidden"])
        near_part = dot(hidden[:near], wdown).astype(BF16)
        far_part = dot(hidden[near:], wdown).astype(BF16)
        return (yield from links.sum_plane(lambda: near_part, far_part))

    def proj_chain():
        found = by_rows(over_rows(attended, kept["grad_proj"]).astype(BF16))
        pieces = [
            lax.dynamic_slice_in_dim(found, (w ^ r) * share, share, 0) for r in (0, 2, 1, 3)
        ]
        found = yield from links.sum_wt(jnp.stack(pieces[:2]), jnp.stack(pieces[2:]))
        found = jnp.pad(found, [(0, n * part - share), (0, 0)])
        found = [
            lax.dynamic_slice_in_dim(found, (c ^ d) * part, part, 0)
            for d in links.halving(bits["proj sum"])
        ]
        found = yield from links.halve(jnp.stack(found), bits["proj sum"])
        return (yield from links.gather(found, bits["proj"], "proj" in SPLIT))

    def input_chain():
        (come,) = yield [(kept["other"], 1, 0)]
        terms = add_low(kept["mine"], come).reshape(n // 2, rows, width)
        return (yield from links.halve(terms, links.bits[1:]))

    def qkv_chain():
        grad_a2, grad_proj, grad_qkv = (kept[name] for name in ("grad_a2", "grad_proj", "grad_qkv"))
        sums = jnp.sum(grad_qkv.astype(F32), axis=0)
        d_shift1 = dot(sums[None], wqkv.astype(F32).T)[0]
        sums = heads.back(sums.reshape(3, heads.wide), c)
        d_up_bias = lax.dynamic_update_slice(
            jnp.zeros((m * 2, per), F32),
            jnp.sum(kept["grad_pre"].astype(F32), axis=0)[None],
            (w * 2 + half, 0),
        ).reshape(m, hid // m // share, share)
        vectors = [
            kept["d_gain1"],
            jnp.sum(grad_a2 * normed2, axis=0),
            d_shift1,
            jnp.sum(grad_a2, axis=0),
            sums[0],
            sums[2],
            jnp.sum(grad_proj.astype(F32), axis=0),
            jnp.sum(grad_out32, axis=0),
        ]
        vectors = jnp.stack([v.reshape(m, share) for v in vectors], axis=1)
        vectors = jnp.concatenate([vectors, d_up_bias], axis=1).astype(BF16)
        vectors = vectors.reshape(m, entries // take, take)
        beside = (more - entries // take, 3 * heads.wide - take)
        vectors = jnp.pad(vectors, [(0, 0), (0, beside[0]), (0, beside[1])])
        vectors = vectors.reshape(m * more, 3 * heads.wide)
        found = by_rows(over_rows(a1, grad_qkv).astype(BF16))
        pieces = [
            jnp.concatenate(
                [
                    lax.dynamic_slice_in_dim(found, (w ^ r) * share, share, 0),
                    lax.dynamic_slice_in_dim(vectors, (w ^ r) * more, more, 0),
                ]
            )
            for r in (0, 2, 1, 3)
        ]
        found = yield from links.sum_wt(jnp.stack(pieces[:2]), jnp.stack(pieces[2:]))
        return (yield from links.gather(found, bits["qkv"], "qkv" in SPLIT))

    chains = {
        "m": main_chain(),
        "d": down_chain(),
        "u": up_chain(),
        "g": input_chain(),
        "q": qkv_chain(),
        "p": proj_chain(),
        "o": output_chain(),
    }
    traffic = Traffic(links, chains)
    traffic.run(TURNS)
    d_down, d_up, d_qkv, d_proj = (traffic.results[name] for name in "duqp")
    output, grad_a1 = traffic.results["o"], traffic.results["g"].astype(F32)
    grad_mid = kept["grad_mid"]

    output = mid + output + bdown
    own1, scale1 = standardize(own.astype(F32))
    d_tokens = grad_mid + finish_norm(grad_a1 * gains[0], own1, scale1)

    def owners(name):
        return [c ^ d for d in links.gathered(bits[name])]

    plan = [
        (
            b,
            (0, 0),
            (min(step, per - place_of(b) * step), width),
            (half_of(b) * per + place_of(b) * step, 0),
        )
        for b in range(n)
        if place_of(b) * step < per
    ]
    d_down_weight = lay(d_down, owners("down"), plan, (2 * per, width))
    size = per // cut
    plan = [
        (
            b,
            (0, 0),
            (share, size),
            (
                0,
                (place_of(b) // cut) * 2 * per + half_of(b) * per + (place_of(b) % cut) * size,
            ),
        )
        for b in range(n)
    ]
    d_up_weight = lay(d_up, owners("up"), plan, (share, hid))
    plan = [
        (b, (0, 0), (min(part, share - b * part), width), (b * part, 0))
        for b in range(n)
        if b * part < share
    ]
    d_proj_weight = lay(d_proj, owners("proj"), plan, (share, width))
    plan = [
        (
            p % n,
            (0, (t * heads.slots + p // n) * 128),
            (share, min(128, width - p * 128)),
            (0, t * width + p * 128),
        )
        for t in range(3)
        for p in range(-(-width // 128))
    ]
    d_qkv_weight, vectors = lay(d_qkv, owners("qkv"), plan, (share, 3 * width), more)
    vectors = vectors[: entries // take, :take].reshape(entries // share, share)
    return (
        output.astype(BF16)[None],
        d_tokens.astype(BF16)[None],
        vectors[0:2],
        vectors[2:4],
        d_qkv_weight,
        vectors[4:6],
        d_proj_weight,
        vectors[6],
        d_up_weight,
        vectors[8 : 8 + hid // width].reshape(-1),
        d_down_weight,
        vectors[7],
    )


def solution(mesh):
    rows, whole = P("wt", "ctx", None), P(None, "wt")
    weight, vector = P("wt", None), P("wt")
    return jax.shard_map(
        on_device,
        mesh=mesh,
        in_specs=(
            rows,
            P(),
            whole,
            whole,
            weight,
            whole,
            weight,
            vector,
            weight,
            vector,
            weight,
            vector,
            rows,
        ),
        out_specs=(
            rows,
            rows,
            whole,
            whole,
            weight,
            whole,
            weight,
            vector,
            weight,
            vector,
            weight,
            vector,
        ),
        check_vma=False,
    )
```

```python
import functools
import math

import jax
import jax.numpy as jnp
from jax import lax
from jax.experimental import pallas as pl
from jax.experimental.layout import Layout, with_layout_constraint
from jax.experimental.pallas import tpu as pltpu
from jax.sharding import PartitionSpec as P

AXES = ("ctx", "wt")
F32 = jnp.float32
BF16 = jnp.bfloat16


def standardize(values):
    centred = values - jnp.mean(values, axis=-1, keepdims=True)
    scale = lax.rsqrt(jnp.mean(centred * centred, axis=-1, keepdims=True) + 1e-05)
    return (centred * scale, scale)


def finish_norm(scaled, normed, scale):
    inner = (
        scaled
        - jnp.mean(scaled, axis=-1, keepdims=True)
        - normed * jnp.mean(scaled * normed, axis=-1, keepdims=True)
    )
    return scale * inner


def gelu(values):
    return (
        0.5
        * values
        * (1.0 + jnp.tanh(0.7978845608028654 * (values + 0.044715 * values * values * values)))
    )


def dot(left, right):
    return jnp.dot(left, right, preferred_element_type=F32)


def over_rows(left, right):
    return lax.dot_general(left, right, (((0,), (0,)), ((), ())), preferred_element_type=F32)


def by_transpose(left, right):
    return lax.dot_general(left, right, (((1,), (1,)), ((), ())), preferred_element_type=F32)


def add_low(left, right):
    return (left.astype(F32) + right.astype(F32)).astype(BF16)


UNROLLED = 1024
BUMP = 1
SPLIT = ("down", "up", "qkv")
TURNS = "mdmudmpudupmgduqpugqdqpuopqpgupqop"


def for_tiles(one, length, tile, key_axis):
    if length <= UNROLLED:
        shape = (tile, tile)
        key = lax.broadcasted_iota(jnp.int32, shape, key_axis)
        query = lax.broadcasted_iota(jnp.int32, shape, 1 - key_axis)
        for turn in range(length // tile):
            one(turn, turn * tile, pl.ds(turn * tile, tile), key <= query)
        return

    def turn_of(turn, carry):
        shape = (tile, length) if key_axis else (length, tile)
        key = lax.broadcasted_iota(jnp.int32, shape, key_axis)
        query = lax.broadcasted_iota(jnp.int32, shape, 1 - key_axis)
        one(turn, 0, pl.ds(0, length), key <= query + turn * tile)
        return carry

    lax.fori_loop(0, length // tile, turn_of, 0)


def attn_forward_kernel(tile, block, place_ref, slots_ref, qkv_ref, out_ref, lse_ref, qs, ks, vs, os):
    length, wide = os.shape

    for i in range(length // block):
        here = pl.ds(pl.multiple_of(place_ref[i] * block, block), block)
        there = slice(i * block, (i + 1) * block)
        qs[here, :] = qkv_ref[there, 0:wide] * 0.125
        ks[here, :] = qkv_ref[there, wide : 2 * wide]
        vs[here, :] = qkv_ref[there, 2 * wide : 3 * wide]
    lane = lax.broadcasted_iota(jnp.int32, (tile, 128), 1)

    def one(turn, before, near, allowed):
        mine = pl.ds(turn * tile, tile)
        stats = jnp.zeros((tile, 128), F32)
        for pair in range(wide // 128):
            cols = slice(pair * 128, (pair + 1) * 128)
            q = qs[mine, cols]
            halves = []
            for half in range(2):
                keep = (lane >= 64) if half else (lane < 64)
                qh = jnp.where(keep, q, jnp.zeros_like(q))
                edge = by_transpose(qh, ks[near, cols])
                edge = jnp.where(allowed, edge, -1e30)
                most = jnp.max(edge, axis=1, keepdims=True)
                if before:
                    past = by_transpose(qh, ks[0:before, cols])
                    most = jnp.maximum(most, jnp.max(past, axis=1, keepdims=True))
                edge = jnp.exp(edge - most)
                total = jnp.sum(edge, axis=1, keepdims=True)
                acc = dot(edge.astype(BF16), vs[near, cols])
                if before:
                    past = jnp.exp(past - most)
                    total = total + jnp.sum(past, axis=1, keepdims=True)
                    acc = acc + dot(past.astype(BF16), vs[0:before, cols])
                halves.append(acc / total)
                stats = jnp.where(lane == 2 * pair + half, most + jnp.log(total), stats)
            os[mine, cols] = jnp.where(lane < 64, halves[0], halves[1]).astype(BF16)
        lse_ref[mine, :] = stats

    for_tiles(one, length, tile, 1)

    for i in range(length // block):
        here = pl.ds(pl.multiple_of(slots_ref[i] * block, block), block)
        out_ref[i // 2, (i % 2) * block : (i % 2 + 1) * block, :] = os[here, :]


def attn_backward_kernel(
    tile, block, place_ref, slots_ref, qkv_ref, lse_ref, grad_ref, out_ref, qs, ks, vs, gs, dq, dk, dv
):
    length, wide = gs.shape
    for i in range(length // block):
        here = pl.ds(pl.multiple_of(place_ref[i] * block, block), block)
        there = slice(i * block, (i + 1) * block)
        qs[here, :] = qkv_ref[there, 0:wide] * 0.125
        ks[here, :] = qkv_ref[there, wide : 2 * wide]
        vs[here, :] = qkv_ref[there, 2 * wide : 3 * wide]
        far = pl.ds(pl.multiple_of(slots_ref[i] * block, block), block)
        gs[far, :] = grad_ref[i // 2, (i % 2) * block : (i % 2 + 1) * block, :]
    lane = lax.broadcasted_iota(jnp.int32, (tile, 128), 1)
    alone = length <= UNROLLED
    if not alone:
        dk[...] = jnp.zeros_like(dk)
        dv[...] = jnp.zeros_like(dv)

    def one(turn, before, near, allowed):
        mine = pl.ds(turn * tile, tile)
        lse = lse_ref[mine, :].T
        for pair in range(wide // 128):
            cols = slice(pair * 128, (pair + 1) * 128)
            q, g = qs[mine, cols], gs[mine, cols]
            halves = []
            for half in range(2):
                keep = (lane >= 64) if half else (lane < 64)
                qh = jnp.where(keep, q, jnp.zeros_like(q))
                gh = jnp.where(keep, g, jnp.zeros_like(g))
                row = lse[2 * pair + half : 2 * pair + half + 1, :]
                edge_p = by_transpose(ks[near, cols], qh)
                edge_p = jnp.where(allowed, jnp.exp(edge_p - row), 0.0)
                edge_t = edge_p * by_transpose(vs[near, cols], gh)
                delta = jnp.sum(edge_t, axis=0, keepdims=True)
                if before:
                    past_p = jnp.exp(by_transpose(ks[0:before, cols], qh) - row)
                    past_t = past_p * by_transpose(vs[0:before, cols], gh)
                    delta = delta + jnp.sum(past_t, axis=0, keepdims=True)
                edge_s = (edge_t - edge_p * delta).astype(BF16)
                own_v = dot(edge_p.astype(BF16), gh)
                own_k = dot(edge_s, qh)
                if half or not alone:
                    dv[near, cols] += own_v
                    dk[near, cols] += own_k
                else:
                    dv[near, cols] = own_v
                    dk[near, cols] = own_k
                acc = over_rows(edge_s, ks[near, cols])
                if before:
                    past_s = (past_t - past_p * delta).astype(BF16)
                    dv[0:before, cols] += dot(past_p.astype(BF16), gh)
                    dk[0:before, cols] += dot(past_s, qh)
                    acc = acc + over_rows(past_s, ks[0:before, cols])
                halves.append(acc)
            dq[mine, cols] = (jnp.where(lane < 64, halves[0], halves[1]) * 0.125).astype(BF16)

    for_tiles(one, length, tile, 0)

    for i in range(length // block):
        here = pl.ds(pl.multiple_of(place_ref[i] * block, block), block)
        there = slice(i * block, (i + 1) * block)
        out_ref[there, 0:wide] = dq[here, :]
        out_ref[there, wide : 2 * wide] = dk[here, :].astype(BF16)
        out_ref[there, 2 * wide : 3 * wide] = dv[here, :].astype(BF16)


SMEM = pl.BlockSpec(memory_space=pltpu.SMEM)
VMEM = pl.BlockSpec(memory_space=pltpu.VMEM)
LIMIT = 48 * 1024 * 1024


def attn_forward(qkv, place, slots, block, tile):
    length, wide = qkv.shape[0], qkv.shape[1] // 3
    return pl.pallas_call(
        functools.partial(attn_forward_kernel, tile, block),
        out_shape=(
            jax.ShapeDtypeStruct((length // (2 * block), 2 * block, wide), BF16),
            jax.ShapeDtypeStruct((length, 128), F32),
        ),
        in_specs=[SMEM, SMEM, VMEM],
        out_specs=(VMEM, VMEM),
        scratch_shapes=[pltpu.VMEM((length, wide), BF16)] * 4,
        compiler_params=pltpu.CompilerParams(vmem_limit_bytes=LIMIT),
        cost_estimate=pl.CostEstimate(
            flops=4 * length * length * wide,
            bytes_accessed=length * wide * 10,
            transcendentals=length * length * wide // 128,
        ),
    )(place, slots, qkv)


def attn_backward(qkv, grads, lse, place, slots, block, tile):
    length, wide = qkv.shape[0], qkv.shape[1] // 3
    return pl.pallas_call(
        functools.partial(attn_backward_kernel, tile, block),
        out_shape=jax.ShapeDtypeStruct((length, 3 * wide), BF16),
        in_specs=[SMEM, SMEM, VMEM, VMEM, VMEM],
        out_specs=VMEM,
        scratch_shapes=[pltpu.VMEM((length, wide), BF16)] * 5
        + [pltpu.VMEM((length, wide), F32)] * 2,
        compiler_params=pltpu.CompilerParams(vmem_limit_bytes=LIMIT),
        cost_estimate=pl.CostEstimate(
            flops=10 * length * length * wide,
            bytes_accessed=length * wide * 16,
            transcendentals=length * length * wide // 128,
        ),
    )(place, slots, qkv, lse, grads)


def rearrange(kernel, outs, numbers, arrays, scratch=()):
    size = sum(math.prod(o.shape) * o.dtype.itemsize for o in (*outs, *arrays))
    return pl.pallas_call(
        kernel,
        out_shape=tuple(jax.ShapeDtypeStruct(o.shape, o.dtype) for o in outs),
        in_specs=[SMEM] + [VMEM] * len(arrays),
        out_specs=(VMEM,) * len(outs),
        scratch_shapes=list(scratch),
        compiler_params=pltpu.CompilerParams(vmem_limit_bytes=LIMIT),
        cost_estimate=pl.CostEstimate(flops=0, bytes_accessed=size, transcendentals=0),
    )(jnp.stack(numbers).astype(jnp.int32), *arrays)


def shaped(shape, dtype=BF16):
    return jax.ShapeDtypeStruct(shape, dtype)


class Heads:
    def __init__(self, n, width):
        self.n, self.width = n, width
        self.full, self.rest = width // 128, width % 128
        self.slots = -(-(self.full + (self.rest > 0)) // n)
        self.wide = 128 * self.slots

    def pick_kernel(self, numbers, from_ref, more_ref, out_ref):
        rows = from_ref.shape[0]
        out_ref[rows:, :] = more_ref[...]
        out_ref = out_ref.at[:rows]
        for t in range(3):
            base = t * self.width
            first, off = base // 128, base % 128
            for j in range(self.slots):
                to = slice((t * self.slots + j) * 128, (t * self.slots + j + 1) * 128)
                p = j * self.n + numbers[0]

                @pl.when(p < self.full)
                def _():
                    start = pl.multiple_of((first + p) * 128, 128)
                    if off:
                        out_ref[:, to] = from_ref[:, pl.ds(start, 256)][:, off : off + 128]
                    else:
                        out_ref[:, to] = from_ref[:, pl.ds(start, 128)]

                @pl.when(p >= self.full)
                def _():
                    out_ref[:, to] = jnp.zeros((rows, 128), out_ref.dtype)

                if self.rest:
                    at = base + self.full * 128

                    @pl.when(p == self.full)
                    def _():
                        out_ref[:, to.start : to.start + self.rest] = from_ref[
                            :, at : at + self.rest
                        ]

    def pick(self, weight, more, c):
        out = shaped((weight.shape[0] + more.shape[0], 3 * self.wide))
        return rearrange(self.pick_kernel, [out], [c], [weight, more])[0]

    def join_kernel(self, from_ref, out_ref):
        for p in range(self.full + (self.rest > 0)):
            size = min(128, self.width - p * 128)
            j, owner = divmod(p, self.n)
            out_ref[:, p * 128 : p * 128 + size] = from_ref[owner, :, j * 128 : j * 128 + size]

    def split_kernel(self, from_ref, out_ref):
        for p in range(self.n * self.slots):
            size = max(0, min(128, self.width - p * 128))
            j, owner = divmod(p, self.n)
            if size:
                out_ref[owner, :, j * 128 : j * 128 + size] = from_ref[:, p * 128 : p * 128 + size]
            if size < 128:
                out_ref[owner, :, j * 128 + size : (j + 1) * 128] = jnp.zeros(
                    (out_ref.shape[1], 128 - size), out_ref.dtype
                )

    def turned(self, kernel, value, shape):
        return pl.pallas_call(
            kernel,
            out_shape=shaped(shape),
            in_specs=[VMEM],
            out_specs=VMEM,
            cost_estimate=pl.CostEstimate(
                flops=0, bytes_accessed=4 * math.prod(shape), transcendentals=0
            ),
        )(value)

    def join(self, blocks):
        return self.turned(self.join_kernel, blocks, (blocks.shape[1], self.width))

    def split(self, value):
        return self.turned(self.split_kernel, value, (self.n, value.shape[0], self.wide))

    def here(self, values, c):
        lead = values.shape[:-1]
        values = jnp.pad(values, [(0, 0)] * len(lead) + [(0, self.n * self.wide - self.width)])
        values = values.reshape(lead + (self.slots, self.n, 128))
        return lax.dynamic_index_in_dim(values, c, len(lead) + 1, False).reshape(
            lead + (self.wide,)
        )

    def back(self, values, c):
        lead = values.shape[:-1]
        zeros = jnp.zeros(lead + (self.slots, self.n, 128), values.dtype)
        values = values.reshape(lead + (self.slots, 1, 128))
        values = lax.dynamic_update_slice(zeros, values, (0,) * (len(lead) + 1) + (c, 0))
        return values.reshape(lead + (self.n * self.wide,))[..., : self.width]


def cut_kernel(per, numbers, from_ref, *outs):
    r = 0
    for out_ref in outs:
        for k in range(out_ref.shape[0]):
            for part in range(from_ref.shape[1] // per):

                @pl.when(numbers[r] == part)
                def _():
                    out_ref[k] = from_ref[:, part * per : (part + 1) * per]

            r += 1


def place_kernel(size, numbers, *refs):
    out_ref, r = refs[-1], 0
    for ref in refs[:-1]:
        for k in range(ref.shape[0]):
            to = pl.ds(pl.multiple_of(numbers[r] * size, 16), size)
            out_ref[to, :] = ref[k, :size, :]
            r += 1


def lay_kernel(plan, more, numbers, *refs):
    refs, held = refs[:-1], refs[-1]
    if more:
        refs, sum_ref = refs[:-1], refs[-1]
        last = slice(held.shape[1] - more, held.shape[1])
        sum_ref[...] = sum(
            ref[k, last, :].astype(F32) for ref in refs[:-1] for k in range(ref.shape[0])
        )
    blocks, out_ref = refs[:-1], refs[-1]
    r = 0
    for ref in blocks:
        for k in range(ref.shape[0]):
            held[numbers[r]] = ref[k]
            r += 1
    for b, from_rows, from_cols, rows, cols in plan:
        out_ref[rows, cols] = held[b, from_rows, from_cols].astype(F32)


def lay(blocks, numbers, plan, shape, more=0):
    steps = [
        (b, slice(r, r + h), slice(q, q + v), slice(tr, tr + h), slice(tq, tq + v))
        for b, (r, q), (h, v), (tr, tq) in plan
    ]
    scratch = [pltpu.VMEM((len(numbers),) + blocks[0].shape[1:], BF16)]
    kernel = functools.partial(lay_kernel, steps, more)
    outs = [shaped(shape, F32)] + ([shaped((more, blocks[0].shape[2]), F32)] if more else [])
    found = rearrange(kernel, outs, numbers, blocks, scratch)
    return found if more else found[0]


def by_rows(value):
    return with_layout_constraint(value, Layout(major_to_minor=tuple(range(value.ndim))))


def after(value, *others):
    return lax.optimization_barrier((value,) + others)[0]


def together(*values):
    return lax.optimization_barrier(values)


class Links:
    def __init__(self):
        self.n, self.m = lax.axis_size("ctx"), lax.axis_size("wt")
        self.c, self.w = lax.axis_index("ctx"), lax.axis_index("wt")
        self.bits = [1 << i for i in range(self.n.bit_length() - 1)]

    def swap(self, value, dc, dw):
        pairs = [
            (c * self.m + w, (c ^ dc) * self.m + (w ^ dw))
            for c in range(self.n)
            for w in range(self.m)
        ]
        return lax.ppermute(value, AXES, pairs)

    def core(self, value):
        return self.swap(value, 0, 1)

    def x(self, value):
        return self.swap(value, 0, 2)


    def gather_wt(self, value):
        near = jnp.stack([value, self.x(value)])
        return [near, self.core(near)]

    def trade_wt(self, own, near, far):
        (far,) = yield [(far, 0, 2)]
        (come,) = yield [(jnp.concatenate([near, far[1:]]), 0, 1)]
        return [own, far[:1], come]

    def sum_wt(self, near, far):
        (come,) = yield [(far, 0, 1)]
        (far,) = yield [(add_low(near[1], come[1]), 0, 2)]
        return add_low(add_low(near[0], come[0]), far)

    def rows_wt(self, blocks, size, numbers=(0, 2, 1, 3)):
        return rearrange(
            functools.partial(place_kernel, size),
            [shaped((self.m * size, blocks[0].shape[2]))],
            [self.w ^ r for r in numbers],
            blocks,
        )[0]


    def gather(self, value, bits, split):
        blocks = value[None]
        for bit in bits[:-2]:
            (come,) = yield [(blocks, bit, 0)]
            blocks = jnp.concatenate([blocks, come])
        if split:
            come, first = yield [(blocks, bits[-2], 0), (blocks, bits[-1], 0)]
            (second,) = yield [(come, bits[-1], 0)]
            return [blocks, come, first, second]
        (come,) = yield [(blocks, bits[-2], 0)]
        blocks = jnp.concatenate([blocks, come])
        (come,) = yield [(blocks, bits[-1], 0)]
        return [blocks, come]

    def gathered(self, bits):
        found = [0]
        for bit in bits:
            found = found + [d | bit for d in found]
        return found

    def halving(self, bits):
        found = [0]
        for bit in reversed(bits):
            found = [d | bit for d in found] + found
        return found

    def halve(self, terms, bits):
        for bit in bits:
            half = terms.shape[0] // 2
            (come,) = yield [(terms[:half], bit, 0)]
            terms = add_low(terms[half:], come)
        return terms[0]


    def plane_hops(self, value):
        return [self.x(value), self.swap(value, 2, 0), self.swap(value, 2, 2)]

    def gather_plane(self, value, come):
        parts = [value] + come
        return jnp.concatenate(parts + [self.core(part) for part in parts])

    def sum_plane(self, near, far):
        (come,) = yield [(far, 0, 1)]
        mine = add_low(near(), come)
        size = mine.shape[0] // 4
        parts = [mine[i * size : (i + 1) * size] for i in range(4)]
        come = yield [(parts[3], 2, 2), (parts[2], 2, 0), (parts[1], 0, 2)]
        return sum((part.astype(F32) for part in come), parts[0].astype(F32))


class Traffic:
    AHEAD = 4

    def __init__(self, links, chains):
        self.links, self.chains, self.results = links, chains, {}
        self.come, self.last, self.open = {}, None, []

    def step(self, name):
        chain, come = self.chains[name], self.come.get(name)
        if come is not None:
            self.open = [part for part in self.open if not any(part is other for other in come)]
            come = [after(part, self.last) for part in come]
        try:
            sends = chain.send(come)
        except StopIteration as end:
            self.results[name] = end.value
            self.come.pop(name, None)
            self.chains.pop(name)
            return
        self.come[name] = []
        for value, dc, dw in sends:
            ties = [] if self.last is None else [self.last]
            if dc is not None:
                while len(self.open) > self.AHEAD:
                    ties.append(self.open.pop(0))
            self.last = after(value, *ties)
            if dc is None:
                come = lax.all_to_all(self.last, "ctx", 0, 0, tiled=True)
            else:
                come = self.links.swap(self.last, dc, dw)
                self.open.append(come)
            self.come[name].append(come)

    def now(self, value):
        return after(value, self.last)

    def run(self, turns):
        for name in turns:
            if name in self.chains:
                self.step(name)
        while self.chains:
            for name in list(self.chains):
                self.step(name)


def on_device(
    tokens,
    slots,
    norm_gains,
    norm_shifts,
    qkv_weight,
    qv_bias,
    proj_weight,
    proj_bias,
    up_weight,
    up_bias,
    down_weight,
    down_bias,
    cotangent,
):
    links = Links()
    n, m, c, w = links.n, links.m, links.c, links.w
    _, rows, width = tokens.shape
    heads = Heads(n, width)
    share = width // m
    block = rows // 2
    length = n * rows
    hid = up_weight.shape[1]
    per = hid // (2 * m)
    tile = 256 if length <= UNROLLED else 128
    near = rows * m
    nq = n // 2
    cut = nq // m

    def half_of(c):
        return (c >> 1) & 1

    def place_of(c):
        return ((c >> 2) << 1) | (c & 1)

    half, place_q = half_of(c), place_of(c)
    spread = links.bits[:1] + links.bits[2:]
    order = links.halving(links.bits)

    own = tokens[0]
    small = jnp.concatenate(
        [
            norm_gains.reshape(-1),
            norm_shifts.reshape(-1),
            qv_bias.reshape(-1),
            proj_bias,
            down_bias,
            up_bias,
        ]
    )
    entries = small.shape[0]
    take = share if 3 * heads.wide >= share else share // 2
    more = -(-max(-(-entries // (3 * heads.wide)), entries // take) // 16) * 16
    small = jnp.pad(small, [(0, more * 3 * heads.wide - entries)]).reshape(more, 3 * heads.wide)
    seen = {0: own}
    for bit in reversed(links.bits[1:]):
        seen.update({d | bit: links.swap(seen[d], bit, 0) for d in list(seen)})
    firsts = [0] + [bit for bit in links.bits[1:]]
    rest = [d for d in seen if d not in firsts]
    seen[1] = links.swap(own, 1, 0)
    for batch in (firsts[1:], rest):
        sent = links.swap(after(jnp.concatenate([seen[d] for d in batch]), seen[1]), 1, 0)
        seen.update({d | 1: sent[i * rows : (i + 1) * rows] for i, d in enumerate(batch)})
    found = links.gather_wt(heads.pick(qkv_weight, small, c))
    wqkv = links.rows_wt(found, share)
    small = jnp.concatenate([part[:, share:].reshape(2, -1)[:, :entries] for part in found])
    word = seen[1][:16, :128]
    for _ in range(5):
        word = links.core(word)
    last = seen[links.n - 1]
    seen = after(jnp.concatenate([seen[d] for d in order]), word)
    wqkv = after(wqkv, word)

    far_bits = links.bits[:1:-1]
    bits = {
        "down": [*far_bits, 2, 1],
        "up": [*far_bits, 2, 1],
        "qkv": [*far_bits, 1, 2],
        "proj": [*far_bits, 2, 1],
        "up sum": [1, *far_bits],
        "down sum": [1, *far_bits],
        "proj sum": [1, 2, *far_bits],
    }
    pieces = rearrange(
        functools.partial(cut_kernel, per),
        [shaped((k, share, per)) for k in (1, 1, 2)],
        [(w ^ r) * 2 + half for r in range(m)],
        [up_weight],
    )
    wproj = links.gather_wt(proj_weight)
    up_far = links.x(after(pieces[2], wproj[0]))
    wdown = lax.dynamic_slice_in_dim(down_weight, half * per, per, 0)
    grad_out = cotangent[0]

    number = jnp.arange(m, dtype=jnp.int32)
    sources = jnp.array([0, 2, 1, 3], jnp.int32) ^ w
    small = dot((number[:, None] == sources[None, :]).astype(BF16), small)
    vectors = small[:, : 6 * share].reshape(m, 3, 2, share).transpose(1, 2, 0, 3)
    gains, shifts, qvb = vectors.reshape(3, 2, width)
    bproj = small[:, 6 * share : 7 * share].reshape(width)
    bdown = small[:, 7 * share : 8 * share].reshape(width)
    bup = small[:, 8 * share :].reshape(m * 2, per)
    bup = lax.dynamic_index_in_dim(bup, w * 2 + half, 0, False)

    a1 = (standardize(seen.astype(F32))[0] * gains[0] + shifts[0]).astype(BF16)
    qvb_here = heads.here(qvb, c)
    bias = jnp.concatenate([qvb_here[0], jnp.zeros((heads.wide,), F32), qvb_here[1]])
    qkv = (dot(a1, wqkv) + bias).astype(BF16)

    table = jnp.arange(slots.shape[0], dtype=jnp.int32)
    wanted = jnp.array(order, jnp.int32)
    wanted = ((wanted[:, None] ^ c) * 2 + jnp.arange(2, dtype=jnp.int32)).reshape(-1)
    place = jnp.sum(jnp.where(wanted[:, None] == table[None, :], slots[None, :], 0), axis=1)

    come = links.plane_hops(after(grad_out, last))
    heads_out, lse = attn_forward(qkv, place, slots, block, tile)

    wproj = links.rows_wt([after(part, heads_out) for part in wproj], share)
    attended = lax.all_to_all(heads_out, "ctx", 0, 0, tiled=True)
    attended = heads.join(after(attended, wproj, up_far))
    grad_out_plane = links.gather_plane(
        after(grad_out, attended), [after(part, attended) for part in come]
    )
    far = after(up_far, attended)
    wup = [pieces[0], far[:1], links.core(jnp.concatenate([pieces[1], far[1:]]))]
    wup = links.rows_wt(wup, share)
    mid = own.astype(F32) + dot(attended, wproj) + bproj
    normed2, scale2 = standardize(mid)
    a2 = (normed2 * gains[1] + shifts[1]).astype(BF16)

    a2_plane = links.gather_plane(a2, links.plane_hops(a2))
    grad_out32 = grad_out.astype(F32)
    middle = length // 2
    step = -(-(-(-per // nq)) // 8) * 8
    part = -(-(-(-share // n)) // 8) * 8
    kept = {}

    def main_chain():
        pre = dot(a2_plane, wup) + bup
        activated, gelu_pull = jax.vjp(gelu, pre)
        hidden = activated.astype(BF16)
        grad_pre = gelu_pull(by_transpose(grad_out_plane, wdown))[0].astype(BF16)
        kept.update(hidden=hidden, grad_pre=grad_pre)
        grad_a2 = yield from links.sum_plane(
            lambda: by_transpose(grad_pre[:near], wup),
            by_transpose(grad_pre[near:], wup).astype(BF16),
        )
        grad_mid = grad_out32 + finish_norm(grad_a2 * gains[1], normed2, scale2)
        grad_proj = grad_mid.astype(BF16)
        kept.update(grad_a2=grad_a2, grad_mid=grad_mid, grad_proj=grad_proj)
        grad_heads = heads.split(by_transpose(grad_proj, wproj).astype(BF16))
        word = after(jnp.zeros((8, 128), F32), grad_heads)
        (grad_heads,) = yield [(grad_heads, None, None)]
        for _ in range(BUMP):
            word = links.core(word)
        grad_heads = after(grad_heads, word)
        grad_qkv = attn_backward(qkv, grad_heads, lse, place, slots, block, tile)
        normed1 = standardize(after(seen, word).astype(F32))[0]
        other, mine = by_transpose(grad_qkv[:middle], wqkv), by_transpose(grad_qkv[middle:], wqkv)
        d_gain1 = jnp.sum(other * normed1[:middle] + mine * normed1[middle:], axis=0)
        kept.update(grad_qkv=grad_qkv, other=other.astype(BF16), mine=mine, d_gain1=d_gain1)

    def down_chain():
        found = by_rows(over_rows(kept["hidden"], grad_out_plane).astype(BF16))
        found = jnp.pad(found, [(0, step * nq - per), (0, 0)])
        found = [
            lax.dynamic_slice_in_dim(found, (place_q ^ place_of(d)) * step, step, 0)
            for d in links.halving(bits["down sum"])
        ]
        found = yield from links.halve(jnp.stack(found), bits["down sum"])
        return (yield from links.gather(found, bits["down"], "down" in SPLIT))

    def up_chain():
        found = by_rows(over_rows(a2_plane, kept["grad_pre"]).astype(BF16))
        pieces = [lax.dynamic_slice_in_dim(found, (w ^ r) * share, share, 0) for r in range(m)]
        found = yield from links.trade_wt(pieces[0][None], pieces[1][None], jnp.stack(pieces[2:]))
        found = jnp.concatenate(found).reshape(m, share, cut, per // cut).transpose(0, 2, 1, 3)
        terms = []
        for d in links.halving(bits["up sum"]):
            b = place_q ^ place_of(d)
            r = w ^ (b // cut)
            r = (r & 1) * 2 + (r >> 1)
            term = lax.dynamic_slice(found, (r, b % cut, 0, 0), (1, 1, share, per // cut))
            terms.append(term[0, 0])
        found = yield from links.halve(jnp.stack(terms), bits["up sum"])
        return (yield from links.gather(found, bits["up"], "up" in SPLIT))

    def output_chain():
        hidden = traffic.now(kept["hidden"])
        near_part = dot(hidden[:near], wdown).astype(BF16)
        far_part = dot(hidden[near:], wdown).astype(BF16)
        return (yield from links.sum_plane(lambda: near_part, far_part))

    def proj_chain():
        found = by_rows(over_rows(attended, kept["grad_proj"]).astype(BF16))
        pieces = [
            lax.dynamic_slice_in_dim(found, (w ^ r) * share, share, 0) for r in (0, 2, 1, 3)
        ]
        found = yield from links.sum_wt(jnp.stack(pieces[:2]), jnp.stack(pieces[2:]))
        found = jnp.pad(found, [(0, n * part - share), (0, 0)])
        found = [
            lax.dynamic_slice_in_dim(found, (c ^ d) * part, part, 0)
            for d in links.halving(bits["proj sum"])
        ]
        found = yield from links.halve(jnp.stack(found), bits["proj sum"])
        return (yield from links.gather(found, bits["proj"], "proj" in SPLIT))

    def input_chain():
        (come,) = yield [(kept["other"], 1, 0)]
        terms = add_low(kept["mine"], come).reshape(n // 2, rows, width)
        return (yield from links.halve(terms, links.bits[1:]))

    def qkv_chain():
        grad_a2, grad_proj, grad_qkv = (kept[name] for name in ("grad_a2", "grad_proj", "grad_qkv"))
        sums = jnp.sum(grad_qkv.astype(F32), axis=0)
        d_shift1 = dot(sums[None], wqkv.astype(F32).T)[0]
        sums = heads.back(sums.reshape(3, heads.wide), c)
        d_up_bias = lax.dynamic_update_slice(
            jnp.zeros((m * 2, per), F32),
            jnp.sum(kept["grad_pre"].astype(F32), axis=0)[None],
            (w * 2 + half, 0),
        ).reshape(m, hid // m // share, share)
        vectors = [
            kept["d_gain1"],
            jnp.sum(grad_a2 * normed2, axis=0),
            d_shift1,
            jnp.sum(grad_a2, axis=0),
            sums[0],
            sums[2],
            jnp.sum(grad_proj.astype(F32), axis=0),
            jnp.sum(grad_out32, axis=0),
        ]
        vectors = jnp.stack([v.reshape(m, share) for v in vectors], axis=1)
        vectors = jnp.concatenate([vectors, d_up_bias], axis=1).astype(BF16)
        vectors = vectors.reshape(m, entries // take, take)
        beside = (more - entries // take, 3 * heads.wide - take)
        vectors = jnp.pad(vectors, [(0, 0), (0, beside[0]), (0, beside[1])])
        vectors = vectors.reshape(m * more, 3 * heads.wide)
        found = by_rows(over_rows(a1, grad_qkv).astype(BF16))
        pieces = [
            jnp.concatenate(
                [
                    lax.dynamic_slice_in_dim(found, (w ^ r) * share, share, 0),
                    lax.dynamic_slice_in_dim(vectors, (w ^ r) * more, more, 0),
                ]
            )
            for r in (0, 2, 1, 3)
        ]
        found = yield from links.sum_wt(jnp.stack(pieces[:2]), jnp.stack(pieces[2:]))
        return (yield from links.gather(found, bits["qkv"], "qkv" in SPLIT))

    chains = {
        "m": main_chain(),
        "d": down_chain(),
        "u": up_chain(),
        "g": input_chain(),
        "q": qkv_chain(),
        "p": proj_chain(),
        "o": output_chain(),
    }
    traffic = Traffic(links, chains)
    traffic.run(TURNS)
    d_down, d_up, d_qkv, d_proj = (traffic.results[name] for name in "duqp")
    output, grad_a1 = traffic.results["o"], traffic.results["g"].astype(F32)
    grad_mid = kept["grad_mid"]

    output = mid + output + bdown
    own1, scale1 = standardize(own.astype(F32))
    d_tokens = grad_mid + finish_norm(grad_a1 * gains[0], own1, scale1)

    def owners(name):
        return [c ^ d for d in links.gathered(bits[name])]

    plan = [
        (
            b,
            (0, 0),
            (min(step, per - place_of(b) * step), width),
            (half_of(b) * per + place_of(b) * step, 0),
        )
        for b in range(n)
        if place_of(b) * step < per
    ]
    d_down_weight = lay(d_down, owners("down"), plan, (2 * per, width))
    size = per // cut
    plan = [
        (
            b,
            (0, 0),
            (share, size),
            (
                0,
                (place_of(b) // cut) * 2 * per + half_of(b) * per + (place_of(b) % cut) * size,
            ),
        )
        for b in range(n)
    ]
    d_up_weight = lay(d_up, owners("up"), plan, (share, hid))
    plan = [
        (b, (0, 0), (min(part, share - b * part), width), (b * part, 0))
        for b in range(n)
        if b * part < share
    ]
    d_proj_weight = lay(d_proj, owners("proj"), plan, (share, width))
    plan = [
        (
            p % n,
            (0, (t * heads.slots + p // n) * 128),
            (share, min(128, width - p * 128)),
            (0, t * width + p * 128),
        )
        for t in range(3)
        for p in range(-(-width // 128))
    ]
    d_qkv_weight, vectors = lay(d_qkv, owners("qkv"), plan, (share, 3 * width), more)
    vectors = vectors[: entries // take, :take].reshape(entries // share, share)
    return (
        output.astype(BF16)[None],
        d_tokens.astype(BF16)[None],
        vectors[0:2],
        vectors[2:4],
        d_qkv_weight,
        vectors[4:6],
        d_proj_weight,
        vectors[6],
        d_up_weight,
        vectors[8 : 8 + hid // width].reshape(-1),
        d_down_weight,
        vectors[7],
    )


def solution(mesh):
    rows, whole = P("wt", "ctx", None), P(None, "wt")
    weight, vector = P("wt", None), P("wt")
    return jax.shard_map(
        on_device,
        mesh=mesh,
        in_specs=(
            rows,
            P(),
            whole,
            whole,
            weight,
            whole,
            weight,
            vector,
            weight,
            vector,
            weight,
            vector,
            rows,
        ),
        out_specs=(
            rows,
            rows,
            whole,
            whole,
            weight,
            whole,
            weight,
            vector,
            weight,
            vector,
            weight,
            vector,
        ),
        check_vma=False,
    )
```
